128 devices in a mesh: history: 16 (over z, y), dp: 8 (over x, core).
Axes of the slice: x: 4, y: 4, z: 4, core: 2. Of those that a mesh axis runs over, the one named last changes fastest.
Arguments:
- actions: bfloat16 [16, 8, 128, 2048], P('history', 'dp'), may hold values from -6 to 6
- cotangent: bfloat16 [16, 8, 128, 2048], P('history', 'dp'), may hold values from -6 to 6
- cache_kv: bfloat16 [2, 16, 8, 512, 2048], P(None, None, 'dp', 'history'), may hold values from -6 to 6
- cache_len: int32 [16, 8], P('history', 'dp'), may hold values from 64 to 512, as said below
- cache_bucket: int32 [16, 8, 512], P(None, 'dp', 'history'), may hold values from 0 to 127
- new_bucket: int32 [16, 8, 128], P('history', 'dp'), may hold values from 0 to 127
- ln_gain: float32 [2048], replicated, may hold values from 0.5 to 1.5
- norm_gain: float32 [2048], replicated, may hold values from 0.5 to 1.5
- w_frozen: bfloat16 [3, 2048, 2048], P(None, None, 'dp'), may hold values from -0.125 to 0.125
- w_query: bfloat16 [2048, 2048], P(None, 'dp'), may hold values from -0.125 to 0.125
- query_m: float32 [2048, 2048], P(None, 'dp'), may hold values from -6 to 6
- query_v: float32 [2048, 2048], P(None, 'dp'), may hold values from 0.1 to 10
- w_out: bfloat16 [2048, 2048], P(None, 'dp'), may hold values from -0.125 to 0.125
- rab_table: float32 [16, 128], replicated, may hold values from -6 to 6
- rab_m: float32 [16, 128], replicated, may hold values from -6 to 6
- rab_v: float32 [16, 128], replicated, may hold values from 0.1 to 10
Outputs:
- output: bfloat16 [16, 8, 128, 2048], P('history', 'dp')
- query_new: bfloat16 [2048, 2048], P(None, 'dp')
- query_m_new: float32 [2048, 2048], P(None, 'dp')
- query_v_new: float32 [2048, 2048], P(None, 'dp')
- rab_new: float32 [16, 128], replicated
- rab_m_new: float32 [16, 128], replicated
- rab_v_new: float32 [16, 128], replicated
The draws below stay inside these ranges and needn't reach their ends.
Inputs may be any that keep to these rules, and one draw needn't show every extreme that they name: `cache_len`: each user has between 64 and 512 valid cached actions; in every draw some user has exactly 512.
All inputs are finite; a program needn't handle non-finite values.
Results may differ from the reference program's by a relative error of at most 0.0094.
Values may be sent and summed in bfloat16 or wider, within the bound.
A program may use at most 128 MiB of HBM per device.

```python
import math
import jax
import jax.numpy as jnp
from jax import lax

D = 2048
HEADS = 16
HEAD_DIM = 128
BUCKETS = 128
NEW = 128
HIST_USERS = 16
GROUPS = 8
MAXC = 512


def draw_cache_len(key, part):
    key = jax.random.fold_in(key, 11)
    key_base, key_shrink, key_pick = jax.random.split(key, 3)
    base_len = jax.random.randint(key_base, (HIST_USERS * GROUPS,), MAXC // 4, MAXC + 1)
    shrink = jax.random.randint(key_shrink, (HIST_USERS * GROUPS,), 0, 2)
    shortened = jnp.maximum(base_len // jnp.left_shift(jnp.ones_like(shrink), shrink), 1)
    chosen = jax.random.randint(key_pick, (), 0, HIST_USERS * GROUPS)
    flat_len = jnp.where(jnp.arange(HIST_USERS * GROUPS) == chosen, MAXC, shortened)
    return flat_len.reshape(HIST_USERS, GROUPS).astype(jnp.int32)


def set_ends(drawn, rng, least, top_value):
    longest = drawn.shape.index(max(drawn.shape))
    spots = []
    for shift in (0, 1):
        where = [jax.random.randint(jax.random.fold_in(rng, axis), (), 0, length) for axis, length in enumerate(drawn.shape)]
        where[longest] = (where[longest] + shift) % drawn.shape[longest]
        spots.append(tuple(where))
    return drawn.at[spots[0]].set(least).at[spots[1]].set(top_value)


def level_of(key, extent, cuts, least, top_value):
    factor_of = 1.0
    for position, shards_of in cuts:
        heights = jax.random.uniform(jax.random.fold_in(jax.random.fold_in(key, 6), position), (shards_of,), jnp.float32, least / len(cuts), top_value / len(cuts))
        factor_of = factor_of * jnp.repeat(jnp.exp(heights), extent[position] // shards_of).reshape((-1,) + (1,) * (len(extent) - 1 - position))
    return factor_of


def bell_draw(key, shape, width, bound, cuts=(), kind=jnp.bfloat16):
    entries = width * jax.random.normal(key, shape, jnp.float32)
    if cuts:
        entries = entries * level_of(key, shape, cuts, -0.22, 0.18)
    return jnp.clip(entries, -bound, bound).astype(kind)


def setup_inputs(seed: int = 0) -> dict:
    arg_keys = jax.random.split(jax.random.key(seed), 17)
    return {
        "actions": bell_draw(arg_keys[0], (HIST_USERS, GROUPS, NEW, D), 1.0, 6.0, ((0, 16), (1, 8))),
        "cotangent": bell_draw(arg_keys[1], (HIST_USERS, GROUPS, NEW, D), 1.0, 6.0, ((0, 16), (1, 8))),
        "cache_kv": bell_draw(arg_keys[2], (2, HIST_USERS, GROUPS, MAXC, D), 1.0, 6.0, ((2, 8), (3, 16))),
        "cache_len": draw_cache_len(jax.random.fold_in(arg_keys[16], 71), 0),
        "cache_bucket": set_ends(jax.random.randint(arg_keys[4], (HIST_USERS, GROUPS, MAXC), 0, BUCKETS), jax.random.fold_in(arg_keys[4], 1), 0, BUCKETS - 1).astype(jnp.int32),
        "new_bucket": set_ends(jax.random.randint(arg_keys[5], (HIST_USERS, GROUPS, NEW), 0, BUCKETS), jax.random.fold_in(arg_keys[5], 1), 0, BUCKETS - 1).astype(jnp.int32),
        "ln_gain": jnp.clip(1.0 + 0.1 * jax.random.normal(arg_keys[6], (D,), jnp.float32), 0.5, 1.5),
        "norm_gain": jnp.clip(1.0 + 0.1 * jax.random.normal(arg_keys[7], (D,), jnp.float32), 0.5, 1.5),
        "w_frozen": bell_draw(arg_keys[8], (3, D, D), D ** -0.5, 0.125, ((2, 8),)),
        "w_query": bell_draw(arg_keys[9], (D, D), D ** -0.5, 0.125, ((1, 8),)),
        "query_m": bell_draw(arg_keys[10], (D, D), 1.0, 6.0, ((1, 8),), jnp.float32),
        "query_v": jnp.clip(jnp.exp(math.log(10.0) - 4.6051702 * jax.random.uniform(arg_keys[11], (D, D), jnp.float32) ** level_of(arg_keys[11], (D, D), ((1, 8),), -0.2, 0.2)), 0.1, 10.0),
        "w_out": bell_draw(arg_keys[12], (D, D), D ** -0.5, 0.125, ((1, 8),)),
        "rab_table": bell_draw(arg_keys[13], (HEADS, BUCKETS), 1.0, 6.0, (), jnp.float32),
        "rab_m": bell_draw(arg_keys[14], (HEADS, BUCKETS), 1.0, 6.0, (), jnp.float32),
        "rab_v": jnp.clip(jnp.exp(jax.random.uniform(arg_keys[15], (HEADS, BUCKETS), jnp.float32, math.log(0.1), math.log(10.0))), 0.1, 10.0),
    }


BETA_ONE = 0.9
BETA_TWO = 0.95
LEARN_RATE = 0.001
ADAM_EPS = 1e-08
NORM_EPS = 1e-05

def layer_norm(values, scaling):
    center = values - lax.optimization_barrier(jnp.mean(values, axis=-1, keepdims=True))
    inverse = lax.rsqrt(lax.optimization_barrier(jnp.mean(center * center, axis=-1, keepdims=True)) + NORM_EPS)
    return center * inverse * scaling

def silu_slope(values):
    sigmoid = jax.nn.sigmoid(values)
    return sigmoid * (1.0 + values * (1.0 - sigmoid))

def rounded(values):
    return lax.optimization_barrier(values.astype(jnp.bfloat16))

def adam_update(weight, moment_one, moment_two, gradient):
    first_new = BETA_ONE * moment_one + (1.0 - BETA_ONE) * gradient
    second_new = BETA_TWO * moment_two + (1.0 - BETA_TWO) * gradient * gradient
    stepped = weight.astype(jnp.float32) - LEARN_RATE * first_new / (jnp.sqrt(second_new) + ADAM_EPS)
    return (stepped.astype(weight.dtype), first_new, second_new)

def one_user(inputs, ln_gain, norm_gain, w_frozen, w_query, w_out, rab_table):
    actions, cotangent, keys_cache, values_cache, bucket_cache, bucket_new, length = inputs
    x_float = actions.astype(jnp.float32)
    normed = layer_norm(x_float, ln_gain).astype(jnp.bfloat16)
    query_pre = jnp.dot(normed, w_query, preferred_element_type=jnp.float32)
    query_act = rounded(jax.nn.silu(query_pre))
    gate_act = rounded(jax.nn.silu(jnp.dot(normed, w_frozen[0], preferred_element_type=jnp.float32)))
    value_new = jax.nn.silu(jnp.dot(normed, w_frozen[1], preferred_element_type=jnp.float32)).astype(jnp.bfloat16)
    key_new = jax.nn.silu(jnp.dot(normed, w_frozen[2], preferred_element_type=jnp.float32)).astype(jnp.bfloat16)
    all_keys = jnp.concatenate([keys_cache, key_new], 0).astype(jnp.float32).reshape(MAXC + NEW, HEADS, HEAD_DIM)
    all_values = jnp.concatenate([values_cache, value_new], 0).astype(jnp.float32).reshape(MAXC + NEW, HEADS, HEAD_DIM)
    buckets = jnp.concatenate([bucket_cache, bucket_new], 0)
    onehot = (buckets[:, None] == jnp.arange(BUCKETS, dtype=jnp.int32)[None, :]).astype(jnp.float32)
    key_bias = jnp.dot(rab_table, onehot.T, precision=lax.Precision.HIGHEST)
    query_heads = query_act.astype(jnp.float32).reshape(NEW, HEADS, HEAD_DIM)
    scores = jnp.einsum('thd,khd->htk', query_heads, all_keys) * HEAD_DIM ** (-0.5) + key_bias[:, None, :]
    key_pos = jnp.arange(MAXC + NEW, dtype=jnp.int32)
    query_pos = jnp.arange(NEW, dtype=jnp.int32)
    visible = jnp.where(key_pos[None, :] < MAXC, key_pos[None, :] < length, key_pos[None, :] - MAXC <= query_pos[:, None])
    key_total = (length + NEW).astype(jnp.float32)
    weights = rounded(jnp.where(visible[None], jax.nn.silu(scores), 0.0) / key_total)
    attended = jnp.einsum('htk,khd->thd', weights.astype(jnp.float32), all_values).reshape(NEW, D)
    nhat = layer_norm(attended, 1.0)
    gate_float = gate_act.astype(jnp.float32)
    gated = (nhat * norm_gain * gate_float).astype(jnp.bfloat16)
    output = (jnp.dot(gated, w_out, preferred_element_type=jnp.float32) + x_float).astype(jnp.bfloat16)
    grad_gated = jnp.dot(cotangent, w_out.T, preferred_element_type=jnp.float32)
    grad_hat = grad_gated * gate_float * norm_gain
    center = attended - lax.optimization_barrier(jnp.mean(attended, axis=-1, keepdims=True))
    inverse = lax.rsqrt(lax.optimization_barrier(jnp.mean(center * center, axis=-1, keepdims=True)) + NORM_EPS)
    grad_att = inverse * (grad_hat - lax.optimization_barrier(jnp.mean(grad_hat, axis=-1, keepdims=True)) - nhat * lax.optimization_barrier(jnp.mean(grad_hat * nhat, axis=-1, keepdims=True)))
    grad_heads = rounded(grad_att).astype(jnp.float32).reshape(NEW, HEADS, HEAD_DIM)
    grad_weights = jnp.einsum('thd,khd->htk', grad_heads, all_values)
    grad_scores = jnp.where(visible[None], grad_weights * silu_slope(scores), 0.0) / key_total
    grad_query = jnp.einsum('htk,khd->thd', rounded(grad_scores).astype(jnp.float32), all_keys).reshape(NEW, D) * HEAD_DIM ** (-0.5)
    grad_table = jnp.dot(lax.optimization_barrier(jnp.sum(grad_scores, axis=1)), onehot, precision=lax.Precision.HIGHEST)
    grad_pre = (grad_query * silu_slope(query_pre)).astype(jnp.bfloat16)
    grad_weight = jnp.dot(normed.T, grad_pre, preferred_element_type=jnp.float32)
    return (output, grad_weight, grad_table)

def reference(actions, cotangent, cache_kv, cache_len, cache_bucket, new_bucket, ln_gain, norm_gain, w_frozen, w_query, query_m, query_v, w_out, rab_table, rab_m, rab_v):
    user_count = HIST_USERS * GROUPS
    per_user = (actions.reshape(user_count, NEW, D), cotangent.reshape(user_count, NEW, D), cache_kv[0].reshape(user_count, MAXC, D), cache_kv[1].reshape(user_count, MAXC, D), cache_bucket.reshape(user_count, MAXC), new_bucket.reshape(user_count, NEW), cache_len.reshape(user_count))

    def scan_body(running, inputs):
        output, grad_weight, grad_table = one_user(inputs, ln_gain, norm_gain, w_frozen, w_query, w_out, rab_table)
        return ((running[0] + grad_weight, running[1] + grad_table), output)
    start_sums = (jnp.zeros((D, D), jnp.float32), jnp.zeros((HEADS, BUCKETS), jnp.float32))
    (grad_weight, grad_table), outputs = lax.scan(scan_body, start_sums, per_user)
    query_new, query_m_new, query_v_new = adam_update(w_query, query_m, query_v, grad_weight)
    rab_new, rab_m_new, rab_v_new = adam_update(rab_table, rab_m, rab_v, grad_table)
    return (outputs.reshape(HIST_USERS, GROUPS, NEW, D), query_new, query_m_new, query_v_new, rab_new, rab_m_new, rab_v_new)
```

```python
import functools

import jax
import jax.numpy as jnp
from jax import lax
from jax.experimental import pallas as pl
from jax.experimental.pallas import tpu as pltpu
from jax.sharding import PartitionSpec as P

BETA_ONE = 0.9
BETA_TWO = 0.95
LEARN_RATE = 0.001
ADAM_EPS = 1e-08
NORM_EPS = 1e-05

MESH = pl.DeviceIdType.MESH
F32 = jnp.float32
BF16 = jnp.bfloat16

TOK = 128
WIDTH = 2048
COLS = 256
HEAD = 128
HEADS = 16
BUCKETS = 128
HIST = 16
DP = 8
SLAB = 32
CACHED = HIST * SLAB
KEYS = CACHED + TOK
SCALE = HEAD ** (-0.5)


def adam_update(weight, moment_one, moment_two, gradient):
    first_new = BETA_ONE * moment_one + (1.0 - BETA_ONE) * gradient
    second_new = BETA_TWO * moment_two + (1.0 - BETA_TWO) * gradient * gradient
    stepped = weight.astype(F32) - LEARN_RATE * first_new / (jnp.sqrt(second_new) + ADAM_EPS)
    return (stepped.astype(weight.dtype), first_new, second_new)


def dot_nn(a, b):
    return jnp.dot(a, b, preferred_element_type=F32)


def dot_nt(a, b):
    return lax.dot_general(a, b, (((1,), (1,)), ((), ())), preferred_element_type=F32)


def three_parts(values):
    first = values.astype(BF16)
    rest = values - first.astype(F32)
    second = rest.astype(BF16)
    third = (rest - second.astype(F32)).astype(BF16)
    return first, second, third


def silu_slope(values):
    sigmoid = 0.5 * jnp.tanh(0.5 * values) + 0.5
    return sigmoid * (1.0 + values * (1.0 - sigmoid))


def kernel(
    act_hbm, cot_hbm, cache_hbm, length, bucket_hbm, new_bucket, ln_gain, norm_gain, frozen_hbm, query_hbm, wout_hbm, rab,
    out_ref, gsum_hbm, gtab_ref,
    act, cot, wts, rows, pre_slope, sent, proj, kv, bks, onehot, bias, att, slope, wout, grad_gated, gated, grad_att,
    tsum, gq_out, gq_in, grad_pre_t, rs_out, rs_in, ag_out, tab_one, tab_two,
    loc_sem, kv_s, kv_r, bk_s, bk_r, g_s, g_r, pj_s, pj_r, w_s, w_r, gq_s, gq_r, rs_s, rs_r, ag_s, ag_r, t1_s, t1_r, t2_s, t2_r,
):
    h = lax.axis_index("history")
    d = lax.axis_index("dp")
    z, y = h // 4, lax.rem(h, 4)
    x, c = d // 2, lax.rem(d, 2)

    def hist(k):
        return lax.rem(z + k // 4, 4) * 4 + lax.rem(y + lax.rem(k, 4), 4)

    def dpx(kx, kc):
        return lax.rem(x + kx, 4) * 2 + lax.rem(c + kc, 2)

    def dpo(k):
        return lax.rem(x + k // 2, 4) * 2 + lax.rem(c + lax.rem(k, 2), 2)

    barrier = pltpu.get_barrier_semaphore()

    def greet_hist(k, carry):
        pl.semaphore_signal(barrier, inc=1, device_id=(hist(k), d), device_id_type=MESH)
        return carry

    def greet_dp(k, carry):
        pl.semaphore_signal(barrier, inc=1, device_id=(h, dpo(k)), device_id_type=MESH)
        return carry

    lax.fori_loop(1, DP, greet_dp, 0)
    lax.fori_loop(1, HIST, greet_hist, 0)

    load_act = pltpu.make_async_copy(act_hbm, act, loc_sem.at[0])
    load_act.start()
    load_query = pltpu.make_async_copy(query_hbm, wts.at[0], loc_sem.at[1])
    load_query.start()
    load_frozen = pltpu.make_async_copy(frozen_hbm, wts.at[pl.ds(1, 3)], loc_sem.at[2])
    load_frozen.start()
    load_cot = pltpu.make_async_copy(cot_hbm, cot, loc_sem.at[3])
    load_cot.start()
    load_wout = pltpu.make_async_copy(wout_hbm, wout.at[d], loc_sem.at[4])
    load_wout.start()
    own_slab = kv.at[:, pl.ds(pl.multiple_of(h * SLAB, SLAB), SLAB), :]
    load_kv = pltpu.make_async_copy(cache_hbm.at[:, h], own_slab, loc_sem.at[5])
    load_kv.start()
    load_bk = pltpu.make_async_copy(bucket_hbm.at[h], bks.at[h], loc_sem.at[6])
    load_bk.start()

    load_act.wait()

    def norm_rows(r, carry):
        part = pl.ds(pl.multiple_of(r * 16, 16), 16)
        values = act[part, :].astype(F32)
        center = values - jnp.mean(values, axis=-1, keepdims=True)
        inverse = lax.rsqrt(jnp.mean(center * center, axis=-1, keepdims=True) + NORM_EPS)
        rows[d, part, :] = (center * inverse * ln_gain[...]).astype(BF16)
        return carry

    lax.fori_loop(0, TOK // 16, norm_rows, 0)
    pl.semaphore_wait(barrier, HIST - 1 + DP - 1)

    def remote(src, dst, send, recv, device):
        return pltpu.make_async_remote_copy(
            src_ref=src, dst_ref=dst, send_sem=send, recv_sem=recv, device_id=device, device_id_type=MESH
        )

    def ring_gather(buffer, half_rows, own, send, recv):
        right, left, sibling = (h, dpx(1, 0)), (h, dpx(3, 0)), (h, dpx(0, 1))
        low, high = pl.ds(0, half_rows), pl.ds(half_rows, half_rows)
        from_left, from_right, far = dpx(3, 0), dpx(1, 0), dpx(2, 0)
        specs = [
            (own, buffer.at[d], sibling),
            (own, buffer.at[d], right),
            (own, buffer.at[d], left),
            (buffer.at[from_left, low], buffer.at[from_left, low], right),
            (buffer.at[from_right, high], buffer.at[from_right, high], left),
            (buffer.at[from_left], buffer.at[from_left], sibling),
            (buffer.at[from_right], buffer.at[from_right], sibling),
            (buffer.at[far, low], buffer.at[far, low], sibling),
            (buffer.at[far, high], buffer.at[far, high], sibling),
        ]
        return [remote(s, t, send.at[i], recv.at[i], dev) for i, (s, t, dev) in enumerate(specs)]

    ring = ring_gather(rows, TOK // 2, rows.at[d], g_s, g_r)
    for i in (1, 2, 0):
        ring[i].start()

    def kv_copy(k):
        to = hist(k)
        return remote(cache_hbm.at[:, to], own_slab, kv_s.at[k], kv_r.at[k], (to, d))

    def bk_copy(k):
        to = hist(k)
        return remote(bucket_hbm.at[to], bks.at[h], bk_s.at[k], bk_r.at[k], (to, d))

    def send_cache(k, carry):
        bk_copy(k).start()
        kv_copy(k).start()
        return carry

    lax.fori_loop(1, HIST, send_cache, 0)

    def project(chip):
        part = pl.ds(pl.multiple_of(chip * 2, 2), 2)
        chip_rows = rows[part].reshape(2 * TOK, WIDTH)
        for j in range(4):
            pre = dot_nn(chip_rows, wts[j])
            sigmoid = 0.5 * jnp.tanh(0.5 * pre) + 0.5
            acted = pre * sigmoid
            if j == 0:
                pre_slope[part] = (sigmoid + acted * (1.0 - sigmoid)).reshape(2, TOK, COLS)
            sent[part, :, pl.ds(j * COLS, COLS)] = acted.astype(BF16).reshape(2, TOK, COLS)

    def pj_copy(k):
        to = dpo(k)
        return remote(sent.at[to], proj.at[d], pj_s.at[k], pj_r.at[k], (h, to))

    load_query.wait()
    load_frozen.wait()
    ring[0].wait_recv()
    project(x)
    pj_copy(1).start()
    own_proj = pltpu.make_async_copy(sent.at[d], proj.at[d], loc_sem.at[7])
    own_proj.start()
    ring[1].wait_recv()
    ring[3].start()
    ring[5].start()
    ring[2].wait_recv()
    ring[4].start()
    ring[6].start()
    ring[5].wait_recv()
    project(lax.rem(x + 3, 4))
    pj_copy(6).start()
    pj_copy(7).start()
    ring[6].wait_recv()
    project(lax.rem(x + 1, 4))
    pj_copy(2).start()
    pj_copy(3).start()
    ring[3].wait_recv()
    ring[7].start()
    ring[4].wait_recv()
    ring[8].start()
    ring[7].wait_recv()
    ring[8].wait_recv()
    project(lax.rem(x + 2, 4))
    pj_copy(4).start()
    pj_copy(5).start()

    wring = ring_gather(wout, WIDTH // 2, wout_hbm, w_s, w_r)
    for i in (1, 2, 0):
        wring[i].start()

    load_bk.wait()

    def wait_bk(k, carry):
        bk_copy(k).wait_recv()
        return carry

    lax.fori_loop(1, HIST, wait_bk, 0)
    levels = lax.broadcasted_iota(jnp.int32, (BUCKETS, TOK), 0)
    for q in range(4):
        ids = (bks[4 * q] + bks[4 * q + 1] + bks[4 * q + 2] + bks[4 * q + 3])[0:1, :]
        onehot[:, pl.ds(q * TOK, TOK)] = jnp.where(levels == ids, 1.0, 0.0).astype(BF16)
    onehot[:, pl.ds(CACHED, TOK)] = jnp.where(levels == new_bucket[...], 1.0, 0.0).astype(BF16)
    hot = onehot[...]
    bias_sum = jnp.zeros((HEADS, KEYS), F32)
    for term in reversed(three_parts(rab[...])):
        bias_sum = bias_sum + dot_nn(term, hot)
    bias[...] = bias_sum

    count = length[0, 0]
    share = 1.0 / jnp.full((1, TOK), count + TOK, jnp.int32).astype(F32)
    cached_pos = lax.broadcasted_iota(jnp.int32, (1, CACHED), 1)
    share_cached = jnp.where(cached_pos < count, jnp.concatenate([share] * 4, axis=1), 0.0)
    row_pos = lax.broadcasted_iota(jnp.int32, (TOK, TOK), 0)
    col_pos = lax.broadcasted_iota(jnp.int32, (TOK, TOK), 1)
    share_new = jnp.where(col_pos <= row_pos, jnp.broadcast_to(share, (TOK, TOK)), 0.0)

    def wait_pj(k, carry):
        pj_copy(k).wait_recv()
        return carry

    own_proj.wait()
    lax.fori_loop(1, DP, wait_pj, 0)

    def wait_kv(k, carry):
        kv_copy(k).wait_recv()
        return carry

    load_kv.wait()
    lax.fori_loop(1, HIST, wait_kv, 0)

    def attend(m, carry):
        for k in range(2):
            head = m * 2 + k
            lanes = pl.ds(pl.multiple_of(head * HEAD, HEAD), HEAD)
            query = proj[m, :, pl.ds(k * HEAD, HEAD)]
            value_new = proj[m, :, pl.ds(2 * COLS + k * HEAD, HEAD)]
            key_new = proj[m, :, pl.ds(3 * COLS + k * HEAD, HEAD)]
            key_bias = bias[pl.ds(head, 1), :]
            total = jnp.zeros((TOK, HEAD), F32)
            parts = (
                (kv[0, :, lanes], kv[1, :, lanes], pl.ds(0, CACHED), key_bias[:, :CACHED], share_cached),
                (key_new, value_new, pl.ds(CACHED, TOK), key_bias[:, CACHED:], share_new),
            )
            for keys, values, where, bias_part, share_part in parts:
                score = dot_nt(query, keys) * SCALE + bias_part
                sigmoid = 0.5 * jnp.tanh(0.5 * score) + 0.5
                weight = score * sigmoid * share_part
                slope[head, :, where] = sigmoid * share_part + weight * (1.0 - sigmoid)
                total = total + dot_nn(weight.astype(BF16), values)
            att[:, lanes] = total
        return carry

    lax.fori_loop(0, DP, attend, 0)

    load_cot.wait()
    load_wout.wait()

    def gated_part(m, first=False):
        lanes = pl.ds(pl.multiple_of(m * COLS, COLS), COLS)
        for n in range(4):
            cols = pl.ds(n * 512, 512)
            part = dot_nt(cot[:, lanes], wout[m, cols, :])
            grad_gated[:, cols] = part if first else grad_gated[:, cols] + part

    gated_part(d, True)
    wring[1].wait_recv()
    wring[3].start()
    wring[5].start()
    wring[2].wait_recv()
    wring[4].start()
    wring[6].start()
    wring[0].wait_recv()
    gated_part(dpx(0, 1))
    gated_part(dpx(3, 0))
    gated_part(dpx(1, 0))
    wring[5].wait_recv()
    gated_part(dpx(3, 1))
    wring[6].wait_recv()
    gated_part(dpx(1, 1))
    wring[3].wait_recv()
    wring[7].start()
    wring[4].wait_recv()
    wring[8].start()
    gated_part(dpx(2, 0))
    wring[7].wait_recv()
    wring[8].wait_recv()
    gated_part(dpx(2, 1))

    def gate_rows(r, carry):
        part = pl.ds(pl.multiple_of(r * 16, 16), 16)
        values = att[part, :]
        center = values - jnp.mean(values, axis=-1, keepdims=True)
        inverse = lax.rsqrt(jnp.mean(center * center, axis=-1, keepdims=True) + NORM_EPS)
        nhat = center * inverse
        gate = jnp.concatenate([proj[m, part, pl.ds(COLS, COLS)] for m in range(DP)], axis=1).astype(F32)
        scaled = gate * norm_gain[...]
        gated[part, :] = (nhat * scaled).astype(BF16)
        grad_hat = grad_gated[part, :] * scaled
        along = jnp.mean(grad_hat * nhat, axis=-1, keepdims=True)
        grad = inverse * (grad_hat - jnp.mean(grad_hat, axis=-1, keepdims=True) - nhat * along)
        grad_att[part, :] = grad.astype(BF16)
        return carry

    lax.fori_loop(0, TOK // 16, gate_rows, 0)

    def gq_copy(k):
        to = dpo(k)
        return remote(gq_out.at[to], gq_in.at[d], gq_s.at[k], gq_r.at[k], (h, to))

    def attend_back(m):
        for k in range(2):
            head = m * 2 + k
            lanes = pl.ds(pl.multiple_of(head * HEAD, HEAD), HEAD)
            value_new = proj[m, :, pl.ds(2 * COLS + k * HEAD, HEAD)]
            key_new = proj[m, :, pl.ds(3 * COLS + k * HEAD, HEAD)]
            grad = grad_att[:, lanes]
            total = jnp.zeros((TOK, HEAD), F32)
            parts = (
                (kv[0, :, lanes], kv[1, :, lanes], pl.ds(0, CACHED)),
                (key_new, value_new, pl.ds(CACHED, TOK)),
            )
            for keys, values, where in parts:
                grad_score = dot_nt(grad, values) * slope[head, :, where]
                tsum[head, :, where] = jnp.sum(grad_score.reshape(TOK // 8, 8, -1), axis=0)
                total = total + dot_nn(grad_score.astype(BF16), keys)
            gq_out[m, :, pl.ds(k * HEAD, HEAD)] = (total * SCALE).astype(BF16)

    def back_step(k, carry):
        attend_back(dpo(k))
        gq_copy(k).start()
        return carry

    lax.fori_loop(1, DP, back_step, 0)
    attend_back(d)
    gq_in[d] = gq_out[d]

    table = jnp.zeros((HEADS, BUCKETS), F32)
    for term in reversed(three_parts(jnp.sum(tsum[...], axis=1))):
        table = table + dot_nt(term, hot)
    tab_one[d] = table

    def t1_copy(k):
        return remote(tab_one.at[d], tab_one.at[d], t1_s.at[k], t1_r.at[k], (h, dpo(k)))

    def t2_copy(k):
        return remote(tab_two.at[h], tab_two.at[h], t2_s.at[k], t2_r.at[k], (hist(k), d))

    def run(copy, stop, what):
        def step(k, carry):
            one = copy(k)
            getattr(one, what)()
            return carry

        lax.fori_loop(1, stop, step, 0)

    run(t1_copy, DP, "start")
    run(gq_copy, DP, "wait_recv")

    for i in range(DP):
        grad_pre = (gq_in[i].astype(F32) * pre_slope[i]).astype(BF16)
        grad_pre_t[:, pl.ds(i * TOK, TOK)] = grad_pre.T

    def rs_copy(k):
        to = hist(k)
        return remote(rs_out.at[to], rs_in.at[h], rs_s.at[k], rs_r.at[k], (to, d))

    def slice_of(s):
        lanes = pl.ds(pl.multiple_of(s * TOK, TOK), TOK)
        return dot_nn(grad_pre_t[...], rows[:, :, lanes].reshape(DP * TOK, TOK))

    def rs_step(k, carry):
        to = hist(k)
        rs_out[to] = slice_of(to).astype(BF16)
        rs_copy(k).start()
        return carry

    lax.fori_loop(1, HIST, rs_step, 0)
    own_slice = slice_of(h)

    run(t1_copy, DP, "wait_recv")
    table = tab_one[0]
    for i in range(1, DP):
        table = table + tab_one[i]
    tab_two[h] = table
    run(t2_copy, HIST, "start")

    def out_cols(m, carry):
        lanes = pl.ds(pl.multiple_of(m * COLS, COLS), COLS)
        out_ref[:, lanes] = (dot_nn(gated[...], wout[m]) + act[:, lanes].astype(F32)).astype(BF16)
        return carry

    lax.fori_loop(0, DP, out_cols, 0)

    rs_in[h] = jnp.zeros((COLS, TOK), BF16)
    run(rs_copy, HIST, "wait_recv")
    total = own_slice
    for i in range(HIST):
        total = total + rs_in[i].astype(F32)
    ag_out[...] = total.T.astype(BF16)

    own_rows = gsum_hbm.at[pl.ds(pl.multiple_of(h * TOK, TOK), TOK), :]

    def ag_copy(k):
        return remote(ag_out, own_rows, ag_s.at[k], ag_r.at[k], (hist(k), d))

    run(ag_copy, HIST, "start")
    own_gsum = pltpu.make_async_copy(ag_out, own_rows, loc_sem.at[8])
    own_gsum.start()

    run(t2_copy, HIST, "wait_recv")
    table = tab_two[0]
    for i in range(1, HIST):
        table = table + tab_two[i]
    gtab_ref[...] = table

    for copy in ring + wring:
        copy.wait_send()
    for copy, stop in ((kv_copy, HIST), (bk_copy, HIST), (pj_copy, DP), (gq_copy, DP), (rs_copy, HIST), (t1_copy, DP), (t2_copy, HIST)):
        run(copy, stop, "wait_send")
    run(ag_copy, HIST, "wait_recv")
    run(ag_copy, HIST, "wait_send")
    own_gsum.wait()


def layer(actions, cotangent, cache, length, buckets, new_bucket, ln_gain, norm_gain, w_frozen, w_query, w_out, rab):
    any_space = pl.BlockSpec(memory_space=pl.ANY)
    vmem = pl.BlockSpec(memory_space=pltpu.VMEM)
    smem = pl.BlockSpec(memory_space=pltpu.SMEM)
    dma = pltpu.SemaphoreType.DMA
    sem_sizes = (9, HIST, HIST, HIST, HIST, 9, 9, DP, DP, 9, 9, DP, DP, HIST, HIST, HIST, HIST, DP, DP, HIST, HIST)
    return pl.pallas_call(
        kernel,
        out_shape=(
            jax.ShapeDtypeStruct((TOK, WIDTH), BF16),
            jax.ShapeDtypeStruct((WIDTH, COLS), BF16),
            jax.ShapeDtypeStruct((HEADS, BUCKETS), F32),
        ),
        in_specs=[any_space, any_space, any_space, smem, any_space, vmem, vmem, vmem, any_space, any_space, any_space, vmem],
        out_specs=(vmem, any_space, vmem),
        scratch_shapes=[
            pltpu.VMEM((TOK, WIDTH), BF16),
            pltpu.VMEM((TOK, WIDTH), BF16),
            pltpu.VMEM((4, WIDTH, COLS), BF16),
            pltpu.VMEM((DP, TOK, WIDTH), BF16),
            pltpu.VMEM((DP, TOK, COLS), F32),
            pltpu.VMEM((DP, TOK, 4 * COLS), BF16),
            pltpu.VMEM((DP, TOK, 4 * COLS), BF16),
            pltpu.VMEM((2, CACHED, WIDTH), BF16),
            pltpu.VMEM((HIST, 8, TOK), jnp.int32),
            pltpu.VMEM((BUCKETS, KEYS), BF16),
            pltpu.VMEM((HEADS, KEYS), F32),
            pltpu.VMEM((TOK, WIDTH), F32),
            pltpu.VMEM((HEADS, TOK, KEYS), F32),
            pltpu.VMEM((DP, WIDTH, COLS), BF16),
            pltpu.VMEM((TOK, WIDTH), F32),
            pltpu.VMEM((TOK, WIDTH), BF16),
            pltpu.VMEM((TOK, WIDTH), BF16),
            pltpu.VMEM((HEADS, 8, KEYS), F32),
            pltpu.VMEM((DP, TOK, COLS), BF16),
            pltpu.VMEM((DP, TOK, COLS), BF16),
            pltpu.VMEM((COLS, DP * TOK), BF16),
            pltpu.VMEM((HIST, COLS, TOK), BF16),
            pltpu.VMEM((HIST, COLS, TOK), BF16),
            pltpu.VMEM((TOK, COLS), BF16),
            pltpu.VMEM((DP, HEADS, BUCKETS), F32),
            pltpu.VMEM((HIST, HEADS, BUCKETS), F32),
        ]
        + [dma((n,)) for n in sem_sizes],
        compiler_params=pltpu.CompilerParams(collective_id=0, has_side_effects=True, vmem_limit_bytes=60 * 1024 * 1024),
        name="layer",
    )(actions, cotangent, cache, length, buckets, new_bucket, ln_gain, norm_gain, w_frozen, w_query, w_out, rab)


def shards(
    actions, cotangent, cache_kv, cache_len, cache_bucket, new_bucket, ln_gain, norm_gain,
    w_frozen, w_query, query_m, query_v, w_out, rab_table, rab_m, rab_v,
):
    lane = lax.broadcasted_iota(jnp.int32, (HIST, 8, 4 * SLAB), 2)
    mine = lane // SLAB == lax.axis_index("history") % 4
    tiled = jnp.tile(cache_bucket.reshape(HIST, 1, SLAB), (1, 8, 4))
    buckets = jnp.where(mine, tiled, 0)
    result, grad_sum, grad_table = layer(
        actions.reshape(TOK, WIDTH),
        cotangent.reshape(TOK, WIDTH),
        cache_kv.reshape(2, HIST, SLAB, WIDTH),
        cache_len.reshape(1, 1),
        buckets,
        new_bucket.reshape(1, TOK),
        ln_gain.reshape(1, WIDTH),
        norm_gain.reshape(1, WIDTH),
        w_frozen,
        w_query,
        w_out,
        rab_table,
    )
    query_new, query_m_new, query_v_new = adam_update(w_query, query_m, query_v, grad_sum.astype(F32))
    rab_new, rab_m_new, rab_v_new = adam_update(rab_table, rab_m, rab_v, grad_table)
    return (result.reshape(actions.shape), query_new, query_m_new, query_v_new, rab_new, rab_m_new, rab_v_new)


def solution(mesh):
    placed = (
        P("history", "dp", None, None),
        P("history", "dp", None, None),
        P(None, None, "dp", "history", None),
        P("history", "dp"),
        P(None, "dp", "history"),
        P("history", "dp", None),
        P(),
        P(),
        P(None, None, "dp"),
        P(None, "dp"),
        P(None, "dp"),
        P(None, "dp"),
        P(None, "dp"),
        P(),
        P(),
        P(),
    )
    return jax.shard_map(
        shards,
        mesh=mesh,
        in_specs=placed,
        out_specs=(
            P("history", "dp", None, None),
            P(None, "dp"),
            P(None, "dp"),
            P(None, "dp"),
            P(),
            P(),
            P(),
        ),
        check_vma=False,
    )
```

```python
import functools

import jax
import jax.numpy as jnp
from jax import lax
from jax.experimental import pallas as pl
from jax.experimental.pallas import tpu as pltpu
from jax.sharding import PartitionSpec as P

BETA_ONE = 0.9
BETA_TWO = 0.95
LEARN_RATE = 0.001
ADAM_EPS = 1e-08
NORM_EPS = 1e-05

MESH = pl.DeviceIdType.MESH
F32 = jnp.float32
BF16 = jnp.bfloat16

TOK = 128
WIDTH = 2048
COLS = 256
HEAD = 128
HEADS = 16
BUCKETS = 128
HIST = 16
DP = 8
SLAB = 32
CACHED = HIST * SLAB
KEYS = CACHED + TOK
SCALE = HEAD ** (-0.5)
KV_COPIES = 4 * (HIST - 1) + 1
KV_HALF = 2 * (HIST - 1) + 1
LINK_ORDER = (1, 4, 3, 12, 2, 8, 5, 15, 7, 13, 6, 9, 14, 11, 10)


def adam_update(weight, moment_one, moment_two, gradient):
    first_new = BETA_ONE * moment_one + (1.0 - BETA_ONE) * gradient
    second_new = BETA_TWO * moment_two + (1.0 - BETA_TWO) * gradient * gradient
    stepped = weight.astype(F32) - LEARN_RATE * first_new / (jnp.sqrt(second_new) + ADAM_EPS)
    return (stepped.astype(weight.dtype), first_new, second_new)


def dot_nn(a, b):
    return jnp.dot(a, b, preferred_element_type=F32)


def dot_nt(a, b):
    return lax.dot_general(a, b, (((1,), (1,)), ((), ())), preferred_element_type=F32)


def three_parts(values):
    first = values.astype(BF16)
    rest = values - first.astype(F32)
    second = rest.astype(BF16)
    third = (rest - second.astype(F32)).astype(BF16)
    return first, second, third


def silu_slope(values):
    sigmoid = 0.5 * jnp.tanh(0.5 * values) + 0.5
    return sigmoid * (1.0 + values * (1.0 - sigmoid))


def kernel(
    act_hbm, cot_hbm, cache_hbm, length, buckets, new_bucket, ln_gain, norm_gain, frozen_hbm, query_hbm, wout_hbm, rab,
    out_ref, gsum_hbm, gtab_ref,
    act, cot, wts, rows, pre_slope, sent, proj, kv, bk_out, bks, onehot, bias, att, slope, wout, grad_gated, gated, grad_att,
    tsum, gq_out, gq_in, grad_pre_t, rs_out, rs_in, ag_out, tab_one, tab_two,
    loc_sem, kv_s, kv_r, bk_s, bk_r, g_s, g_r, pj_s, pj_r, w_s, w_r, px_s, px_r, p1_s, p1_r, p2_s, p2_r, p3_s, p3_r, gq_s, gq_r, rs_s, rs_r, ag_s, ag_r, t1_s, t1_r, t2_s, t2_r,
):
    h = lax.axis_index("history")
    d = lax.axis_index("dp")
    z, y = h // 4, lax.rem(h, 4)
    x, c = d // 2, lax.rem(d, 2)

    def hist(k):
        return lax.rem(z + k // 4, 4) * 4 + lax.rem(y + lax.rem(k, 4), 4)

    def dpx(kx, kc):
        return lax.rem(x + kx, 4) * 2 + lax.rem(c + kc, 2)

    def dpo(k):
        return lax.rem(x + k // 2, 4) * 2 + lax.rem(c + lax.rem(k, 2), 2)

    barrier = pltpu.get_barrier_semaphore()

    def greet_hist(k, carry):
        pl.semaphore_signal(barrier, inc=1, device_id=(hist(k), d), device_id_type=MESH)
        return carry

    def greet_dp(k, carry):
        pl.semaphore_signal(barrier, inc=1, device_id=(h, dpo(k)), device_id_type=MESH)
        return carry

    lax.fori_loop(1, DP, greet_dp, 0)
    lax.fori_loop(1, HIST, greet_hist, 0)

    load_act = pltpu.make_async_copy(act_hbm, act, loc_sem.at[0])
    load_act.start()
    load_query = pltpu.make_async_copy(query_hbm, wts.at[0], loc_sem.at[1])
    load_query.start()
    load_frozen = pltpu.make_async_copy(frozen_hbm, wts.at[pl.ds(1, 3)], loc_sem.at[2])
    load_frozen.start()
    load_cot = pltpu.make_async_copy(cot_hbm, cot, loc_sem.at[3])
    load_cot.start()
    load_wout = pltpu.make_async_copy(wout_hbm, wout.at[d], loc_sem.at[4])
    load_wout.start()
    own_slab = kv.at[:, pl.ds(pl.multiple_of(h * SLAB, SLAB), SLAB), :]
    load_kv = pltpu.make_async_copy(cache_hbm.at[:, h], own_slab, loc_sem.at[5])
    load_kv.start()
    lane = lax.broadcasted_iota(jnp.int32, (HIST, TOK), 1)
    placed = jnp.where(lane // SLAB == y, jnp.concatenate([buckets[:, 0, :]] * 4, axis=1), 0)
    for u in range(HIST):
        bk_out[u] = jnp.broadcast_to(placed[u : u + 1, :], (8, TOK))

    load_act.wait()

    def norm_rows(r, carry):
        part = pl.ds(pl.multiple_of(r * 16, 16), 16)
        values = act[part, :].astype(F32)
        center = values - jnp.mean(values, axis=-1, keepdims=True)
        inverse = lax.rsqrt(jnp.mean(center * center, axis=-1, keepdims=True) + NORM_EPS)
        rows[d, part, :] = (center * inverse * ln_gain[...]).astype(BF16)
        return carry

    lax.fori_loop(0, TOK // 16, norm_rows, 0)
    pl.semaphore_wait(barrier, HIST - 1 + DP - 1)

    def remote(src, dst, send, recv, device):
        return pltpu.make_async_remote_copy(
            src_ref=src, dst_ref=dst, send_sem=send, recv_sem=recv, device_id=device, device_id_type=MESH
        )

    def ring_gather(block, half, own, send, recv, first=0):
        right, left, sibling = (h, dpx(1, 0)), (h, dpx(3, 0)), (h, dpx(0, 1))
        from_left, from_right, far = dpx(3, 0), dpx(1, 0), dpx(2, 0)
        specs = [
            (own, block(d), sibling),
            (own, block(d), right),
            (own, block(d), left),
            (half(from_left, 0), half(from_left, 0), right),
            (half(from_right, 1), half(from_right, 1), left),
            (block(from_left), block(from_left), sibling),
            (block(from_right), block(from_right), sibling),
            (half(far, 0), half(far, 0), sibling),
            (half(far, 1), half(far, 1), sibling),
        ]
        numbered = list(enumerate(specs))[first:]
        return {i: remote(s, t, send.at[i], recv.at[i], dev) for i, (s, t, dev) in numbered}

    ring = ring_gather(
        lambda i: rows.at[i],
        lambda i, k: rows.at[i, pl.ds(k * (TOK // 2), TOK // 2)],
        rows.at[d],
        g_s,
        g_r,
    )
    for i in (1, 2, 0):
        ring[i].start()

    def kv_copy(i):
        piece, turn = divmod(i - 1, HIST - 1)
        to = hist(LINK_ORDER[turn])
        part, low = piece % 2, piece // 2 * 16
        src = cache_hbm.at[part, to, pl.ds(low, 16)]
        dst = kv.at[part, pl.ds(pl.multiple_of(h * SLAB + low, 16), 16), :]
        return remote(src, dst, kv_s.at[i], kv_r.at[i], (to, d))

    def bk_copy(k):
        to = hist(k)
        return remote(bk_out.at[to], bks.at[h], bk_s.at[k], bk_r.at[k], (to, d))

    def plane_x(k):
        return remote(wout_hbm.at[0, z, y], wout.at[d, 0, z, y], px_s.at[k], px_r.at[k], (h, dpx(k, 0)))

    def plane_one(k, kx):
        slot, i = dpx(kx, 0), 3 * (k - 1) + kx - 1
        over_z, over_y = wout.at[slot, 0, z, y, 0], wout.at[slot, 0, z, y, 1]
        to_z, to_y = lax.rem(z + k, 4) * 4 + y, z * 4 + lax.rem(y + k, 4)
        return (
            remote(over_z, over_z, p1_s.at[i], p1_r.at[i], (to_z, d)),
            remote(over_y, over_y, p1_s.at[9 + i], p1_r.at[9 + i], (to_y, d)),
        )

    def plane_two(k, kx):
        slot, i = dpx(kx, 0), 3 * (k - 1) + kx - 1
        over_y, over_z = wout.at[slot, 0, :, y, 0], wout.at[slot, 0, z, :, 1]
        to_z, to_y = lax.rem(z + k, 4) * 4 + y, z * 4 + lax.rem(y + k, 4)
        return (
            remote(over_y, over_y, p2_s.at[i], p2_r.at[i], (to_y, d)),
            remote(over_z, over_z, p2_s.at[9 + i], p2_r.at[9 + i], (to_z, d)),
        )

    def plane_share(kx):
        block = wout.at[dpx(kx, 0), 0]
        return remote(block, block, p3_s.at[kx], p3_r.at[kx], (h, dpx(0, 1)))

    own_wout = remote(wout_hbm, wout.at[d], p3_s.at[0], p3_r.at[0], (h, dpx(0, 1)))
    wring = ring_gather(
        lambda i: wout.at[i, 1],
        lambda i, k: wout.at[i, 1, pl.ds(2 * k, 2)],
        wout_hbm.at[1],
        w_s,
        w_r,
        first=1,
    )
    plane_steps = [(k, kx) for k in (1, 3, 2) for kx in (1, 2, 3)]
    for k in range(1, 4):
        plane_x(k).start()

    def send_bk(k, carry):
        bk_copy(k).start()
        return carry

    lax.fori_loop(1, HIST, send_bk, 0)
    for i in range(1, KV_HALF):
        kv_copy(i).start()

    def project(chip):
        part = pl.ds(pl.multiple_of(chip * 2, 2), 2)
        chip_rows = rows[part].reshape(2 * TOK, WIDTH)
        for j in range(4):
            pre = dot_nn(chip_rows, wts[j])
            sigmoid = 0.5 * jnp.tanh(0.5 * pre) + 0.5
            acted = pre * sigmoid
            if j == 0:
                pre_slope[part] = (sigmoid + acted * (1.0 - sigmoid)).reshape(2, TOK, COLS)
            sent[part, :, pl.ds(j * COLS, COLS)] = acted.astype(BF16).reshape(2, TOK, COLS)

    def pj_copy(k):
        to = dpo(k)
        return remote(sent.at[to], proj.at[d], pj_s.at[k], pj_r.at[k], (h, to))

    load_query.wait()
    load_frozen.wait()
    ring[0].wait_recv()
    project(x)
    pj_copy(1).start()
    own_proj = pltpu.make_async_copy(sent.at[d], proj.at[d], loc_sem.at[7])
    own_proj.start()
    for k in range(1, 4):
        plane_x(k).wait_recv()
    for step in plane_steps:
        for copy in plane_one(*step):
            copy.start()
    for i in range(KV_HALF, KV_COPIES):
        kv_copy(i).start()
    ring[1].wait_recv()
    ring[3].start()
    ring[5].start()
    ring[2].wait_recv()
    ring[4].start()
    ring[6].start()
    ring[5].wait_recv()
    project(lax.rem(x + 3, 4))
    pj_copy(6).start()
    pj_copy(7).start()
    ring[6].wait_recv()
    project(lax.rem(x + 1, 4))
    pj_copy(2).start()
    pj_copy(3).start()
    for i in (1, 2):
        wring[i].start()
    own_wout.start()
    ring[3].wait_recv()
    ring[7].start()
    ring[4].wait_recv()
    ring[8].start()
    ring[7].wait_recv()
    ring[8].wait_recv()
    project(lax.rem(x + 2, 4))
    pj_copy(4).start()
    pj_copy(5).start()

    for step in plane_steps:
        for copy in plane_one(*step):
            copy.wait_recv()
    for step in plane_steps:
        for copy in plane_two(*step):
            copy.start()

    bks[h] = bk_out[h]

    def wait_bk(k, carry):
        bk_copy(k).wait_recv()
        return carry

    lax.fori_loop(1, HIST, wait_bk, 0)
    levels = lax.broadcasted_iota(jnp.int32, (BUCKETS, TOK), 0)
    for q in range(4):
        ids = (bks[4 * q] + bks[4 * q + 1] + bks[4 * q + 2] + bks[4 * q + 3])[0:1, :]
        onehot[:, pl.ds(q * TOK, TOK)] = jnp.where(levels == ids, 1.0, 0.0).astype(BF16)
    onehot[:, pl.ds(CACHED, TOK)] = jnp.where(levels == new_bucket[...], 1.0, 0.0).astype(BF16)
    hot = onehot[...]
    bias_sum = jnp.zeros((HEADS, KEYS), F32)
    for term in reversed(three_parts(rab[...])):
        bias_sum = bias_sum + dot_nn(term, hot)
    bias[...] = bias_sum

    count = length[0, 0]
    share = 1.0 / jnp.full((1, TOK), count + TOK, jnp.int32).astype(F32)
    cached_pos = lax.broadcasted_iota(jnp.int32, (1, CACHED), 1)
    share_cached = jnp.where(cached_pos < count, jnp.concatenate([share] * 4, axis=1), 0.0)
    row_pos = lax.broadcasted_iota(jnp.int32, (TOK, TOK), 0)
    col_pos = lax.broadcasted_iota(jnp.int32, (TOK, TOK), 1)
    share_new = jnp.where(col_pos <= row_pos, jnp.broadcast_to(share, (TOK, TOK)), 0.0)

    for i in (1, 2):
        wring[i].wait_recv()
        wring[i + 2].start()
        wring[i + 4].start()

    def wait_pj(k, carry):
        pj_copy(k).wait_recv()
        return carry

    own_proj.wait()
    lax.fori_loop(1, DP, wait_pj, 0)

    load_kv.wait()
    for i in range(1, KV_COPIES):
        kv_copy(i).wait_recv()

    def attend(m, carry):
        for k in range(2):
            head = m * 2 + k
            lanes = pl.ds(pl.multiple_of(head * HEAD, HEAD), HEAD)
            query = proj[m, :, pl.ds(k * HEAD, HEAD)]
            value_new = proj[m, :, pl.ds(2 * COLS + k * HEAD, HEAD)]
            key_new = proj[m, :, pl.ds(3 * COLS + k * HEAD, HEAD)]
            key_bias = bias[pl.ds(head, 1), :]
            total = jnp.zeros((TOK, HEAD), F32)
            parts = (
                (kv[0, :, lanes], kv[1, :, lanes], pl.ds(0, CACHED), key_bias[:, :CACHED], share_cached),
                (key_new, value_new, pl.ds(CACHED, TOK), key_bias[:, CACHED:], share_new),
            )
            for keys, values, where, bias_part, share_part in parts:
                score = dot_nt(query, keys) * SCALE + bias_part
                sigmoid = 0.5 * jnp.tanh(0.5 * score) + 0.5
                weight = score * sigmoid * share_part
                slope[head, :, where] = sigmoid * share_part + weight * (1.0 - sigmoid)
                total = total + dot_nn(weight.astype(BF16), values)
            att[:, lanes] = total
        return carry

    lax.fori_loop(0, DP // 2, attend, 0)
    for step in plane_steps:
        for copy in plane_two(*step):
            copy.wait_recv()
    for k in range(1, 4):
        plane_share(k).start()
    for i in (3, 4):
        wring[i].wait_recv()
        wring[i + 4].start()
    lax.fori_loop(DP // 2, DP, attend, 0)

    load_cot.wait()
    load_wout.wait()

    def gated_part(m, half, first=False):
        lanes = pl.ds(pl.multiple_of(m * COLS, COLS), COLS)
        for n in range(2):
            cols = pl.ds(half * 1024 + n * 512, 512)
            part = dot_nt(cot[:, lanes], wout[m, half, pl.ds(2 * n, 2)].reshape(512, COLS))
            grad_gated[:, cols] = part if first else grad_gated[:, cols] + part

    gated_part(d, 0, True)
    gated_part(d, 1, True)
    own_wout.wait_recv()
    gated_part(dpx(0, 1), 0)
    gated_part(dpx(0, 1), 1)
    for k in (3, 1, 2):
        gated_part(dpx(k, 0), 0)
    for k in (3, 1, 2):
        plane_share(k).wait_recv()
        gated_part(dpx(k, 1), 0)
    gated_part(dpx(3, 0), 1)
    gated_part(dpx(1, 0), 1)
    wring[5].wait_recv()
    gated_part(dpx(3, 1), 1)
    wring[6].wait_recv()
    gated_part(dpx(1, 1), 1)
    gated_part(dpx(2, 0), 1)
    wring[7].wait_recv()
    wring[8].wait_recv()
    gated_part(dpx(2, 1), 1)

    def gate_rows(r, carry):
        part = pl.ds(pl.multiple_of(r * 16, 16), 16)
        values = att[part, :]
        center = values - jnp.mean(values, axis=-1, keepdims=True)
        inverse = lax.rsqrt(jnp.mean(center * center, axis=-1, keepdims=True) + NORM_EPS)
        nhat = center * inverse
        gate = jnp.concatenate([proj[m, part, pl.ds(COLS, COLS)] for m in range(DP)], axis=1).astype(F32)
        scaled = gate * norm_gain[...]
        gated[part, :] = (nhat * scaled).astype(BF16)
        grad_hat = grad_gated[part, :] * scaled
        along = jnp.mean(grad_hat * nhat, axis=-1, keepdims=True)
        grad = inverse * (grad_hat - jnp.mean(grad_hat, axis=-1, keepdims=True) - nhat * along)
        grad_att[part, :] = grad.astype(BF16)
        return carry

    lax.fori_loop(0, TOK // 16, gate_rows, 0)

    def gq_copy(half, k):
        to, i = dpo(k), half * DP + k
        return remote(gq_out.at[half, to], gq_in.at[half, d], gq_s.at[i], gq_r.at[i], (h, to))

    def attend_back(m, k):
        head = m * 2 + k
        lanes = pl.ds(pl.multiple_of(head * HEAD, HEAD), HEAD)
        value_new = proj[m, :, pl.ds(2 * COLS + k * HEAD, HEAD)]
        key_new = proj[m, :, pl.ds(3 * COLS + k * HEAD, HEAD)]
        grad = grad_att[:, lanes]
        total = jnp.zeros((TOK, HEAD), F32)
        parts = (
            (kv[0, :, lanes], kv[1, :, lanes], pl.ds(0, CACHED)),
            (key_new, value_new, pl.ds(CACHED, TOK)),
        )
        for keys, values, where in parts:
            grad_score = dot_nt(grad, values) * slope[head, :, where]
            tsum[head, :, where] = jnp.sum(grad_score.reshape(TOK // 8, 8, -1), axis=0)
            total = total + dot_nn(grad_score.astype(BF16), keys)
        gq_out[k, m] = (total * SCALE).astype(BF16)

    def back_steps(half, first, stop):
        def step(k, carry):
            attend_back(dpo(k), half)
            gq_copy(half, k).start()
            return carry

        lax.fori_loop(first, stop, step, 0)

    def run(copy, stop, what, *half):
        def step(k, carry):
            getattr(copy(*half, k), what)()
            return carry

        lax.fori_loop(1, stop, step, 0)

    def own_back(half):
        attend_back(d, half)
        gq_in[half, d] = gq_out[half, d]

    def rs_copy(half, k):
        to, i = hist(k), half * HIST + k
        return remote(rs_out.at[half, to], rs_in.at[half, h], rs_s.at[i], rs_r.at[i], (to, d))

    def weight_half(half):
        run(gq_copy, DP, "wait_recv", half)
        for i in range(DP):
            pre = pre_slope[i, :, pl.ds(half * HEAD, HEAD)]
            grad_pre_t[half, :, pl.ds(i * TOK, TOK)] = (gq_in[half, i].astype(F32) * pre).astype(BF16).T
        for kz in (1, 3, 2, 0):
            to_z = lax.rem(z + kz, 4)
            lanes = pl.ds(pl.multiple_of(to_z * 512, 512), 512)
            piece = dot_nn(grad_pre_t[half], rows[:, :, lanes].reshape(DP * TOK, 512)).astype(BF16)
            for j in range(4):
                rs_out[half, to_z * 4 + j] = piece[:, j * TOK : (j + 1) * TOK]
            for ky in (1, 0, 3, 2):
                if kz or ky:
                    rs_copy(half, kz * 4 + ky).start()
        rs_in[half, h] = rs_out[half, h]

    def ag_copy(half, k):
        block = gsum_hbm.at[pl.ds(pl.multiple_of(h * TOK, TOK), TOK), pl.ds(half * HEAD, HEAD)]
        i = half * HIST + k
        return remote(ag_out.at[half], block, ag_s.at[i], ag_r.at[i], (hist(k), d))

    def own_gsum(half):
        block = gsum_hbm.at[pl.ds(pl.multiple_of(h * TOK, TOK), TOK), pl.ds(half * HEAD, HEAD)]
        return pltpu.make_async_copy(ag_out.at[half], block, loc_sem.at[8 + half])

    def gather_half(half):
        run(rs_copy, HIST, "wait_recv", half)
        total = rs_in[half, 0].astype(F32)
        for i in range(1, HIST):
            total = total + rs_in[half, i].astype(F32)
        ag_out[half] = total.T.astype(BF16)
        for k in LINK_ORDER:
            ag_copy(half, k).start()
        own_gsum(half).start()

    def out_cols(m, carry):
        lanes = pl.ds(pl.multiple_of(m * COLS, COLS), COLS)
        product = dot_nn(gated[...], wout[m].reshape(WIDTH, COLS))
        out_ref[:, lanes] = (product + act[:, lanes].astype(F32)).astype(BF16)
        return carry

    def t1_copy(k):
        return remote(tab_one.at[d], tab_one.at[d], t1_s.at[k], t1_r.at[k], (h, dpo(k)))

    def t2_copy(k):
        return remote(tab_two.at[h], tab_two.at[h], t2_s.at[k], t2_r.at[k], (hist(k), d))

    back_steps(0, 1, DP)
    own_back(0)
    back_steps(1, 1, 4)
    weight_half(0)
    back_steps(1, 4, DP)
    own_back(1)

    table = jnp.zeros((HEADS, BUCKETS), F32)
    for term in reversed(three_parts(jnp.sum(tsum[...], axis=1))):
        table = table + dot_nt(term, hot)
    tab_one[d] = table
    run(t1_copy, DP, "start")

    lax.fori_loop(0, DP // 2, out_cols, 0)
    weight_half(1)
    gather_half(0)

    run(t1_copy, DP, "wait_recv")
    table = tab_one[0]
    for i in range(1, DP):
        table = table + tab_one[i]
    tab_two[h] = table
    run(t2_copy, HIST, "start")

    lax.fori_loop(DP // 2, DP, out_cols, 0)
    gather_half(1)

    run(t2_copy, HIST, "wait_recv")
    table = tab_two[0]
    for i in range(1, HIST):
        table = table + tab_two[i]
    gtab_ref[...] = table

    for copy in [*ring.values(), *wring.values(), own_wout]:
        copy.wait_send()
    for k in range(1, 4):
        plane_x(k).wait_send()
        plane_share(k).wait_send()
    for step in plane_steps:
        for copy in plane_one(*step) + plane_two(*step):
            copy.wait_send()
    for i in range(1, KV_COPIES):
        kv_copy(i).wait_send()
    for copy, stop in ((bk_copy, HIST), (pj_copy, DP), (t1_copy, DP), (t2_copy, HIST)):
        run(copy, stop, "wait_send")
    for half in range(2):
        run(gq_copy, DP, "wait_send", half)
        run(rs_copy, HIST, "wait_send", half)
        run(ag_copy, HIST, "wait_recv", half)
        run(ag_copy, HIST, "wait_send", half)
        own_gsum(half).wait()


def layer(actions, cotangent, cache, length, buckets, new_bucket, ln_gain, norm_gain, w_frozen, w_query, w_out, rab):
    any_space = pl.BlockSpec(memory_space=pl.ANY)
    vmem = pl.BlockSpec(memory_space=pltpu.VMEM)
    smem = pl.BlockSpec(memory_space=pltpu.SMEM)
    dma = pltpu.SemaphoreType.DMA
    sem_sizes = (10, KV_COPIES, KV_COPIES, HIST, HIST, 9, 9, DP, DP, 9, 9, 4, 4, 18, 18, 18, 18, 4, 4, 2 * DP, 2 * DP, 2 * HIST, 2 * HIST, 2 * HIST, 2 * HIST, DP, DP, HIST, HIST)
    return pl.pallas_call(
        kernel,
        out_shape=(
            jax.ShapeDtypeStruct((TOK, WIDTH), BF16),
            jax.ShapeDtypeStruct((WIDTH, COLS), BF16),
            jax.ShapeDtypeStruct((HEADS, BUCKETS), F32),
        ),
        in_specs=[any_space, any_space, any_space, smem, vmem, vmem, vmem, vmem, any_space, any_space, any_space, vmem],
        out_specs=(vmem, any_space, vmem),
        scratch_shapes=[
            pltpu.VMEM((TOK, WIDTH), BF16),
            pltpu.VMEM((TOK, WIDTH), BF16),
            pltpu.VMEM((4, WIDTH, COLS), BF16),
            pltpu.VMEM((DP, TOK, WIDTH), BF16),
            pltpu.VMEM((DP, TOK, COLS), F32),
            pltpu.VMEM((DP, TOK, 4 * COLS), BF16),
            pltpu.VMEM((DP, TOK, 4 * COLS), BF16),
            pltpu.VMEM((2, CACHED, WIDTH), BF16),
            pltpu.VMEM((HIST, 8, TOK), jnp.int32),
        pltpu.VMEM((HIST, 8, TOK), jnp.int32),
            pltpu.VMEM((BUCKETS, KEYS), BF16),
            pltpu.VMEM((HEADS, KEYS), F32),
            pltpu.VMEM((TOK, WIDTH), F32),
            pltpu.VMEM((HEADS, TOK, KEYS), F32),
            pltpu.VMEM((DP, 2, 4, 4, 2, 32, COLS), BF16),
            pltpu.VMEM((TOK, WIDTH), F32),
            pltpu.VMEM((TOK, WIDTH), BF16),
            pltpu.VMEM((TOK, WIDTH), BF16),
            pltpu.VMEM((HEADS, 8, KEYS), F32),
            pltpu.VMEM((2, DP, TOK, HEAD), BF16),
            pltpu.VMEM((2, DP, TOK, HEAD), BF16),
            pltpu.VMEM((2, HEAD, DP * TOK), BF16),
            pltpu.VMEM((2, HIST, HEAD, TOK), BF16),
            pltpu.VMEM((2, HIST, HEAD, TOK), BF16),
            pltpu.VMEM((2, TOK, HEAD), BF16),
            pltpu.VMEM((DP, HEADS, BUCKETS), F32),
            pltpu.VMEM((HIST, HEADS, BUCKETS), F32),
        ]
        + [dma((n,)) for n in sem_sizes],
        compiler_params=pltpu.CompilerParams(collective_id=0, has_side_effects=True, vmem_limit_bytes=60 * 1024 * 1024),
        name="layer",
    )(actions, cotangent, cache, length, buckets, new_bucket, ln_gain, norm_gain, w_frozen, w_query, w_out, rab)


def shards(
    actions, cotangent, cache_kv, cache_len, cache_bucket, new_bucket, ln_gain, norm_gain,
    w_frozen, w_query, query_m, query_v, w_out, rab_table, rab_m, rab_v,
):
    result, grad_sum, grad_table = layer(
        actions.reshape(TOK, WIDTH),
        cotangent.reshape(TOK, WIDTH),
        cache_kv.reshape(2, HIST, SLAB, WIDTH),
        cache_len.reshape(1, 1),
        cache_bucket,
        new_bucket.reshape(1, TOK),
        ln_gain.reshape(1, WIDTH),
        norm_gain.reshape(1, WIDTH),
        w_frozen,
        w_query,
        w_out.reshape(2, 4, 4, 2, 32, COLS),
        rab_table,
    )
    query_new, query_m_new, query_v_new = adam_update(w_query, query_m, query_v, grad_sum.astype(F32))
    rab_new, rab_m_new, rab_v_new = adam_update(rab_table, rab_m, rab_v, grad_table)
    return (result.reshape(actions.shape), query_new, query_m_new, query_v_new, rab_new, rab_m_new, rab_v_new)


def solution(mesh):
    placed = (
        P("history", "dp", None, None),
        P("history", "dp", None, None),
        P(None, None, "dp", "history", None),
        P("history", "dp"),
        P(None, "dp", "history"),
        P("history", "dp", None),
        P(),
        P(),
        P(None, None, "dp"),
        P(None, "dp"),
        P(None, "dp"),
        P(None, "dp"),
        P(None, "dp"),
        P(),
        P(),
        P(),
    )
    return jax.shard_map(
        shards,
        mesh=mesh,
        in_specs=placed,
        out_specs=(
            P("history", "dp", None, None),
            P(None, "dp"),
            P(None, "dp"),
            P(None, "dp"),
            P(),
            P(),
            P(),
        ),
        check_vma=False,
    )
```

```python
import functools

import jax
import jax.numpy as jnp
from jax import lax
from jax.experimental import pallas as pl
from jax.experimental.pallas import tpu as pltpu
from jax.sharding import PartitionSpec as P

BETA_ONE = 0.9
BETA_TWO = 0.95
LEARN_RATE = 0.001
ADAM_EPS = 1e-08
NORM_EPS = 1e-05

MESH = pl.DeviceIdType.MESH
F32 = jnp.float32
BF16 = jnp.bfloat16

TOK = 128
WIDTH = 2048
COLS = 256
HEAD = 128
HEADS = 16
BUCKETS = 128
HIST = 16
DP = 8
SLAB = 32
CACHED = HIST * SLAB
KEYS = CACHED + TOK
SCALE = HEAD ** (-0.5)
KV_COPIES = 4 * (HIST - 1) + 1
KV_HALF = 2 * (HIST - 1) + 1
LINK_ORDER = (1, 4, 3, 12, 2, 8, 5, 15, 7, 13, 6, 9, 14, 11, 10)


def adam_update(weight, moment_one, moment_two, gradient):
    first_new = BETA_ONE * moment_one + (1.0 - BETA_ONE) * gradient
    second_new = BETA_TWO * moment_two + (1.0 - BETA_TWO) * gradient * gradient
    stepped = weight.astype(F32) - LEARN_RATE * first_new / (jnp.sqrt(second_new) + ADAM_EPS)
    return (stepped.astype(weight.dtype), first_new, second_new)


def dot_nn(a, b):
    return jnp.dot(a, b, preferred_element_type=F32)


def dot_nt(a, b):
    return lax.dot_general(a, b, (((1,), (1,)), ((), ())), preferred_element_type=F32)


def three_parts(values):
    first = values.astype(BF16)
    rest = values - first.astype(F32)
    second = rest.astype(BF16)
    third = (rest - second.astype(F32)).astype(BF16)
    return first, second, third


def silu_slope(values):
    sigmoid = 0.5 * jnp.tanh(0.5 * values) + 0.5
    return sigmoid * (1.0 + values * (1.0 - sigmoid))


def kernel(
    act_hbm, cot_hbm, cache_hbm, length, buckets, new_bucket, ln_gain, norm_gain, frozen_hbm, query_hbm, wout_hbm, rab,
    out_ref, gsum_hbm, gtab_ref,
    act, cot, wts, rows, pre_slope, sent, proj, kv, bk_out, bks, onehot, bias, att, slope, wout, grad_gated, gated, grad_att,
    tsum, gq_out, gq_in, grad_pre_t, rs_out, r1_in, r2_out, r2_in, ag_buf, tab_one, tab_two,
    loc_sem, kv_s, kv_r, bk_s, bk_r, g_s, g_r, pj_s, pj_r, w_s, w_r, px_s, px_r, p1_s, p1_r, p2_s, p2_r, p3_s, p3_r, gq_s, gq_r, r1_s, r1_r, r2_s, r2_r, a1_s, a1_r, a2_s, a2_r, t1_s, t1_r, t2_s, t2_r,
):
    h = lax.axis_index("history")
    d = lax.axis_index("dp")
    z, y = h // 4, lax.rem(h, 4)
    x, c = d // 2, lax.rem(d, 2)

    def hist(k):
        return lax.rem(z + k // 4, 4) * 4 + lax.rem(y + lax.rem(k, 4), 4)

    def dpx(kx, kc):
        return lax.rem(x + kx, 4) * 2 + lax.rem(c + kc, 2)

    def dpo(k):
        return lax.rem(x + k // 2, 4) * 2 + lax.rem(c + lax.rem(k, 2), 2)

    barrier = pltpu.get_barrier_semaphore()

    def greet_hist(k, carry):
        pl.semaphore_signal(barrier, inc=1, device_id=(hist(k), d), device_id_type=MESH)
        return carry

    def greet_dp(k, carry):
        pl.semaphore_signal(barrier, inc=1, device_id=(h, dpo(k)), device_id_type=MESH)
        return carry

    lax.fori_loop(1, DP, greet_dp, 0)
    lax.fori_loop(1, HIST, greet_hist, 0)

    load_act = pltpu.make_async_copy(act_hbm, act, loc_sem.at[0])
    load_act.start()
    load_query = pltpu.make_async_copy(query_hbm, wts.at[0], loc_sem.at[1])
    load_query.start()
    load_frozen = pltpu.make_async_copy(frozen_hbm, wts.at[pl.ds(1, 3)], loc_sem.at[2])
    load_frozen.start()
    load_cot = pltpu.make_async_copy(cot_hbm, cot, loc_sem.at[3])
    load_cot.start()
    load_wout = pltpu.make_async_copy(wout_hbm, wout.at[d], loc_sem.at[4])
    load_wout.start()
    own_slab = kv.at[:, pl.ds(pl.multiple_of(h * SLAB, SLAB), SLAB), :]
    load_kv = pltpu.make_async_copy(cache_hbm.at[:, h], own_slab, loc_sem.at[5])
    load_kv.start()
    lane = lax.broadcasted_iota(jnp.int32, (HIST, TOK), 1)
    placed = jnp.where(lane // SLAB == y, jnp.concatenate([buckets[:, 0, :]] * 4, axis=1), 0)
    for u in range(HIST):
        bk_out[u] = jnp.broadcast_to(placed[u : u + 1, :], (8, TOK))

    load_act.wait()

    def norm_rows(r, carry):
        part = pl.ds(pl.multiple_of(r * 16, 16), 16)
        values = act[part, :].astype(F32)
        center = values - jnp.mean(values, axis=-1, keepdims=True)
        inverse = lax.rsqrt(jnp.mean(center * center, axis=-1, keepdims=True) + NORM_EPS)
        rows[d, part, :] = (center * inverse * ln_gain[...]).astype(BF16)
        return carry

    lax.fori_loop(0, TOK // 16, norm_rows, 0)
    pl.semaphore_wait(barrier, HIST - 1 + DP - 1)

    def remote(src, dst, send, recv, device):
        return pltpu.make_async_remote_copy(
            src_ref=src, dst_ref=dst, send_sem=send, recv_sem=recv, device_id=device, device_id_type=MESH
        )

    def ring_gather(block, half, own, send, recv, first=0):
        right, left, sibling = (h, dpx(1, 0)), (h, dpx(3, 0)), (h, dpx(0, 1))
        from_left, from_right, far = dpx(3, 0), dpx(1, 0), dpx(2, 0)
        specs = [
            (own, block(d), sibling),
            (own, block(d), right),
            (own, block(d), left),
            (half(from_left, 0), half(from_left, 0), right),
            (half(from_right, 1), half(from_right, 1), left),
            (block(from_left), block(from_left), sibling),
            (block(from_right), block(from_right), sibling),
            (half(far, 0), half(far, 0), sibling),
            (half(far, 1), half(far, 1), sibling),
        ]
        numbered = list(enumerate(specs))[first:]
        return {i: remote(s, t, send.at[i], recv.at[i], dev) for i, (s, t, dev) in numbered}

    ring = ring_gather(
        lambda i: rows.at[i],
        lambda i, k: rows.at[i, pl.ds(k * (TOK // 2), TOK // 2)],
        rows.at[d],
        g_s,
        g_r,
    )
    for i in (1, 2, 0):
        ring[i].start()

    def kv_copy(i):
        piece, turn = divmod(i - 1, HIST - 1)
        to = hist(LINK_ORDER[turn])
        part, low = piece % 2, piece // 2 * 16
        src = cache_hbm.at[part, to, pl.ds(low, 16)]
        dst = kv.at[part, pl.ds(pl.multiple_of(h * SLAB + low, 16), 16), :]
        return remote(src, dst, kv_s.at[i], kv_r.at[i], (to, d))

    def bk_copy(k):
        to = hist(k)
        return remote(bk_out.at[to], bks.at[h], bk_s.at[k], bk_r.at[k], (to, d))

    def plane_x(k):
        return remote(wout_hbm.at[0, z, y], wout.at[d, 0, z, y], px_s.at[k], px_r.at[k], (h, dpx(k, 0)))

    def plane_one(k, kx):
        slot, i = dpx(kx, 0), 3 * (k - 1) + kx - 1
        over_z, over_y = wout.at[slot, 0, z, y, 0], wout.at[slot, 0, z, y, 1]
        to_z, to_y = lax.rem(z + k, 4) * 4 + y, z * 4 + lax.rem(y + k, 4)
        return (
            remote(over_z, over_z, p1_s.at[i], p1_r.at[i], (to_z, d)),
            remote(over_y, over_y, p1_s.at[9 + i], p1_r.at[9 + i], (to_y, d)),
        )

    def plane_two(k, kx):
        slot, i = dpx(kx, 0), 3 * (k - 1) + kx - 1
        over_y, over_z = wout.at[slot, 0, :, y, 0], wout.at[slot, 0, z, :, 1]
        to_z, to_y = lax.rem(z + k, 4) * 4 + y, z * 4 + lax.rem(y + k, 4)
        return (
            remote(over_y, over_y, p2_s.at[i], p2_r.at[i], (to_y, d)),
            remote(over_z, over_z, p2_s.at[9 + i], p2_r.at[9 + i], (to_z, d)),
        )

    def plane_share(kx):
        block = wout.at[dpx(kx, 0), 0]
        return remote(block, block, p3_s.at[kx], p3_r.at[kx], (h, dpx(0, 1)))

    own_wout = remote(wout_hbm, wout.at[d], p3_s.at[0], p3_r.at[0], (h, dpx(0, 1)))
    wring = ring_gather(
        lambda i: wout.at[i, 1],
        lambda i, k: wout.at[i, 1, pl.ds(2 * k, 2)],
        wout_hbm.at[1],
        w_s,
        w_r,
        first=1,
    )
    plane_steps = [(k, kx) for k in (1, 3, 2) for kx in (1, 2, 3)]
    for k in range(1, 4):
        plane_x(k).start()

    def send_bk(k, carry):
        bk_copy(k).start()
        return carry

    lax.fori_loop(1, HIST, send_bk, 0)
    for i in range(1, KV_HALF):
        kv_copy(i).start()

    def project(chip):
        part = pl.ds(pl.multiple_of(chip * 2, 2), 2)
        chip_rows = rows[part].reshape(2 * TOK, WIDTH)
        for j in range(4):
            pre = dot_nn(chip_rows, wts[j])
            sigmoid = 0.5 * jnp.tanh(0.5 * pre) + 0.5
            acted = pre * sigmoid
            if j == 0:
                pre_slope[part] = (sigmoid + acted * (1.0 - sigmoid)).reshape(2, TOK, COLS)
            sent[part, :, pl.ds(j * COLS, COLS)] = acted.astype(BF16).reshape(2, TOK, COLS)

    def pj_copy(k):
        to = dpo(k)
        return remote(sent.at[to], proj.at[d], pj_s.at[k], pj_r.at[k], (h, to))

    load_query.wait()
    load_frozen.wait()
    ring[0].wait_recv()
    project(x)
    pj_copy(1).start()
    own_proj = pltpu.make_async_copy(sent.at[d], proj.at[d], loc_sem.at[7])
    own_proj.start()
    for k in range(1, 4):
        plane_x(k).wait_recv()
    for step in plane_steps:
        for copy in plane_one(*step):
            copy.start()
    for i in range(KV_HALF, KV_COPIES):
        kv_copy(i).start()
    ring[1].wait_recv()
    ring[3].start()
    ring[5].start()
    ring[2].wait_recv()
    ring[4].start()
    ring[6].start()
    ring[5].wait_recv()
    project(lax.rem(x + 3, 4))
    pj_copy(6).start()
    pj_copy(7).start()
    ring[6].wait_recv()
    project(lax.rem(x + 1, 4))
    pj_copy(2).start()
    pj_copy(3).start()
    for i in (1, 2):
        wring[i].start()
    own_wout.start()
    ring[3].wait_recv()
    ring[7].start()
    ring[4].wait_recv()
    ring[8].start()
    ring[7].wait_recv()
    ring[8].wait_recv()
    project(lax.rem(x + 2, 4))
    pj_copy(4).start()
    pj_copy(5).start()

    for step in plane_steps:
        for copy in plane_one(*step):
            copy.wait_recv()
    for step in plane_steps:
        for copy in plane_two(*step):
            copy.start()

    bks[h] = bk_out[h]

    def wait_bk(k, carry):
        bk_copy(k).wait_recv()
        return carry

    lax.fori_loop(1, HIST, wait_bk, 0)
    levels = lax.broadcasted_iota(jnp.int32, (BUCKETS, TOK), 0)
    for q in range(4):
        ids = (bks[4 * q] + bks[4 * q + 1] + bks[4 * q + 2] + bks[4 * q + 3])[0:1, :]
        onehot[:, pl.ds(q * TOK, TOK)] = jnp.where(levels == ids, 1.0, 0.0).astype(BF16)
    onehot[:, pl.ds(CACHED, TOK)] = jnp.where(levels == new_bucket[...], 1.0, 0.0).astype(BF16)
    hot = onehot[...]
    bias_sum = jnp.zeros((HEADS, KEYS), F32)
    for term in reversed(three_parts(rab[...])):
        bias_sum = bias_sum + dot_nn(term, hot)
    bias[...] = bias_sum

    count = length[0, 0]
    share = 1.0 / jnp.full((1, TOK), count + TOK, jnp.int32).astype(F32)
    cached_pos = lax.broadcasted_iota(jnp.int32, (1, CACHED), 1)
    share_cached = jnp.where(cached_pos < count, jnp.concatenate([share] * 4, axis=1), 0.0)
    row_pos = lax.broadcasted_iota(jnp.int32, (TOK, TOK), 0)
    col_pos = lax.broadcasted_iota(jnp.int32, (TOK, TOK), 1)
    share_new = jnp.where(col_pos <= row_pos, jnp.broadcast_to(share, (TOK, TOK)), 0.0)

    for i in (1, 2):
        wring[i].wait_recv()
        wring[i + 2].start()
        wring[i + 4].start()

    def wait_pj(k, carry):
        pj_copy(k).wait_recv()
        return carry

    own_proj.wait()
    lax.fori_loop(1, DP, wait_pj, 0)

    load_kv.wait()
    for i in range(1, KV_COPIES):
        kv_copy(i).wait_recv()

    def attend(m, carry):
        for k in range(2):
            head = m * 2 + k
            lanes = pl.ds(pl.multiple_of(head * HEAD, HEAD), HEAD)
            query = proj[m, :, pl.ds(k * HEAD, HEAD)]
            value_new = proj[m, :, pl.ds(2 * COLS + k * HEAD, HEAD)]
            key_new = proj[m, :, pl.ds(3 * COLS + k * HEAD, HEAD)]
            key_bias = bias[pl.ds(head, 1), :]
            total = jnp.zeros((TOK, HEAD), F32)
            parts = (
                (kv[0, :, lanes], kv[1, :, lanes], pl.ds(0, CACHED), key_bias[:, :CACHED], share_cached),
                (key_new, value_new, pl.ds(CACHED, TOK), key_bias[:, CACHED:], share_new),
            )
            for keys, values, where, bias_part, share_part in parts:
                score = dot_nt(query, keys) * SCALE + bias_part
                sigmoid = 0.5 * jnp.tanh(0.5 * score) + 0.5
                weight = score * sigmoid * share_part
                slope[head, :, where] = sigmoid * share_part + weight * (1.0 - sigmoid)
                total = total + dot_nn(weight.astype(BF16), values)
            att[:, lanes] = total
        return carry

    lax.fori_loop(0, DP, attend, 0)

    load_cot.wait()
    load_wout.wait()

    def gated_part(m, half, first=False):
        lanes = pl.ds(pl.multiple_of(m * COLS, COLS), COLS)
        for n in range(2):
            cols = pl.ds(half * 1024 + n * 512, 512)
            part = dot_nt(cot[:, lanes], wout[m, half, pl.ds(2 * n, 2)].reshape(512, COLS))
            grad_gated[:, cols] = part if first else grad_gated[:, cols] + part

    for step in plane_steps:
        for copy in plane_two(*step):
            copy.wait_recv()
    for k in range(1, 4):
        plane_share(k).start()
    gated_part(d, 0, True)
    gated_part(d, 1, True)
    own_wout.wait_recv()
    gated_part(dpx(0, 1), 0)
    gated_part(dpx(0, 1), 1)
    gated_part(dpx(3, 0), 1)
    gated_part(dpx(1, 0), 1)
    for k in (3, 1, 2):
        gated_part(dpx(k, 0), 0)
    for k in (3, 1, 2):
        plane_share(k).wait_recv()
        gated_part(dpx(k, 1), 0)
    wring[5].wait_recv()
    gated_part(dpx(3, 1), 1)
    wring[6].wait_recv()
    gated_part(dpx(1, 1), 1)
    for i in (3, 4):
        wring[i].wait_recv()
        wring[i + 4].start()
    gated_part(dpx(2, 0), 1)
    wring[7].wait_recv()
    wring[8].wait_recv()
    gated_part(dpx(2, 1), 1)

    def gate_rows(r, carry):
        part = pl.ds(pl.multiple_of(r * 16, 16), 16)
        values = att[part, :]
        center = values - jnp.mean(values, axis=-1, keepdims=True)
        inverse = lax.rsqrt(jnp.mean(center * center, axis=-1, keepdims=True) + NORM_EPS)
        nhat = center * inverse
        gate = jnp.concatenate([proj[m, part, pl.ds(COLS, COLS)] for m in range(DP)], axis=1).astype(F32)
        scaled = gate * norm_gain[...]
        gated[part, :] = (nhat * scaled).astype(BF16)
        grad_hat = grad_gated[part, :] * scaled
        along = jnp.mean(grad_hat * nhat, axis=-1, keepdims=True)
        grad = inverse * (grad_hat - jnp.mean(grad_hat, axis=-1, keepdims=True) - nhat * along)
        grad_att[part, :] = grad.astype(BF16)
        return carry

    lax.fori_loop(0, TOK // 16, gate_rows, 0)

    def gq_copy(half, k):
        to, i = dpo(k), half * DP + k
        return remote(gq_out.at[half, to], gq_in.at[half, d], gq_s.at[i], gq_r.at[i], (h, to))

    def attend_back(m, k):
        head = m * 2 + k
        lanes = pl.ds(pl.multiple_of(head * HEAD, HEAD), HEAD)
        value_new = proj[m, :, pl.ds(2 * COLS + k * HEAD, HEAD)]
        key_new = proj[m, :, pl.ds(3 * COLS + k * HEAD, HEAD)]
        grad = grad_att[:, lanes]
        total = jnp.zeros((TOK, HEAD), F32)
        parts = (
            (kv[0, :, lanes], kv[1, :, lanes], pl.ds(0, CACHED)),
            (key_new, value_new, pl.ds(CACHED, TOK)),
        )
        for keys, values, where in parts:
            grad_score = dot_nt(grad, values) * slope[head, :, where]
            tsum[head, :, where] = jnp.sum(grad_score.reshape(TOK // 8, 8, -1), axis=0)
            total = total + dot_nn(grad_score.astype(BF16), keys)
        gq_out[k, m] = (total * SCALE).astype(BF16)

    def back_steps(half, first, stop):
        def step(i, carry):
            k = 2 * i + 1
            attend_back(dpo(k), half)
            attend_back(dpo(k + 1), half)
            gq_copy(half, k).start()
            gq_copy(half, k + 1).start()
            return carry

        lax.fori_loop(first, stop, step, 0)

    def run(copy, stop, what, *half):
        def step(k, carry):
            getattr(copy(*half, k), what)()
            return carry

        lax.fori_loop(1, stop, step, 0)

    def own_back(half):
        attend_back(dpo(DP - 1), half)
        attend_back(d, half)
        gq_copy(half, DP - 1).start()
        gq_in[half, d] = gq_out[half, d]

    def weight_half(half):
        run(gq_copy, DP, "wait_recv", half)
        for i in range(DP):
            pre = pre_slope[i, :, pl.ds(half * HEAD, HEAD)]
            grad_pre_t[half, :, pl.ds(i * TOK, TOK)] = (gq_in[half, i].astype(F32) * pre).astype(BF16).T
        for i in range(4):
            piece = dot_nn(grad_pre_t[half], rows[:, :, pl.ds(i * 512, 512)].reshape(DP * TOK, 512)).astype(BF16)
            rs_out[half, i] = piece.T.reshape(4, 2, HEAD // 2, HEAD)
        for k in (1, 3, 2):
            for side in range(2):
                sum_one(half, side, k).start()

    def along(side, k):
        return (lax.rem(z + k, 4), y) if side == 0 else (z, lax.rem(y + k, 4))

    def place(zy):
        return (zy[0] * 4 + zy[1], d)

    def line(ref, half, side, zy):
        return ref.at[half, zy[0], :, side] if side == 0 else ref.at[half, :, zy[1], side]

    def own(side):
        return z if side == 0 else y

    def sems(pair, half, side, k):
        i = (half * 2 + side) * 4 + k
        return pair[0].at[i], pair[1].at[i]

    def sum_one(half, side, k):
        to = along(side, k)
        return remote(line(rs_out, half, side, to), r1_in.at[half, side, own(side)], *sems((r1_s, r1_r), half, side, k), place(to))

    def sum_two(half, side, k):
        to = along(1 - side, k)
        src = r2_out.at[half, side, to[1 - side]]
        return remote(src, r2_in.at[half, side, own(1 - side)], *sems((r2_s, r2_r), half, side, k), place(to))

    def gather_one(half, side, k):
        block = ag_buf.at[half, z, y, side]
        return remote(block, block, *sems((a1_s, a1_r), half, side, k), place(along(1 - side, k)))

    def gsum_line(half, side):
        lanes = pl.ds(half * HEAD, HEAD)
        return gsum_hbm.at[z, :, side, :, lanes] if side == 0 else gsum_hbm.at[:, y, side, :, lanes]

    def gather_two(half, side, k):
        src = line(ag_buf, half, side, (z, y))
        return remote(src, gsum_line(half, side), *sems((a2_s, a2_r), half, side, k), place(along(side, k)))

    def own_gsum(half, side):
        return pltpu.make_async_copy(line(ag_buf, half, side, (z, y)), gsum_line(half, side), loc_sem.at[8 + half * 2 + side])

    def after_one(half):
        for side in range(2):
            r1_in[half, side, own(side)] = rs_out[half, z, :, 0] if side == 0 else rs_out[half, :, y, 1]
            for k in (1, 3, 2):
                sum_one(half, side, k).wait_recv()
            total = r1_in[half, side, 0].astype(F32)
            for i in range(1, 4):
                total = total + r1_in[half, side, i].astype(F32)
            r2_out[half, side] = total
            for k in (1, 3, 2):
                sum_two(half, side, k).start()

    def after_two(half):
        for side in range(2):
            r2_in[half, side, own(1 - side)] = r2_out[half, side, own(1 - side)]
            for k in (1, 3, 2):
                sum_two(half, side, k).wait_recv()
            total = r2_in[half, side, 0]
            for i in range(1, 4):
                total = total + r2_in[half, side, i]
            ag_buf[half, z, y, side] = total.astype(BF16)
            for k in (1, 3, 2):
                gather_one(half, side, k).start()

    def after_three(half):
        for side in range(2):
            for k in (1, 3, 2):
                gather_one(half, side, k).wait_recv()
            for k in (1, 3, 2):
                gather_two(half, side, k).start()
            own_gsum(half, side).start()

    def out_cols(m, carry):
        lanes = pl.ds(pl.multiple_of(m * COLS, COLS), COLS)
        product = dot_nn(gated[...], wout[m].reshape(WIDTH, COLS))
        out_ref[:, lanes] = (product + act[:, lanes].astype(F32)).astype(BF16)
        return carry

    def t1_copy(k):
        return remote(tab_one.at[d], tab_one.at[d], t1_s.at[k], t1_r.at[k], (h, dpo(k)))

    def t2_copy(k):
        return remote(tab_two.at[h], tab_two.at[h], t2_s.at[k], t2_r.at[k], (hist(k), d))

    back_steps(0, 0, 3)
    own_back(0)
    back_steps(1, 0, 2)
    weight_half(0)
    back_steps(1, 2, 3)
    own_back(1)

    table = jnp.zeros((HEADS, BUCKETS), F32)
    for term in reversed(three_parts(jnp.sum(tsum[...], axis=1))):
        table = table + dot_nt(term, hot)
    tab_one[d] = table
    run(t1_copy, DP, "start")

    lax.fori_loop(0, 2, out_cols, 0)
    after_one(0)
    weight_half(1)
    lax.fori_loop(2, 4, out_cols, 0)
    after_two(0)

    run(t1_copy, DP, "wait_recv")
    table = tab_one[0]
    for i in range(1, DP):
        table = table + tab_one[i]
    tab_two[h] = table
    run(t2_copy, HIST, "start")

    after_one(1)
    lax.fori_loop(4, 6, out_cols, 0)
    after_three(0)
    after_two(1)
    lax.fori_loop(6, DP, out_cols, 0)
    after_three(1)

    run(t2_copy, HIST, "wait_recv")
    table = tab_two[0]
    for i in range(1, HIST):
        table = table + tab_two[i]
    gtab_ref[...] = table

    for copy in [*ring.values(), *wring.values(), own_wout]:
        copy.wait_send()
    for k in range(1, 4):
        plane_x(k).wait_send()
        plane_share(k).wait_send()
    for step in plane_steps:
        for copy in plane_one(*step) + plane_two(*step):
            copy.wait_send()
    for i in range(1, KV_COPIES):
        kv_copy(i).wait_send()
    for copy, stop in ((bk_copy, HIST), (pj_copy, DP), (t1_copy, DP), (t2_copy, HIST)):
        run(copy, stop, "wait_send")
    for half in range(2):
        run(gq_copy, DP, "wait_send", half)
        for side in range(2):
            for k in (1, 3, 2):
                for copy in (sum_one, sum_two, gather_one):
                    copy(half, side, k).wait_send()
                gather_two(half, side, k).wait()
            own_gsum(half, side).wait()


def layer(actions, cotangent, cache, length, buckets, new_bucket, ln_gain, norm_gain, w_frozen, w_query, w_out, rab):
    any_space = pl.BlockSpec(memory_space=pl.ANY)
    vmem = pl.BlockSpec(memory_space=pltpu.VMEM)
    smem = pl.BlockSpec(memory_space=pltpu.SMEM)
    dma = pltpu.SemaphoreType.DMA
    sem_sizes = (12, KV_COPIES, KV_COPIES, HIST, HIST, 9, 9, DP, DP, 9, 9, 4, 4, 18, 18, 18, 18, 4, 4, 2 * DP, 2 * DP, *[16] * 8, DP, DP, HIST, HIST)
    return pl.pallas_call(
        kernel,
        out_shape=(
            jax.ShapeDtypeStruct((TOK, WIDTH), BF16),
            jax.ShapeDtypeStruct((4, 4, 2, HEAD // 2, COLS), BF16),
            jax.ShapeDtypeStruct((HEADS, BUCKETS), F32),
        ),
        in_specs=[any_space, any_space, any_space, smem, vmem, vmem, vmem, vmem, any_space, any_space, any_space, vmem],
        out_specs=(vmem, any_space, vmem),
        scratch_shapes=[
            pltpu.VMEM((TOK, WIDTH), BF16),
            pltpu.VMEM((TOK, WIDTH), BF16),
            pltpu.VMEM((4, WIDTH, COLS), BF16),
            pltpu.VMEM((DP, TOK, WIDTH), BF16),
            pltpu.VMEM((DP, TOK, COLS), F32),
            pltpu.VMEM((DP, TOK, 4 * COLS), BF16),
            pltpu.VMEM((DP, TOK, 4 * COLS), BF16),
            pltpu.VMEM((2, CACHED, WIDTH), BF16),
            pltpu.VMEM((HIST, 8, TOK), jnp.int32),
        pltpu.VMEM((HIST, 8, TOK), jnp.int32),
            pltpu.VMEM((BUCKETS, KEYS), BF16),
            pltpu.VMEM((HEADS, KEYS), F32),
            pltpu.VMEM((TOK, WIDTH), F32),
            pltpu.VMEM((HEADS, TOK, KEYS), F32),
            pltpu.VMEM((DP, 2, 4, 4, 2, 32, COLS), BF16),
            pltpu.VMEM((TOK, WIDTH), F32),
            pltpu.VMEM((TOK, WIDTH), BF16),
            pltpu.VMEM((TOK, WIDTH), BF16),
            pltpu.VMEM((HEADS, 8, KEYS), F32),
            pltpu.VMEM((2, DP, TOK, HEAD), BF16),
            pltpu.VMEM((2, DP, TOK, HEAD), BF16),
            pltpu.VMEM((2, HEAD, DP * TOK), BF16),
            pltpu.VMEM((2, 4, 4, 2, HEAD // 2, HEAD), BF16),
            pltpu.VMEM((2, 2, 4, 4, HEAD // 2, HEAD), BF16),
            pltpu.VMEM((2, 2, 4, HEAD // 2, HEAD), F32),
            pltpu.VMEM((2, 2, 4, HEAD // 2, HEAD), F32),
            pltpu.VMEM((2, 4, 4, 2, HEAD // 2, HEAD), BF16),
            pltpu.VMEM((DP, HEADS, BUCKETS), F32),
            pltpu.VMEM((HIST, HEADS, BUCKETS), F32),
        ]
        + [dma((n,)) for n in sem_sizes],
        compiler_params=pltpu.CompilerParams(collective_id=0, has_side_effects=True, vmem_limit_bytes=60 * 1024 * 1024),
        name="layer",
    )(actions, cotangent, cache, length, buckets, new_bucket, ln_gain, norm_gain, w_frozen, w_query, w_out, rab)


def shards(
    actions, cotangent, cache_kv, cache_len, cache_bucket, new_bucket, ln_gain, norm_gain,
    w_frozen, w_query, query_m, query_v, w_out, rab_table, rab_m, rab_v,
):
    result, grad_sum, grad_table = layer(
        actions.reshape(TOK, WIDTH),
        cotangent.reshape(TOK, WIDTH),
        cache_kv.reshape(2, HIST, SLAB, WIDTH),
        cache_len.reshape(1, 1),
        cache_bucket,
        new_bucket.reshape(1, TOK),
        ln_gain.reshape(1, WIDTH),
        norm_gain.reshape(1, WIDTH),
        w_frozen,
        w_query,
        w_out.reshape(2, 4, 4, 2, 32, COLS),
        rab_table,
    )
    query_new, query_m_new, query_v_new = adam_update(w_query, query_m, query_v, grad_sum.reshape(WIDTH, COLS).astype(F32))
    rab_new, rab_m_new, rab_v_new = adam_update(rab_table, rab_m, rab_v, grad_table)
    return (result.reshape(actions.shape), query_new, query_m_new, query_v_new, rab_new, rab_m_new, rab_v_new)


def solution(mesh):
    placed = (
        P("history", "dp", None, None),
        P("history", "dp", None, None),
        P(None, None, "dp", "history", None),
        P("history", "dp"),
        P(None, "dp", "history"),
        P("history", "dp", None),
        P(),
        P(),
        P(None, None, "dp"),
        P(None, "dp"),
        P(None, "dp"),
        P(None, "dp"),
        P(None, "dp"),
        P(),
        P(),
        P(),
    )
    return jax.shard_map(
        shards,
        mesh=mesh,
        in_specs=placed,
        out_specs=(
            P("history", "dp", None, None),
            P(None, "dp"),
            P(None, "dp"),
            P(None, "dp"),
            P(),
            P(),
            P(),
        ),
        check_vma=False,
    )
```

```python
import functools

import jax
import jax.numpy as jnp
from jax import lax
from jax.experimental import pallas as pl
from jax.experimental.pallas import tpu as pltpu
from jax.sharding import PartitionSpec as P

BETA_ONE = 0.9
BETA_TWO = 0.95
LEARN_RATE = 0.001
ADAM_EPS = 1e-08
NORM_EPS = 1e-05

MESH = pl.DeviceIdType.MESH
F32 = jnp.float32
BF16 = jnp.bfloat16

TOK = 128
WIDTH = 2048
COLS = 256
HEAD = 128
HEADS = 16
BUCKETS = 128
HIST = 16
DP = 8
SLAB = 32
CACHED = HIST * SLAB
KEYS = CACHED + TOK
SCALE = HEAD ** (-0.5)
KV_COPIES = 4 * (HIST - 1) + 1
KV_HALF = 2 * (HIST - 1) + 1
LINK_ORDER = (1, 4, 3, 12, 2, 8, 5, 15, 7, 13, 6, 9, 14, 11, 10)


def adam_update(weight, moment_one, moment_two, gradient):
    first_new = BETA_ONE * moment_one + (1.0 - BETA_ONE) * gradient
    second_new = BETA_TWO * moment_two + (1.0 - BETA_TWO) * gradient * gradient
    stepped = weight.astype(F32) - LEARN_RATE * first_new / (jnp.sqrt(second_new) + ADAM_EPS)
    return (stepped.astype(weight.dtype), first_new, second_new)


def dot_nn(a, b):
    return jnp.dot(a, b, preferred_element_type=F32)


def dot_nt(a, b):
    return lax.dot_general(a, b, (((1,), (1,)), ((), ())), preferred_element_type=F32)


def three_parts(values):
    first = values.astype(BF16)
    rest = values - first.astype(F32)
    second = rest.astype(BF16)
    third = (rest - second.astype(F32)).astype(BF16)
    return first, second, third


def silu_slope(values):
    sigmoid = 0.5 * jnp.tanh(0.5 * values) + 0.5
    return sigmoid * (1.0 + values * (1.0 - sigmoid))


def kernel(
    act_hbm, cot_hbm, cache_hbm, length, buckets, new_bucket, ln_gain, norm_gain, frozen_hbm, query_hbm, wout_hbm, rab,
    out_ref, gsum_hbm, gtab_ref,
    act, cot, wts, rows, pre_slope, sent, proj, kv, bk_out, bks, onehot, bias, att, slope, wout, grad_gated, gate_scaled, inverse_std, gated, grad_att,
    tsum, gq_out, gq_in, grad_pre_t, rs_out, r1_in, r2_out, r2_in, ag_buf, tab_one, tab_two, tab_three,
    loc_sem, kv_s, kv_r, bk_s, bk_r, g_s, g_r, pj_s, pj_r, w_s, w_r, px_s, px_r, p1_s, p1_r, p2_s, p2_r, p3_s, p3_r, gq_s, gq_r, r1_s, r1_r, r2_s, r2_r, a1_s, a1_r, a2_s, a2_r, t1_s, t1_r, t2_s, t2_r, t3_s, t3_r,
):
    h = lax.axis_index("history")
    d = lax.axis_index("dp")
    z, y = h // 4, lax.rem(h, 4)
    x, c = d // 2, lax.rem(d, 2)

    def hist(k):
        return lax.rem(z + k // 4, 4) * 4 + lax.rem(y + lax.rem(k, 4), 4)

    def dpx(kx, kc):
        return lax.rem(x + kx, 4) * 2 + lax.rem(c + kc, 2)

    def dpo(k):
        return lax.rem(x + k // 2, 4) * 2 + lax.rem(c + lax.rem(k, 2), 2)

    barrier = pltpu.get_barrier_semaphore()

    def greet_hist(k, carry):
        pl.semaphore_signal(barrier, inc=1, device_id=(hist(k), d), device_id_type=MESH)
        return carry

    def greet_dp(k, carry):
        pl.semaphore_signal(barrier, inc=1, device_id=(h, dpo(k)), device_id_type=MESH)
        return carry

    lax.fori_loop(1, DP, greet_dp, 0)
    lax.fori_loop(1, HIST, greet_hist, 0)

    load_act = pltpu.make_async_copy(act_hbm, act, loc_sem.at[0])
    load_act.start()
    load_query = pltpu.make_async_copy(query_hbm, wts.at[0], loc_sem.at[1])
    load_query.start()
    load_frozen = pltpu.make_async_copy(frozen_hbm, wts.at[pl.ds(1, 3)], loc_sem.at[2])
    load_frozen.start()
    load_cot = pltpu.make_async_copy(cot_hbm, cot, loc_sem.at[3])
    load_cot.start()
    load_wout = pltpu.make_async_copy(wout_hbm, wout.at[d], loc_sem.at[4])
    load_wout.start()
    own_slab = kv.at[:, pl.ds(pl.multiple_of(h * SLAB, SLAB), SLAB), :]
    load_kv = pltpu.make_async_copy(cache_hbm.at[:, h], own_slab, loc_sem.at[5])
    load_kv.start()
    lane = lax.broadcasted_iota(jnp.int32, (HIST, TOK), 1)
    placed = jnp.where(lane // SLAB == y, jnp.concatenate([buckets[:, 0, :]] * 4, axis=1), 0)
    for u in range(HIST):
        bk_out[u] = jnp.broadcast_to(placed[u : u + 1, :], (8, TOK))

    def run(copy, stop, what, *half):
        def step(k, carry):
            getattr(copy(*half, k), what)()
            return carry

        lax.fori_loop(1, stop, step, 0)

    load_act.wait()

    def norm_rows(r, carry):
        part = pl.ds(pl.multiple_of(r * 16, 16), 16)
        values = act[part, :].astype(F32)
        center = values - jnp.mean(values, axis=-1, keepdims=True)
        inverse = lax.rsqrt(jnp.mean(center * center, axis=-1, keepdims=True) + NORM_EPS)
        rows[d, part, :] = (center * inverse * ln_gain[...]).astype(BF16)
        return carry

    lax.fori_loop(0, TOK // 16, norm_rows, 0)
    pl.semaphore_wait(barrier, HIST - 1 + DP - 1)

    def remote(src, dst, send, recv, device):
        return pltpu.make_async_remote_copy(
            src_ref=src, dst_ref=dst, send_sem=send, recv_sem=recv, device_id=device, device_id_type=MESH
        )

    def ring_gather(block, half, own, send, recv, first=0):
        right, left, sibling = (h, dpx(1, 0)), (h, dpx(3, 0)), (h, dpx(0, 1))
        from_left, from_right, far = dpx(3, 0), dpx(1, 0), dpx(2, 0)
        specs = [
            (own, block(d), sibling),
            (own, block(d), right),
            (own, block(d), left),
            (half(from_left, 0), half(from_left, 0), right),
            (half(from_right, 1), half(from_right, 1), left),
            (block(from_left), block(from_left), sibling),
            (block(from_right), block(from_right), sibling),
            (half(far, 0), half(far, 0), sibling),
            (half(far, 1), half(far, 1), sibling),
        ]
        numbered = list(enumerate(specs))[first:]
        return {i: remote(s, t, send.at[i], recv.at[i], dev) for i, (s, t, dev) in numbered}

    ring = ring_gather(
        lambda i: rows.at[i],
        lambda i, k: rows.at[i, pl.ds(k * (TOK // 2), TOK // 2)],
        rows.at[d],
        g_s,
        g_r,
    )
    for i in (1, 2, 0):
        ring[i].start()

    def kv_copy(i):
        piece, turn = divmod(i - 1, HIST - 1)
        to = hist(LINK_ORDER[turn])
        part, low = piece % 2, piece // 2 * 16
        src = cache_hbm.at[part, to, pl.ds(low, 16)]
        dst = kv.at[part, pl.ds(pl.multiple_of(h * SLAB + low, 16), 16), :]
        return remote(src, dst, kv_s.at[i], kv_r.at[i], (to, d))

    def bk_copy(k):
        to = hist(k)
        return remote(bk_out.at[to], bks.at[h], bk_s.at[k], bk_r.at[k], (to, d))

    def plane_x(k):
        return remote(wout_hbm.at[0, z, y], wout.at[d, 0, z, y], px_s.at[k], px_r.at[k], (h, dpx(k, 0)))

    def plane_one(k, kx):
        slot, i = dpx(kx, 0), 3 * (k - 1) + kx - 1
        over_z, over_y = wout.at[slot, 0, z, y, 0], wout.at[slot, 0, z, y, 1]
        to_z, to_y = lax.rem(z + k, 4) * 4 + y, z * 4 + lax.rem(y + k, 4)
        return (
            remote(over_z, over_z, p1_s.at[i], p1_r.at[i], (to_z, d)),
            remote(over_y, over_y, p1_s.at[9 + i], p1_r.at[9 + i], (to_y, d)),
        )

    def plane_two(k, kx):
        slot, i = dpx(kx, 0), 3 * (k - 1) + kx - 1
        over_y, over_z = wout.at[slot, 0, :, y, 0], wout.at[slot, 0, z, :, 1]
        to_z, to_y = lax.rem(z + k, 4) * 4 + y, z * 4 + lax.rem(y + k, 4)
        return (
            remote(over_y, over_y, p2_s.at[i], p2_r.at[i], (to_y, d)),
            remote(over_z, over_z, p2_s.at[9 + i], p2_r.at[9 + i], (to_z, d)),
        )

    def plane_share(kx):
        block = wout.at[dpx(kx, 0), 0]
        return remote(block, block, p3_s.at[kx], p3_r.at[kx], (h, dpx(0, 1)))

    own_wout = remote(wout_hbm, wout.at[d], p3_s.at[0], p3_r.at[0], (h, dpx(0, 1)))
    wring = ring_gather(
        lambda i: wout.at[i, 1],
        lambda i, k: wout.at[i, 1, pl.ds(2 * k, 2)],
        wout_hbm.at[1],
        w_s,
        w_r,
        first=1,
    )
    plane_steps = [(k, kx) for k in (1, 3, 2) for kx in (1, 2, 3)]
    for k in range(1, 4):
        plane_x(k).start()

    def send_bk(k, carry):
        bk_copy(k).start()
        return carry

    lax.fori_loop(1, HIST, send_bk, 0)
    for i in range(1, KV_HALF):
        kv_copy(i).start()

    def project(chip):
        part = pl.ds(pl.multiple_of(chip * 2, 2), 2)
        chip_rows = rows[part].reshape(2 * TOK, WIDTH)
        for j in range(4):
            pre = dot_nn(chip_rows, wts[j])
            sigmoid = 0.5 * jnp.tanh(0.5 * pre) + 0.5
            acted = pre * sigmoid
            if j == 0:
                pre_slope[part] = (sigmoid + acted * (1.0 - sigmoid)).reshape(2, TOK, COLS)
            sent[part, :, pl.ds(j * COLS, COLS)] = acted.astype(BF16).reshape(2, TOK, COLS)

    def pj_copy(k):
        to = dpo(k)
        return remote(sent.at[to], proj.at[d], pj_s.at[k], pj_r.at[k], (h, to))

    load_query.wait()
    load_frozen.wait()
    ring[0].wait_recv()
    project(x)
    pj_copy(1).start()
    own_proj = pltpu.make_async_copy(sent.at[d], proj.at[d], loc_sem.at[7])
    own_proj.start()
    for k in range(1, 4):
        plane_x(k).wait_recv()
    for step in plane_steps:
        for copy in plane_one(*step):
            copy.start()
    for i in range(KV_HALF, KV_COPIES):
        kv_copy(i).start()
    ring[1].wait_recv()
    ring[3].start()
    ring[5].start()
    ring[2].wait_recv()
    ring[4].start()
    ring[6].start()
    ring[5].wait_recv()
    project(lax.rem(x + 3, 4))
    pj_copy(6).start()
    pj_copy(7).start()
    ring[6].wait_recv()
    project(lax.rem(x + 1, 4))
    pj_copy(2).start()
    pj_copy(3).start()
    for i in (1, 2):
        wring[i].start()
    own_wout.start()
    ring[3].wait_recv()
    ring[7].start()
    ring[4].wait_recv()
    ring[8].start()
    ring[7].wait_recv()
    ring[8].wait_recv()
    project(lax.rem(x + 2, 4))
    pj_copy(4).start()
    pj_copy(5).start()

    for step in plane_steps:
        for copy in plane_one(*step):
            copy.wait_recv()
    for step in plane_steps:
        for copy in plane_two(*step):
            copy.start()

    bks[h] = bk_out[h]

    def wait_bk(k, carry):
        bk_copy(k).wait_recv()
        return carry

    lax.fori_loop(1, HIST, wait_bk, 0)
    levels = lax.broadcasted_iota(jnp.int32, (BUCKETS, TOK), 0)
    for q in range(4):
        ids = (bks[4 * q] + bks[4 * q + 1] + bks[4 * q + 2] + bks[4 * q + 3])[0:1, :]
        onehot[:, pl.ds(q * TOK, TOK)] = jnp.where(levels == ids, 1.0, 0.0).astype(BF16)
    onehot[:, pl.ds(CACHED, TOK)] = jnp.where(levels == new_bucket[...], 1.0, 0.0).astype(BF16)
    hot = onehot[...]
    bias_sum = jnp.zeros((HEADS, KEYS), F32)
    for term in reversed(three_parts(rab[...])):
        bias_sum = bias_sum + dot_nn(term, hot)
    bias[...] = bias_sum

    count = length[0, 0]
    share = 1.0 / jnp.full((1, TOK), count + TOK, jnp.int32).astype(F32)
    cached_pos = lax.broadcasted_iota(jnp.int32, (1, CACHED), 1)
    share_cached = jnp.where(cached_pos < count, jnp.concatenate([share] * 4, axis=1), 0.0)
    row_pos = lax.broadcasted_iota(jnp.int32, (TOK, TOK), 0)
    col_pos = lax.broadcasted_iota(jnp.int32, (TOK, TOK), 1)
    share_new = jnp.where(col_pos <= row_pos, jnp.broadcast_to(share, (TOK, TOK)), 0.0)

    for i in (1, 2):
        wring[i].wait_recv()
        wring[i + 2].start()
        wring[i + 4].start()

    def wait_pj(k, carry):
        pj_copy(k).wait_recv()
        return carry

    own_proj.wait()
    lax.fori_loop(1, DP, wait_pj, 0)

    load_kv.wait()
    for i in range(1, KV_COPIES):
        kv_copy(i).wait_recv()

    def attend(m, carry):
        for k in range(2):
            head = m * 2 + k
            lanes = pl.ds(pl.multiple_of(head * HEAD, HEAD), HEAD)
            query = proj[m, :, pl.ds(k * HEAD, HEAD)]
            value_new = proj[m, :, pl.ds(2 * COLS + k * HEAD, HEAD)]
            key_new = proj[m, :, pl.ds(3 * COLS + k * HEAD, HEAD)]
            key_bias = bias[pl.ds(head, 1), :]
            total = jnp.zeros((TOK, HEAD), F32)
            parts = (
                (kv[0, :, lanes], kv[1, :, lanes], pl.ds(0, CACHED), key_bias[:, :CACHED], share_cached),
                (key_new, value_new, pl.ds(CACHED, TOK), key_bias[:, CACHED:], share_new),
            )
            for keys, values, where, bias_part, share_part in parts:
                score = dot_nt(query, keys) * SCALE + bias_part
                sigmoid = 0.5 * jnp.tanh(0.5 * score) + 0.5
                weight = score * sigmoid * share_part
                slope[head, :, where] = sigmoid * share_part + weight * (1.0 - sigmoid)
                total = total + dot_nn(weight.astype(BF16), values)
            att[:, lanes] = total
        return carry

    lax.fori_loop(0, DP, attend, 0)

    def stat_rows(r, carry):
        part = pl.ds(pl.multiple_of(r * 16, 16), 16)
        values = att[part, :]
        center = values - jnp.mean(values, axis=-1, keepdims=True)
        inverse = lax.rsqrt(jnp.mean(center * center, axis=-1, keepdims=True) + NORM_EPS)
        nhat = center * inverse
        gate = jnp.concatenate([proj[m, part, pl.ds(COLS, COLS)] for m in range(DP)], axis=1).astype(F32)
        scaled = gate * norm_gain[...]
        att[part, :] = nhat
        gate_scaled[part, :] = scaled
        gated[part, :] = (nhat * scaled).astype(BF16)
        inverse_std[part, :] = jnp.broadcast_to(inverse, (16, TOK))
        return carry

    lax.fori_loop(0, TOK // 16, stat_rows, 0)

    load_cot.wait()
    load_wout.wait()

    def gated_part(m, half, first=False):
        lanes = pl.ds(pl.multiple_of(m * COLS, COLS), COLS)
        for n in range(2):
            cols = pl.ds(half * 1024 + n * 512, 512)
            part = dot_nt(cot[:, lanes], wout[m, half, pl.ds(2 * n, 2)].reshape(512, COLS))
            grad_gated[:, cols] = part if first else grad_gated[:, cols] + part

    run(bk_copy, HIST, "wait_send")
    run(pj_copy, DP, "wait_send")
    for i in range(1, KV_COPIES):
        kv_copy(i).wait_send()
    for copy in ring.values():
        copy.wait_send()
    for k in range(1, 4):
        plane_x(k).wait_send()
    for step in plane_steps:
        for copy in plane_one(*step):
            copy.wait_send()

    for step in plane_steps:
        for copy in plane_two(*step):
            copy.wait_recv()
    for k in range(1, 4):
        plane_share(k).start()
    gated_part(d, 0, True)
    gated_part(d, 1, True)
    own_wout.wait_recv()
    gated_part(dpx(0, 1), 0)
    gated_part(dpx(0, 1), 1)
    gated_part(dpx(3, 0), 1)
    gated_part(dpx(1, 0), 1)
    for i in (3, 4):
        wring[i].wait_recv()
        wring[i + 4].start()
    for k in (3, 1, 2):
        gated_part(dpx(k, 0), 0)
    for k in (3, 1, 2):
        plane_share(k).wait_recv()
        gated_part(dpx(k, 1), 0)
    wring[5].wait_recv()
    gated_part(dpx(3, 1), 1)
    wring[6].wait_recv()
    gated_part(dpx(1, 1), 1)
    gated_part(dpx(2, 0), 1)
    wring[7].wait_recv()
    wring[8].wait_recv()
    gated_part(dpx(2, 1), 1)

    def gate_rows(r, carry):
        part = pl.ds(pl.multiple_of(r * 16, 16), 16)
        nhat = att[part, :]
        grad_hat = grad_gated[part, :] * gate_scaled[part, :]
        along = jnp.mean(grad_hat * nhat, axis=-1, keepdims=True)
        grad = inverse_std[part, 0:1] * (grad_hat - jnp.mean(grad_hat, axis=-1, keepdims=True) - nhat * along)
        grad_att[part, :] = grad.astype(BF16)
        return carry

    lax.fori_loop(0, TOK // 16, gate_rows, 0)

    def gq_copy(half, k):
        to, i = dpo(k), half * DP + k
        return remote(gq_out.at[half, to], gq_in.at[half, d], gq_s.at[i], gq_r.at[i], (h, to))

    def attend_back(m, k):
        head = m * 2 + k
        lanes = pl.ds(pl.multiple_of(head * HEAD, HEAD), HEAD)
        value_new = proj[m, :, pl.ds(2 * COLS + k * HEAD, HEAD)]
        key_new = proj[m, :, pl.ds(3 * COLS + k * HEAD, HEAD)]
        grad = grad_att[:, lanes]
        total = jnp.zeros((TOK, HEAD), F32)
        parts = (
            (kv[0, :, lanes], kv[1, :, lanes], pl.ds(0, CACHED)),
            (key_new, value_new, pl.ds(CACHED, TOK)),
        )
        for keys, values, where in parts:
            grad_score = dot_nt(grad, values) * slope[head, :, where]
            tsum[head, :, where] = jnp.sum(grad_score.reshape(TOK // 8, 8, -1), axis=0)
            total = total + dot_nn(grad_score.astype(BF16), keys)
        gq_out[k, m] = (total * SCALE).astype(BF16)

    def back_steps(half, first, stop):
        def step(i, carry):
            k = 2 * i + 1
            attend_back(dpo(k), half)
            attend_back(dpo(k + 1), half)
            gq_copy(half, k).start()
            gq_copy(half, k + 1).start()
            return carry

        lax.fori_loop(first, stop, step, 0)

    def own_back(half):
        attend_back(dpo(DP - 1), half)
        attend_back(d, half)
        gq_copy(half, DP - 1).start()
        gq_in[half, d] = gq_out[half, d]

    def weight_half(half):
        run(gq_copy, DP, "wait_recv", half)
        for i in range(DP):
            pre = pre_slope[i, :, pl.ds(half * HEAD, HEAD)]
            grad_pre_t[half, :, pl.ds(i * TOK, TOK)] = (gq_in[half, i].astype(F32) * pre).astype(BF16).T
        for i in range(4):
            piece = dot_nn(grad_pre_t[half], rows[:, :, pl.ds(i * 512, 512)].reshape(DP * TOK, 512)).astype(BF16)
            rs_out[half, i] = piece.T.reshape(4, 2, HEAD // 2, HEAD)
        for k in (1, 3, 2):
            for side in range(2):
                sum_one(half, side, k).start()

    def along(side, k):
        return (lax.rem(z + k, 4), y) if side == 0 else (z, lax.rem(y + k, 4))

    def place(zy):
        return (zy[0] * 4 + zy[1], d)

    def line(ref, half, side, zy):
        return ref.at[half, zy[0], :, side] if side == 0 else ref.at[half, :, zy[1], side]

    def own(side):
        return z if side == 0 else y

    def sems(pair, half, side, k):
        i = (half * 2 + side) * 4 + k
        return pair[0].at[i], pair[1].at[i]

    def sum_one(half, side, k):
        to = along(side, k)
        return remote(line(rs_out, half, side, to), r1_in.at[half, side, own(side)], *sems((r1_s, r1_r), half, side, k), place(to))

    def sum_two(half, side, k):
        to = along(1 - side, k)
        src = r2_out.at[half, side, to[1 - side]]
        return remote(src, r2_in.at[half, side, own(1 - side)], *sems((r2_s, r2_r), half, side, k), place(to))

    def gather_one(half, side, k):
        block = ag_buf.at[half, z, y, side]
        return remote(block, block, *sems((a1_s, a1_r), half, side, k), place(along(1 - side, k)))

    def gsum_line(half, side):
        lanes = pl.ds(half * HEAD, HEAD)
        return gsum_hbm.at[z, :, side, :, lanes] if side == 0 else gsum_hbm.at[:, y, side, :, lanes]

    def gather_two(half, side, k):
        src = line(ag_buf, half, side, (z, y))
        return remote(src, gsum_line(half, side), *sems((a2_s, a2_r), half, side, k), place(along(side, k)))

    def own_gsum(half, side):
        return pltpu.make_async_copy(line(ag_buf, half, side, (z, y)), gsum_line(half, side), loc_sem.at[8 + half * 2 + side])

    def after_one(half):
        for side in range(2):
            r1_in[half, side, own(side)] = rs_out[half, z, :, 0] if side == 0 else rs_out[half, :, y, 1]
            for k in (1, 3, 2):
                sum_one(half, side, k).wait_recv()
            total = r1_in[half, side, 0].astype(F32)
            for i in range(1, 4):
                total = total + r1_in[half, side, i].astype(F32)
            r2_out[half, side] = total
            for k in (1, 3, 2):
                sum_two(half, side, k).start()

    def after_two(half):
        for side in range(2):
            r2_in[half, side, own(1 - side)] = r2_out[half, side, own(1 - side)]
            for k in (1, 3, 2):
                sum_two(half, side, k).wait_recv()
            total = r2_in[half, side, 0]
            for i in range(1, 4):
                total = total + r2_in[half, side, i]
            ag_buf[half, z, y, side] = total.astype(BF16)
            for k in (1, 3, 2):
                gather_one(half, side, k).start()

    def after_three(half):
        for side in range(2):
            for k in (1, 3, 2):
                gather_one(half, side, k).wait_recv()
            for k in (1, 3, 2):
                gather_two(half, side, k).start()
            own_gsum(half, side).start()

    def out_cols(m, carry):
        lanes = pl.ds(pl.multiple_of(m * COLS, COLS), COLS)
        product = dot_nn(gated[...], wout[m].reshape(WIDTH, COLS))
        out_ref[:, lanes] = (product + act[:, lanes].astype(F32)).astype(BF16)
        return carry

    def t1_copy(k):
        return remote(tab_one.at[d], tab_one.at[d], t1_s.at[k], t1_r.at[k], (h, dpo(k)))

    def t2_copy(k):
        return remote(tab_two.at[z], tab_two.at[z], t2_s.at[k], t2_r.at[k], place(along(0, k)))

    def t3_copy(k):
        return remote(tab_three.at[y], tab_three.at[y], t3_s.at[k], t3_r.at[k], place(along(1, k)))

    def table_sum(ref, count):
        total = ref[0]
        for i in range(1, count):
            total = total + ref[i]
        return total

    back_steps(0, 0, 3)
    own_back(0)
    back_steps(1, 0, 2)
    weight_half(0)
    back_steps(1, 2, 3)
    own_back(1)

    table = jnp.zeros((HEADS, BUCKETS), F32)
    for term in reversed(three_parts(jnp.sum(tsum[...], axis=1))):
        table = table + dot_nt(term, hot)
    tab_one[d] = table
    run(t1_copy, DP, "start")

    lax.fori_loop(0, 2, out_cols, 0)
    after_one(0)
    weight_half(1)
    lax.fori_loop(2, 4, out_cols, 0)
    for copy in [*wring.values(), own_wout]:
        copy.wait_send()
    for k in range(1, 4):
        plane_share(k).wait_send()
    for step in plane_steps:
        for copy in plane_two(*step):
            copy.wait_send()
    after_two(0)

    run(t1_copy, DP, "wait_recv")
    tab_two[z] = table_sum(tab_one, DP)
    for k in (1, 3, 2):
        t2_copy(k).start()

    after_one(1)
    lax.fori_loop(4, 6, out_cols, 0)
    after_three(0)
    after_two(1)
    for k in (1, 3, 2):
        t2_copy(k).wait_recv()
    tab_three[y] = table_sum(tab_two, 4)
    for k in (1, 3, 2):
        t3_copy(k).start()
    lax.fori_loop(6, DP, out_cols, 0)
    after_three(1)

    for k in (1, 3, 2):
        t3_copy(k).wait_recv()
    gtab_ref[...] = table_sum(tab_three, 4)

    run(t1_copy, DP, "wait_send")
    for k in (1, 3, 2):
        t2_copy(k).wait_send()
        t3_copy(k).wait_send()
    for half in range(2):
        run(gq_copy, DP, "wait_send", half)
        for side in range(2):
            for k in (1, 3, 2):
                for copy in (sum_one, sum_two, gather_one):
                    copy(half, side, k).wait_send()
                gather_two(half, side, k).wait()
            own_gsum(half, side).wait()


def layer(actions, cotangent, cache, length, buckets, new_bucket, ln_gain, norm_gain, w_frozen, w_query, w_out, rab):
    any_space = pl.BlockSpec(memory_space=pl.ANY)
    vmem = pl.BlockSpec(memory_space=pltpu.VMEM)
    smem = pl.BlockSpec(memory_space=pltpu.SMEM)
    dma = pltpu.SemaphoreType.DMA
    sem_sizes = (12, KV_COPIES, KV_COPIES, HIST, HIST, 9, 9, DP, DP, 9, 9, 4, 4, 18, 18, 18, 18, 4, 4, 2 * DP, 2 * DP, *[16] * 8, DP, DP, 4, 4, 4, 4)
    return pl.pallas_call(
        kernel,
        out_shape=(
            jax.ShapeDtypeStruct((TOK, WIDTH), BF16),
            jax.ShapeDtypeStruct((4, 4, 2, HEAD // 2, COLS), BF16),
            jax.ShapeDtypeStruct((HEADS, BUCKETS), F32),
        ),
        in_specs=[any_space, any_space, any_space, smem, vmem, vmem, vmem, vmem, any_space, any_space, any_space, vmem],
        out_specs=(vmem, any_space, vmem),
        scratch_shapes=[
            pltpu.VMEM((TOK, WIDTH), BF16),
            pltpu.VMEM((TOK, WIDTH), BF16),
            pltpu.VMEM((4, WIDTH, COLS), BF16),
            pltpu.VMEM((DP, TOK, WIDTH), BF16),
            pltpu.VMEM((DP, TOK, COLS), F32),
            pltpu.VMEM((DP, TOK, 4 * COLS), BF16),
            pltpu.VMEM((DP, TOK, 4 * COLS), BF16),
            pltpu.VMEM((2, CACHED, WIDTH), BF16),
            pltpu.VMEM((HIST, 8, TOK), jnp.int32),
        pltpu.VMEM((HIST, 8, TOK), jnp.int32),
            pltpu.VMEM((BUCKETS, KEYS), BF16),
            pltpu.VMEM((HEADS, KEYS), F32),
            pltpu.VMEM((TOK, WIDTH), F32),
            pltpu.VMEM((HEADS, TOK, KEYS), F32),
            pltpu.VMEM((DP, 2, 4, 4, 2, 32, COLS), BF16),
            pltpu.VMEM((TOK, WIDTH), F32),
            pltpu.VMEM((TOK, WIDTH), F32),
            pltpu.VMEM((TOK, TOK), F32),
            pltpu.VMEM((TOK, WIDTH), BF16),
            pltpu.VMEM((TOK, WIDTH), BF16),
            pltpu.VMEM((HEADS, 8, KEYS), F32),
            pltpu.VMEM((2, DP, TOK, HEAD), BF16),
            pltpu.VMEM((2, DP, TOK, HEAD), BF16),
            pltpu.VMEM((2, HEAD, DP * TOK), BF16),
            pltpu.VMEM((2, 4, 4, 2, HEAD // 2, HEAD), BF16),
            pltpu.VMEM((2, 2, 4, 4, HEAD // 2, HEAD), BF16),
            pltpu.VMEM((2, 2, 4, HEAD // 2, HEAD), F32),
            pltpu.VMEM((2, 2, 4, HEAD // 2, HEAD), F32),
            pltpu.VMEM((2, 4, 4, 2, HEAD // 2, HEAD), BF16),
            pltpu.VMEM((DP, HEADS, BUCKETS), F32),
            pltpu.VMEM((4, HEADS, BUCKETS), F32),
            pltpu.VMEM((4, HEADS, BUCKETS), F32),
        ]
        + [dma((n,)) for n in sem_sizes],
        compiler_params=pltpu.CompilerParams(collective_id=0, has_side_effects=True, vmem_limit_bytes=60 * 1024 * 1024),
        name="layer",
    )(actions, cotangent, cache, length, buckets, new_bucket, ln_gain, norm_gain, w_frozen, w_query, w_out, rab)


ADAM_ROWS = 1024


def adam_kernel(
    grad, weight, moment_one, moment_two, table_grad, table, table_one, table_two, done,
    weight_new, one_new, two_new, table_new, table_one_new, table_two_new, result,
):
    updated = adam_update(weight[...], moment_one[...], moment_two[...], grad[...].astype(F32))
    weight_new[...], one_new[...], two_new[...] = updated
    result[...] = done[...]

    @pl.when(pl.program_id(0) == 0)
    def _():
        updated = adam_update(table[...], table_one[...], table_two[...], table_grad[...])
        table_new[...], table_one_new[...], table_two_new[...] = updated


def adam(grad, weight, moment_one, moment_two, table_grad, table, table_one, table_two, done):
    steps = WIDTH // ADAM_ROWS
    rows = pl.BlockSpec((ADAM_ROWS, COLS), lambda i: (i, 0))
    small = pl.BlockSpec((HEADS, BUCKETS), lambda i: (0, 0))
    tokens = pl.BlockSpec((TOK // steps, WIDTH), lambda i: (i, 0))
    operands = (grad, weight, moment_one, moment_two, table_grad, table, table_one, table_two, done)
    return pl.pallas_call(
        adam_kernel,
        grid=(steps,),
        out_shape=[jax.ShapeDtypeStruct(a.shape, a.dtype) for a in operands[1:4] + operands[5:]],
        in_specs=[rows] * 4 + [small] * 4 + [tokens],
        out_specs=[rows] * 3 + [small] * 3 + [tokens],
        name="adam",
    )(*operands)


def shards(
    actions, cotangent, cache_kv, cache_len, cache_bucket, new_bucket, ln_gain, norm_gain,
    w_frozen, w_query, query_m, query_v, w_out, rab_table, rab_m, rab_v,
):
    result, grad_sum, grad_table = layer(
        actions.reshape(TOK, WIDTH),
        cotangent.reshape(TOK, WIDTH),
        cache_kv.reshape(2, HIST, SLAB, WIDTH),
        cache_len.reshape(1, 1),
        cache_bucket,
        new_bucket.reshape(1, TOK),
        ln_gain.reshape(1, WIDTH),
        norm_gain.reshape(1, WIDTH),
        w_frozen,
        w_query,
        w_out.reshape(2, 4, 4, 2, 32, COLS),
        rab_table,
    )
    query_new, query_m_new, query_v_new, rab_new, rab_m_new, rab_v_new, result = adam(
        grad_sum.reshape(WIDTH, COLS), w_query, query_m, query_v, grad_table, rab_table, rab_m, rab_v, result
    )
    return (result.reshape(actions.shape), query_new, query_m_new, query_v_new, rab_new, rab_m_new, rab_v_new)


def solution(mesh):
    placed = (
        P("history", "dp", None, None),
        P("history", "dp", None, None),
        P(None, None, "dp", "history", None),
        P("history", "dp"),
        P(None, "dp", "history"),
        P("history", "dp", None),
        P(),
        P(),
        P(None, None, "dp"),
        P(None, "dp"),
        P(None, "dp"),
        P(None, "dp"),
        P(None, "dp"),
        P(),
        P(),
        P(),
    )
    return jax.shard_map(
        shards,
        mesh=mesh,
        in_specs=placed,
        out_specs=(
            P("history", "dp", None, None),
            P(None, "dp"),
            P(None, "dp"),
            P(None, "dp"),
            P(),
            P(),
            P(),
        ),
        check_vma=False,
    )
```

```python
import functools

import jax
import jax.numpy as jnp
from jax import lax
from jax.experimental import pallas as pl
from jax.experimental.pallas import tpu as pltpu
from jax.sharding import PartitionSpec as P

BETA_ONE = 0.9
BETA_TWO = 0.95
LEARN_RATE = 0.001
ADAM_EPS = 1e-08
NORM_EPS = 1e-05

MESH = pl.DeviceIdType.MESH
F32 = jnp.float32
BF16 = jnp.bfloat16

TOK = 128
WIDTH = 2048
COLS = 256
HEAD = 128
HEADS = 16
BUCKETS = 128
HIST = 16
DP = 8
SLAB = 32
CACHED = HIST * SLAB
KEYS = CACHED + TOK
SCALE = HEAD ** (-0.5)
KV_COPIES = 4 * (HIST - 1) + 1
KV_HALF = 2 * (HIST - 1) + 1
LINK_ORDER = (1, 4, 3, 12, 2, 8, 5, 15, 7, 13, 6, 9, 14, 11, 10)


def adam_update(weight, moment_one, moment_two, gradient):
    first_new = BETA_ONE * moment_one + (1.0 - BETA_ONE) * gradient
    second_new = BETA_TWO * moment_two + (1.0 - BETA_TWO) * gradient * gradient
    stepped = weight.astype(F32) - LEARN_RATE * first_new / (jnp.sqrt(second_new) + ADAM_EPS)
    return (stepped.astype(weight.dtype), first_new, second_new)


def dot_nn(a, b):
    return jnp.dot(a, b, preferred_element_type=F32)


def dot_nt(a, b):
    return lax.dot_general(a, b, (((1,), (1,)), ((), ())), preferred_element_type=F32)


def three_parts(values):
    first = values.astype(BF16)
    rest = values - first.astype(F32)
    second = rest.astype(BF16)
    third = (rest - second.astype(F32)).astype(BF16)
    return first, second, third


def silu_slope(values):
    sigmoid = 0.5 * jnp.tanh(0.5 * values) + 0.5
    return sigmoid * (1.0 + values * (1.0 - sigmoid))


def kernel(
    act_hbm, cot_hbm, cache_hbm, length, buckets, new_bucket, ln_gain, norm_gain, frozen_hbm, query_hbm, wout_hbm, rab,
    out_ref, gsum_hbm, gtab_ref,
    act, cot, wts, rows, pre_slope, sent, proj, kv, bk_out, bks, onehot, bias, att, slope, wout, grad_gated, gate_scaled, inverse_std, gated, grad_att,
    tsum, gq_out, gq_in, grad_pre_t, rs_out, r1_in, r2_out, r2_in, ag_buf, tab_one, tab_two, tab_three,
    loc_sem, kv_s, kv_r, bk_s, bk_r, g_s, g_r, pj_s, pj_r, w_s, w_r, px_s, px_r, p1_s, p1_r, p2_s, p2_r, p3_s, p3_r, gq_s, gq_r, r1_s, r1_r, r2_s, r2_r, a2_s, a2_r, t1_s, t1_r, t2_s, t2_r, t3_s, t3_r,
):
    h = lax.axis_index("history")
    d = lax.axis_index("dp")
    z, y = h // 4, lax.rem(h, 4)
    x, c = d // 2, lax.rem(d, 2)

    def hist(k):
        return lax.rem(z + k // 4, 4) * 4 + lax.rem(y + lax.rem(k, 4), 4)

    def dpx(kx, kc):
        return lax.rem(x + kx, 4) * 2 + lax.rem(c + kc, 2)

    def dpo(k):
        return lax.rem(x + k // 2, 4) * 2 + lax.rem(c + lax.rem(k, 2), 2)

    barrier = pltpu.get_barrier_semaphore()

    def greet_hist(k, carry):
        pl.semaphore_signal(barrier, inc=1, device_id=(hist(k), d), device_id_type=MESH)
        return carry

    def greet_dp(k, carry):
        pl.semaphore_signal(barrier, inc=1, device_id=(h, dpo(k)), device_id_type=MESH)
        return carry

    lax.fori_loop(1, DP, greet_dp, 0)
    lax.fori_loop(1, HIST, greet_hist, 0)

    load_act = pltpu.make_async_copy(act_hbm, act, loc_sem.at[0])
    load_act.start()
    load_query = pltpu.make_async_copy(query_hbm, wts.at[0], loc_sem.at[1])
    load_query.start()
    load_frozen = pltpu.make_async_copy(frozen_hbm, wts.at[pl.ds(1, 3)], loc_sem.at[2])
    load_frozen.start()
    load_cot = pltpu.make_async_copy(cot_hbm, cot, loc_sem.at[3])
    load_cot.start()
    load_wout = pltpu.make_async_copy(wout_hbm, wout.at[d], loc_sem.at[4])
    load_wout.start()
    own_slab = kv.at[:, pl.ds(pl.multiple_of(h * SLAB, SLAB), SLAB), :]
    load_kv = pltpu.make_async_copy(cache_hbm.at[:, h], own_slab, loc_sem.at[5])
    load_kv.start()
    lane = lax.broadcasted_iota(jnp.int32, (HIST, TOK), 1)
    placed = jnp.where(lane // SLAB == y, jnp.concatenate([buckets[:, 0, :]] * 4, axis=1), 0)
    for u in range(HIST):
        bk_out[u] = jnp.broadcast_to(placed[u : u + 1, :], (8, TOK))

    def run(copy, stop, what, *half):
        def step(k, carry):
            getattr(copy(*half, k), what)()
            return carry

        lax.fori_loop(1, stop, step, 0)

    load_act.wait()

    def norm_rows(r, carry):
        part = pl.ds(pl.multiple_of(r * 16, 16), 16)
        values = act[part, :].astype(F32)
        center = values - jnp.mean(values, axis=-1, keepdims=True)
        inverse = lax.rsqrt(jnp.mean(center * center, axis=-1, keepdims=True) + NORM_EPS)
        rows[d, part, :] = (center * inverse * ln_gain[...]).astype(BF16)
        return carry

    lax.fori_loop(0, TOK // 16, norm_rows, 0)
    pl.semaphore_wait(barrier, HIST - 1 + DP - 1)

    def remote(src, dst, send, recv, device):
        return pltpu.make_async_remote_copy(
            src_ref=src, dst_ref=dst, send_sem=send, recv_sem=recv, device_id=device, device_id_type=MESH
        )

    def ring_gather(block, half, own, send, recv, first=0):
        right, left, sibling = (h, dpx(1, 0)), (h, dpx(3, 0)), (h, dpx(0, 1))
        from_left, from_right, far = dpx(3, 0), dpx(1, 0), dpx(2, 0)
        specs = [
            (own, block(d), sibling),
            (own, block(d), right),
            (own, block(d), left),
            (half(from_left, 0), half(from_left, 0), right),
            (half(from_right, 1), half(from_right, 1), left),
            (block(from_left), block(from_left), sibling),
            (block(from_right), block(from_right), sibling),
            (half(far, 0), half(far, 0), sibling),
            (half(far, 1), half(far, 1), sibling),
        ]
        numbered = list(enumerate(specs))[first:]
        return {i: remote(s, t, send.at[i], recv.at[i], dev) for i, (s, t, dev) in numbered}

    ring = ring_gather(
        lambda i: rows.at[i],
        lambda i, k: rows.at[i, pl.ds(k * (TOK // 2), TOK // 2)],
        rows.at[d],
        g_s,
        g_r,
    )
    for i in (1, 2, 0):
        ring[i].start()

    def kv_copy(i):
        piece, turn = divmod(i - 1, HIST - 1)
        to = hist(LINK_ORDER[turn])
        part, low = piece % 2, piece // 2 * 16
        src = cache_hbm.at[part, to, pl.ds(low, 16)]
        dst = kv.at[part, pl.ds(pl.multiple_of(h * SLAB + low, 16), 16), :]
        return remote(src, dst, kv_s.at[i], kv_r.at[i], (to, d))

    def bk_copy(k):
        to = hist(k)
        return remote(bk_out.at[to], bks.at[h], bk_s.at[k], bk_r.at[k], (to, d))

    def plane_x(k):
        return remote(wout_hbm.at[0, z, y], wout.at[d, 0, z, y], px_s.at[k], px_r.at[k], (h, dpx(k, 0)))

    def plane_one(k, kx):
        slot, i = dpx(kx, 0), 3 * (k - 1) + kx - 1
        over_z, over_y = wout.at[slot, 0, z, y, 0], wout.at[slot, 0, z, y, 1]
        to_z, to_y = lax.rem(z + k, 4) * 4 + y, z * 4 + lax.rem(y + k, 4)
        return (
            remote(over_z, over_z, p1_s.at[i], p1_r.at[i], (to_z, d)),
            remote(over_y, over_y, p1_s.at[9 + i], p1_r.at[9 + i], (to_y, d)),
        )

    def plane_two(k, kx):
        slot, i = dpx(kx, 0), 3 * (k - 1) + kx - 1
        over_y, over_z = wout.at[slot, 0, :, y, 0], wout.at[slot, 0, z, :, 1]
        to_z, to_y = lax.rem(z + k, 4) * 4 + y, z * 4 + lax.rem(y + k, 4)
        return (
            remote(over_y, over_y, p2_s.at[i], p2_r.at[i], (to_y, d)),
            remote(over_z, over_z, p2_s.at[9 + i], p2_r.at[9 + i], (to_z, d)),
        )

    def plane_share(kx):
        block = wout.at[dpx(kx, 0), 0]
        return remote(block, block, p3_s.at[kx], p3_r.at[kx], (h, dpx(0, 1)))

    own_wout = remote(wout_hbm, wout.at[d], p3_s.at[0], p3_r.at[0], (h, dpx(0, 1)))
    wring = ring_gather(
        lambda i: wout.at[i, 1],
        lambda i, k: wout.at[i, 1, pl.ds(2 * k, 2)],
        wout_hbm.at[1],
        w_s,
        w_r,
        first=1,
    )
    plane_steps = [(k, kx) for k in (1, 3, 2) for kx in (1, 2, 3)]
    for k in range(1, 4):
        plane_x(k).start()

    def send_bk(k, carry):
        bk_copy(k).start()
        return carry

    lax.fori_loop(1, HIST, send_bk, 0)
    for i in range(1, KV_HALF):
        kv_copy(i).start()

    def project(chip):
        part = pl.ds(pl.multiple_of(chip * 2, 2), 2)
        chip_rows = rows[part].reshape(2 * TOK, WIDTH)
        for j in range(4):
            pre = dot_nn(chip_rows, wts[j])
            sigmoid = 0.5 * jnp.tanh(0.5 * pre) + 0.5
            acted = pre * sigmoid
            if j == 0:
                pre_slope[part] = (sigmoid + acted * (1.0 - sigmoid)).reshape(2, TOK, COLS)
            sent[part, :, pl.ds(j * COLS, COLS)] = acted.astype(BF16).reshape(2, TOK, COLS)

    def pj_copy(k):
        to = dpo(k)
        return remote(sent.at[to], proj.at[d], pj_s.at[k], pj_r.at[k], (h, to))

    load_query.wait()
    load_frozen.wait()
    ring[0].wait_recv()
    project(x)
    pj_copy(1).start()
    own_proj = pltpu.make_async_copy(sent.at[d], proj.at[d], loc_sem.at[7])
    own_proj.start()
    for k in range(1, 4):
        plane_x(k).wait_recv()
    for step in plane_steps:
        for copy in plane_one(*step):
            copy.start()
    for i in range(KV_HALF, KV_COPIES):
        kv_copy(i).start()
    ring[1].wait_recv()
    ring[3].start()
    ring[5].start()
    ring[2].wait_recv()
    ring[4].start()
    ring[6].start()
    ring[5].wait_recv()
    project(lax.rem(x + 3, 4))
    pj_copy(6).start()
    pj_copy(7).start()
    ring[6].wait_recv()
    project(lax.rem(x + 1, 4))
    pj_copy(2).start()
    pj_copy(3).start()
    for i in (1, 2):
        wring[i].start()
    own_wout.start()
    ring[3].wait_recv()
    ring[7].start()
    ring[4].wait_recv()
    ring[8].start()
    ring[7].wait_recv()
    ring[8].wait_recv()
    project(lax.rem(x + 2, 4))
    pj_copy(4).start()
    pj_copy(5).start()

    for step in plane_steps:
        for copy in plane_one(*step):
            copy.wait_recv()
    for step in plane_steps:
        for copy in plane_two(*step):
            copy.start()

    bks[h] = bk_out[h]

    def wait_bk(k, carry):
        bk_copy(k).wait_recv()
        return carry

    lax.fori_loop(1, HIST, wait_bk, 0)
    levels = lax.broadcasted_iota(jnp.int32, (BUCKETS, TOK), 0)
    for q in range(4):
        ids = (bks[4 * q] + bks[4 * q + 1] + bks[4 * q + 2] + bks[4 * q + 3])[0:1, :]
        onehot[:, pl.ds(q * TOK, TOK)] = jnp.where(levels == ids, 1.0, 0.0).astype(BF16)
    onehot[:, pl.ds(CACHED, TOK)] = jnp.where(levels == new_bucket[...], 1.0, 0.0).astype(BF16)
    hot = onehot[...]
    bias_sum = jnp.zeros((HEADS, KEYS), F32)
    for term in reversed(three_parts(rab[...])):
        bias_sum = bias_sum + dot_nn(term, hot)
    bias[...] = bias_sum

    count = length[0, 0]
    share = 1.0 / jnp.full((1, TOK), count + TOK, jnp.int32).astype(F32)
    cached_pos = lax.broadcasted_iota(jnp.int32, (1, CACHED), 1)
    share_cached = jnp.where(cached_pos < count, jnp.concatenate([share] * 4, axis=1), 0.0)
    row_pos = lax.broadcasted_iota(jnp.int32, (TOK, TOK), 0)
    col_pos = lax.broadcasted_iota(jnp.int32, (TOK, TOK), 1)
    share_new = jnp.where(col_pos <= row_pos, jnp.broadcast_to(share, (TOK, TOK)), 0.0)

    for i in (1, 2):
        wring[i].wait_recv()
        wring[i + 2].start()
        wring[i + 4].start()

    def wait_pj(k, carry):
        pj_copy(k).wait_recv()
        return carry

    own_proj.wait()
    lax.fori_loop(1, DP, wait_pj, 0)

    load_kv.wait()
    for i in range(1, KV_COPIES):
        kv_copy(i).wait_recv()

    def attend(m, carry):
        for k in range(2):
            head = m * 2 + k
            lanes = pl.ds(pl.multiple_of(head * HEAD, HEAD), HEAD)
            query = proj[m, :, pl.ds(k * HEAD, HEAD)]
            value_new = proj[m, :, pl.ds(2 * COLS + k * HEAD, HEAD)]
            key_new = proj[m, :, pl.ds(3 * COLS + k * HEAD, HEAD)]
            key_bias = bias[pl.ds(head, 1), :]
            total = jnp.zeros((TOK, HEAD), F32)
            parts = (
                (kv[0, :, lanes], kv[1, :, lanes], pl.ds(0, CACHED), key_bias[:, :CACHED], share_cached),
                (key_new, value_new, pl.ds(CACHED, TOK), key_bias[:, CACHED:], share_new),
            )
            for keys, values, where, bias_part, share_part in parts:
                score = dot_nt(query, keys) * SCALE + bias_part
                sigmoid = 0.5 * jnp.tanh(0.5 * score) + 0.5
                weight = score * sigmoid * share_part
                slope[head, :, where] = sigmoid * share_part + weight * (1.0 - sigmoid)
                total = total + dot_nn(weight.astype(BF16), values)
            att[:, lanes] = total
        return carry

    lax.fori_loop(0, DP, attend, 0)

    def stat_rows(r, carry):
        part = pl.ds(pl.multiple_of(r * 16, 16), 16)
        values = att[part, :]
        center = values - jnp.mean(values, axis=-1, keepdims=True)
        inverse = lax.rsqrt(jnp.mean(center * center, axis=-1, keepdims=True) + NORM_EPS)
        nhat = center * inverse
        gate = jnp.concatenate([proj[m, part, pl.ds(COLS, COLS)] for m in range(DP)], axis=1).astype(F32)
        scaled = gate * norm_gain[...]
        att[part, :] = nhat
        gate_scaled[part, :] = scaled
        gated[part, :] = (nhat * scaled).astype(BF16)
        inverse_std[part, :] = jnp.broadcast_to(inverse, (16, TOK))
        return carry

    lax.fori_loop(0, TOK // 16, stat_rows, 0)

    load_cot.wait()
    load_wout.wait()

    def gated_part(m, half, first=False):
        lanes = pl.ds(pl.multiple_of(m * COLS, COLS), COLS)
        for n in range(2):
            cols = pl.ds(half * 1024 + n * 512, 512)
            part = dot_nt(cot[:, lanes], wout[m, half, pl.ds(2 * n, 2)].reshape(512, COLS))
            grad_gated[:, cols] = part if first else grad_gated[:, cols] + part

    run(bk_copy, HIST, "wait_send")
    run(pj_copy, DP, "wait_send")
    for i in range(1, KV_COPIES):
        kv_copy(i).wait_send()
    for copy in ring.values():
        copy.wait_send()
    for k in range(1, 4):
        plane_x(k).wait_send()
    for step in plane_steps:
        for copy in plane_one(*step):
            copy.wait_send()

    for step in plane_steps:
        for copy in plane_two(*step):
            copy.wait_recv()
    for k in range(1, 4):
        plane_share(k).start()
    gated_part(d, 0, True)
    gated_part(d, 1, True)
    own_wout.wait_recv()
    gated_part(dpx(0, 1), 0)
    gated_part(dpx(0, 1), 1)
    gated_part(dpx(3, 0), 1)
    gated_part(dpx(1, 0), 1)
    for i in (3, 4):
        wring[i].wait_recv()
        wring[i + 4].start()
    for k in (3, 1, 2):
        gated_part(dpx(k, 0), 0)
    for k in (3, 1, 2):
        plane_share(k).wait_recv()
        gated_part(dpx(k, 1), 0)
    wring[5].wait_recv()
    gated_part(dpx(3, 1), 1)
    wring[6].wait_recv()
    gated_part(dpx(1, 1), 1)
    gated_part(dpx(2, 0), 1)
    wring[7].wait_recv()
    wring[8].wait_recv()
    gated_part(dpx(2, 1), 1)

    def gate_rows(r, carry):
        part = pl.ds(pl.multiple_of(r * 16, 16), 16)
        nhat = att[part, :]
        grad_hat = grad_gated[part, :] * gate_scaled[part, :]
        along = jnp.mean(grad_hat * nhat, axis=-1, keepdims=True)
        grad = inverse_std[part, 0:1] * (grad_hat - jnp.mean(grad_hat, axis=-1, keepdims=True) - nhat * along)
        grad_att[part, :] = grad.astype(BF16)
        return carry

    lax.fori_loop(0, TOK // 16, gate_rows, 0)

    def gq_copy(half, k):
        to, i = dpo(k), half * DP + k
        return remote(gq_out.at[half, to], gq_in.at[half, d], gq_s.at[i], gq_r.at[i], (h, to))

    def attend_back(m, k):
        head = m * 2 + k
        lanes = pl.ds(pl.multiple_of(head * HEAD, HEAD), HEAD)
        value_new = proj[m, :, pl.ds(2 * COLS + k * HEAD, HEAD)]
        key_new = proj[m, :, pl.ds(3 * COLS + k * HEAD, HEAD)]
        grad = grad_att[:, lanes]
        total = jnp.zeros((TOK, HEAD), F32)
        parts = (
            (kv[0, :, lanes], kv[1, :, lanes], pl.ds(0, CACHED)),
            (key_new, value_new, pl.ds(CACHED, TOK)),
        )
        for keys, values, where in parts:
            grad_score = dot_nt(grad, values) * slope[head, :, where]
            tsum[head, :, where] = jnp.sum(grad_score.reshape(TOK // 8, 8, -1), axis=0)
            total = total + dot_nn(grad_score.astype(BF16), keys)
        gq_out[k, m] = (total * SCALE).astype(BF16)

    def back_steps(half, first, stop):
        def step(i, carry):
            k = 2 * i + 1
            attend_back(dpo(k), half)
            attend_back(dpo(k + 1), half)
            gq_copy(half, k).start()
            gq_copy(half, k + 1).start()
            return carry

        lax.fori_loop(first, stop, step, 0)

    def own_back(half):
        attend_back(dpo(DP - 1), half)
        attend_back(d, half)
        gq_copy(half, DP - 1).start()
        gq_in[half, d] = gq_out[half, d]

    def weight_half(half):
        run(gq_copy, DP, "wait_recv", half)
        for i in range(DP):
            pre = pre_slope[i, :, pl.ds(half * HEAD, HEAD)]
            grad_pre_t[half, :, pl.ds(i * TOK, TOK)] = (gq_in[half, i].astype(F32) * pre).astype(BF16).T
        for i in range(4):
            piece = dot_nn(grad_pre_t[half], rows[:, :, pl.ds(i * 512, 512)].reshape(DP * TOK, 512)).astype(BF16)
            rs_out[half, i] = piece.T.reshape(4, 2, HEAD // 2, HEAD)
        for k in (1, 3, 2):
            for side in range(2):
                sum_one(half, side, k).start()

    def along(side, k):
        return (lax.rem(z + k, 4), y) if side == 0 else (z, lax.rem(y + k, 4))

    def place(zy):
        return (zy[0] * 4 + zy[1], d)

    def line(ref, half, side, zy):
        return ref.at[half, zy[0], :, side] if side == 0 else ref.at[half, :, zy[1], side]

    def own(side):
        return z if side == 0 else y

    def sems(pair, half, side, k):
        i = (half * 2 + side) * 4 + k
        return pair[0].at[i], pair[1].at[i]

    def sum_one(half, side, k):
        to = along(side, k)
        return remote(line(rs_out, half, side, to), r1_in.at[half, side, own(side)], *sems((r1_s, r1_r), half, side, k), place(to))

    def sum_two(half, side, k):
        src, dst = r2_out.at[half, side], r2_in.at[half, side, own(1 - side)]
        return remote(src, dst, *sems((r2_s, r2_r), half, side, k), place(along(1 - side, k)))

    def gsum_line(half, side):
        lanes = pl.ds(half * HEAD, HEAD)
        return gsum_hbm.at[z, :, side, :, lanes] if side == 0 else gsum_hbm.at[:, y, side, :, lanes]

    def gather_two(half, side, k):
        src = line(ag_buf, half, side, (z, y))
        return remote(src, gsum_line(half, side), *sems((a2_s, a2_r), half, side, k), place(along(side, k)))

    def own_gsum(half, side):
        return pltpu.make_async_copy(line(ag_buf, half, side, (z, y)), gsum_line(half, side), loc_sem.at[8 + half * 2 + side])

    def after_one(half):
        for side in range(2):
            r1_in[half, side, own(side)] = rs_out[half, z, :, 0] if side == 0 else rs_out[half, :, y, 1]
            for k in (1, 3, 2):
                sum_one(half, side, k).wait_recv()
            total = r1_in[half, side, 0].astype(F32)
            for i in range(1, 4):
                total = total + r1_in[half, side, i].astype(F32)
            r2_out[half, side] = total.astype(BF16)
            for k in (1, 3, 2):
                sum_two(half, side, k).start()

    def after_two(half):
        for side in range(2):
            r2_in[half, side, own(1 - side)] = r2_out[half, side]
            for k in (1, 3, 2):
                sum_two(half, side, k).wait_recv()
            total = r2_in[half, side, 0].astype(F32)
            for i in range(1, 4):
                total = total + r2_in[half, side, i].astype(F32)
            if side == 0:
                ag_buf[half, z, :, 0] = total.astype(BF16)
            else:
                ag_buf[half, :, y, 1] = total.astype(BF16)
            for k in (1, 3, 2):
                gather_two(half, side, k).start()
            own_gsum(half, side).start()

    def out_cols(m, carry):
        lanes = pl.ds(pl.multiple_of(m * COLS, COLS), COLS)
        product = dot_nn(gated[...], wout[m].reshape(WIDTH, COLS))
        out_ref[:, lanes] = (product + act[:, lanes].astype(F32)).astype(BF16)
        return carry

    def t1_copy(k):
        return remote(tab_one.at[d], tab_one.at[d], t1_s.at[k], t1_r.at[k], (h, dpo(k)))

    def t2_copy(k):
        return remote(tab_two.at[z], tab_two.at[z], t2_s.at[k], t2_r.at[k], place(along(0, k)))

    def t3_copy(k):
        return remote(tab_three.at[y], tab_three.at[y], t3_s.at[k], t3_r.at[k], place(along(1, k)))

    def table_sum(ref, count):
        total = ref[0]
        for i in range(1, count):
            total = total + ref[i]
        return total

    back_steps(0, 0, 3)
    own_back(0)
    back_steps(1, 0, 2)
    weight_half(0)
    back_steps(1, 2, 3)
    own_back(1)

    table = jnp.zeros((HEADS, BUCKETS), F32)
    for term in reversed(three_parts(jnp.sum(tsum[...], axis=1))):
        table = table + dot_nt(term, hot)
    tab_one[d] = table
    run(t1_copy, DP, "start")

    lax.fori_loop(0, 2, out_cols, 0)
    after_one(0)
    weight_half(1)
    lax.fori_loop(2, 4, out_cols, 0)
    for copy in [*wring.values(), own_wout]:
        copy.wait_send()
    for k in range(1, 4):
        plane_share(k).wait_send()
    for step in plane_steps:
        for copy in plane_two(*step):
            copy.wait_send()
    after_two(0)

    run(t1_copy, DP, "wait_recv")
    tab_two[z] = table_sum(tab_one, DP)
    for k in (1, 3, 2):
        t2_copy(k).start()

    after_one(1)
    lax.fori_loop(4, 6, out_cols, 0)
    after_two(1)
    for k in (1, 3, 2):
        t2_copy(k).wait_recv()
    tab_three[y] = table_sum(tab_two, 4)
    for k in (1, 3, 2):
        t3_copy(k).start()
    lax.fori_loop(6, DP, out_cols, 0)

    for k in (1, 3, 2):
        t3_copy(k).wait_recv()
    gtab_ref[...] = table_sum(tab_three, 4)

    run(t1_copy, DP, "wait_send")
    for k in (1, 3, 2):
        t2_copy(k).wait_send()
        t3_copy(k).wait_send()
    for half in range(2):
        run(gq_copy, DP, "wait_send", half)
        for side in range(2):
            for k in (1, 3, 2):
                for copy in (sum_one, sum_two):
                    copy(half, side, k).wait_send()
                gather_two(half, side, k).wait()
            own_gsum(half, side).wait()


def layer(actions, cotangent, cache, length, buckets, new_bucket, ln_gain, norm_gain, w_frozen, w_query, w_out, rab):
    any_space = pl.BlockSpec(memory_space=pl.ANY)
    vmem = pl.BlockSpec(memory_space=pltpu.VMEM)
    smem = pl.BlockSpec(memory_space=pltpu.SMEM)
    dma = pltpu.SemaphoreType.DMA
    sem_sizes = (12, KV_COPIES, KV_COPIES, HIST, HIST, 9, 9, DP, DP, 9, 9, 4, 4, 18, 18, 18, 18, 4, 4, 2 * DP, 2 * DP, *[16] * 6, DP, DP, 4, 4, 4, 4)
    return pl.pallas_call(
        kernel,
        out_shape=(
            jax.ShapeDtypeStruct((TOK, WIDTH), BF16),
            jax.ShapeDtypeStruct((4, 4, 2, HEAD // 2, COLS), BF16),
            jax.ShapeDtypeStruct((HEADS, BUCKETS), F32),
        ),
        in_specs=[any_space, any_space, any_space, smem, vmem, vmem, vmem, vmem, any_space, any_space, any_space, vmem],
        out_specs=(vmem, any_space, vmem),
        scratch_shapes=[
            pltpu.VMEM((TOK, WIDTH), BF16),
            pltpu.VMEM((TOK, WIDTH), BF16),
            pltpu.VMEM((4, WIDTH, COLS), BF16),
            pltpu.VMEM((DP, TOK, WIDTH), BF16),
            pltpu.VMEM((DP, TOK, COLS), F32),
            pltpu.VMEM((DP, TOK, 4 * COLS), BF16),
            pltpu.VMEM((DP, TOK, 4 * COLS), BF16),
            pltpu.VMEM((2, CACHED, WIDTH), BF16),
            pltpu.VMEM((HIST, 8, TOK), jnp.int32),
        pltpu.VMEM((HIST, 8, TOK), jnp.int32),
            pltpu.VMEM((BUCKETS, KEYS), BF16),
            pltpu.VMEM((HEADS, KEYS), F32),
            pltpu.VMEM((TOK, WIDTH), F32),
            pltpu.VMEM((HEADS, TOK, KEYS), F32),
            pltpu.VMEM((DP, 2, 4, 4, 2, 32, COLS), BF16),
            pltpu.VMEM((TOK, WIDTH), F32),
            pltpu.VMEM((TOK, WIDTH), F32),
            pltpu.VMEM((TOK, TOK), F32),
            pltpu.VMEM((TOK, WIDTH), BF16),
            pltpu.VMEM((TOK, WIDTH), BF16),
            pltpu.VMEM((HEADS, 8, KEYS), F32),
            pltpu.VMEM((2, DP, TOK, HEAD), BF16),
            pltpu.VMEM((2, DP, TOK, HEAD), BF16),
            pltpu.VMEM((2, HEAD, DP * TOK), BF16),
            pltpu.VMEM((2, 4, 4, 2, HEAD // 2, HEAD), BF16),
            pltpu.VMEM((2, 2, 4, 4, HEAD // 2, HEAD), BF16),
            pltpu.VMEM((2, 2, 4, HEAD // 2, HEAD), BF16),
            pltpu.VMEM((2, 2, 4, 4, HEAD // 2, HEAD), BF16),
            pltpu.VMEM((2, 4, 4, 2, HEAD // 2, HEAD), BF16),
            pltpu.VMEM((DP, HEADS, BUCKETS), F32),
            pltpu.VMEM((4, HEADS, BUCKETS), F32),
            pltpu.VMEM((4, HEADS, BUCKETS), F32),
        ]
        + [dma((n,)) for n in sem_sizes],
        compiler_params=pltpu.CompilerParams(collective_id=0, has_side_effects=True, vmem_limit_bytes=60 * 1024 * 1024),
        name="layer",
    )(actions, cotangent, cache, length, buckets, new_bucket, ln_gain, norm_gain, w_frozen, w_query, w_out, rab)


ADAM_ROWS = 1024


def adam_kernel(
    grad, weight, moment_one, moment_two, table_grad, table, table_one, table_two, done,
    weight_new, one_new, two_new, table_new, table_one_new, table_two_new, result,
):
    updated = adam_update(weight[...], moment_one[...], moment_two[...], grad[...].astype(F32))
    weight_new[...], one_new[...], two_new[...] = updated
    result[...] = done[...]

    @pl.when(pl.program_id(0) == 0)
    def _():
        updated = adam_update(table[...], table_one[...], table_two[...], table_grad[...])
        table_new[...], table_one_new[...], table_two_new[...] = updated


def adam(grad, weight, moment_one, moment_two, table_grad, table, table_one, table_two, done):
    steps = WIDTH // ADAM_ROWS
    rows = pl.BlockSpec((ADAM_ROWS, COLS), lambda i: (i, 0))
    small = pl.BlockSpec((HEADS, BUCKETS), lambda i: (0, 0))
    tokens = pl.BlockSpec((TOK // steps, WIDTH), lambda i: (i, 0))
    operands = (grad, weight, moment_one, moment_two, table_grad, table, table_one, table_two, done)
    return pl.pallas_call(
        adam_kernel,
        grid=(steps,),
        out_shape=[jax.ShapeDtypeStruct(a.shape, a.dtype) for a in operands[1:4] + operands[5:]],
        in_specs=[rows] * 4 + [small] * 4 + [tokens],
        out_specs=[rows] * 3 + [small] * 3 + [tokens],
        name="adam",
    )(*operands)


def shards(
    actions, cotangent, cache_kv, cache_len, cache_bucket, new_bucket, ln_gain, norm_gain,
    w_frozen, w_query, query_m, query_v, w_out, rab_table, rab_m, rab_v,
):
    result, grad_sum, grad_table = layer(
        actions.reshape(TOK, WIDTH),
        cotangent.reshape(TOK, WIDTH),
        cache_kv.reshape(2, HIST, SLAB, WIDTH),
        cache_len.reshape(1, 1),
        cache_bucket,
        new_bucket.reshape(1, TOK),
        ln_gain.reshape(1, WIDTH),
        norm_gain.reshape(1, WIDTH),
        w_frozen,
        w_query,
        w_out.reshape(2, 4, 4, 2, 32, COLS),
        rab_table,
    )
    query_new, query_m_new, query_v_new, rab_new, rab_m_new, rab_v_new, result = adam(
        grad_sum.reshape(WIDTH, COLS), w_query, query_m, query_v, grad_table, rab_table, rab_m, rab_v, result
    )
    return (result.reshape(actions.shape), query_new, query_m_new, query_v_new, rab_new, rab_m_new, rab_v_new)


def solution(mesh):
    placed = (
        P("history", "dp", None, None),
        P("history", "dp", None, None),
        P(None, None, "dp", "history", None),
        P("history", "dp"),
        P(None, "dp", "history"),
        P("history", "dp", None),
        P(),
        P(),
        P(None, None, "dp"),
        P(None, "dp"),
        P(None, "dp"),
        P(None, "dp"),
        P(None, "dp"),
        P(),
        P(),
        P(),
    )
    return jax.shard_map(
        shards,
        mesh=mesh,
        in_specs=placed,
        out_specs=(
            P("history", "dp", None, None),
            P(None, "dp"),
            P(None, "dp"),
            P(None, "dp"),
            P(),
            P(),
            P(),
        ),
        check_vma=False,
    )
```

```python
import functools

import jax
import jax.numpy as jnp
from jax import lax
from jax.experimental import pallas as pl
from jax.experimental.pallas import tpu as pltpu
from jax.sharding import PartitionSpec as P

BETA_ONE = 0.9
BETA_TWO = 0.95
LEARN_RATE = 0.001
ADAM_EPS = 1e-08
NORM_EPS = 1e-05

MESH = pl.DeviceIdType.MESH
F32 = jnp.float32
BF16 = jnp.bfloat16

TOK = 128
WIDTH = 2048
COLS = 256
HEAD = 128
HEADS = 16
BUCKETS = 128
HIST = 16
DP = 8
SLAB = 32
CACHED = HIST * SLAB
KEYS = CACHED + TOK
SCALE = HEAD ** (-0.5)
KV_COPIES = 4 * (HIST - 1) + 1
KV_HALF = 2 * (HIST - 1) + 1
LINK_ORDER = (1, 4, 3, 12, 2, 8, 5, 15, 7, 13, 6, 9, 14, 11, 10)


def adam_update(weight, moment_one, moment_two, gradient):
    first_new = BETA_ONE * moment_one + (1.0 - BETA_ONE) * gradient
    second_new = BETA_TWO * moment_two + (1.0 - BETA_TWO) * gradient * gradient
    stepped = weight.astype(F32) - LEARN_RATE * first_new / (jnp.sqrt(second_new) + ADAM_EPS)
    return (stepped.astype(weight.dtype), first_new, second_new)


def dot_nn(a, b):
    return jnp.dot(a, b, preferred_element_type=F32)


def dot_nt(a, b):
    return lax.dot_general(a, b, (((1,), (1,)), ((), ())), preferred_element_type=F32)


def three_parts(values):
    first = values.astype(BF16)
    rest = values - first.astype(F32)
    second = rest.astype(BF16)
    third = (rest - second.astype(F32)).astype(BF16)
    return first, second, third


def silu_slope(values):
    sigmoid = 0.5 * jnp.tanh(0.5 * values) + 0.5
    return sigmoid * (1.0 + values * (1.0 - sigmoid))


def kernel(
    act_hbm, cot_hbm, cache_hbm, length, buckets, new_bucket, ln_gain, norm_gain, frozen_hbm, query_hbm, wout_hbm, rab,
    out_ref, gsum_hbm, gtab_ref,
    act, cot, wts, rows, pre_slope, sent, proj, kv, bk_out, bks, onehot, bias, att, slope, wout, grad_gated, gate_scaled, inverse_std, gated, grad_att,
    tsum, gq_out, gq_in, grad_pre_t, rs_out, r1_in, r2_out, r2_in, ag_buf, tab_one, tab_two, tab_three,
    loc_sem, kv_s, kv_r, bk_s, bk_r, g_s, g_r, pj_s, pj_r, w_s, w_r, px_s, px_r, p1_s, p1_r, p2_s, p2_r, p3_s, p3_r, gq_s, gq_r, r1_s, r1_r, r2_s, r2_r, a2_s, a2_r, t1_s, t1_r, t2_s, t2_r, t3_s, t3_r,
):
    h = lax.axis_index("history")
    d = lax.axis_index("dp")
    z, y = h // 4, lax.rem(h, 4)
    x, c = d // 2, lax.rem(d, 2)

    def hist(k):
        return lax.rem(z + k // 4, 4) * 4 + lax.rem(y + lax.rem(k, 4), 4)

    def dpx(kx, kc):
        return lax.rem(x + kx, 4) * 2 + lax.rem(c + kc, 2)

    def dpo(k):
        return lax.rem(x + k // 2, 4) * 2 + lax.rem(c + lax.rem(k, 2), 2)

    barrier = pltpu.get_barrier_semaphore()

    def greet_hist(k, carry):
        pl.semaphore_signal(barrier, inc=1, device_id=(hist(k), d), device_id_type=MESH)
        return carry

    def greet_dp(k, carry):
        pl.semaphore_signal(barrier, inc=1, device_id=(h, dpo(k)), device_id_type=MESH)
        return carry

    lax.fori_loop(1, DP, greet_dp, 0)
    lax.fori_loop(1, HIST, greet_hist, 0)

    load_act = pltpu.make_async_copy(act_hbm, act, loc_sem.at[0])
    load_act.start()
    load_query = pltpu.make_async_copy(query_hbm, wts.at[0], loc_sem.at[1])
    load_query.start()
    load_frozen = pltpu.make_async_copy(frozen_hbm, wts.at[pl.ds(1, 3)], loc_sem.at[2])
    load_frozen.start()
    load_cot = pltpu.make_async_copy(cot_hbm, cot, loc_sem.at[3])
    load_cot.start()
    load_wout = pltpu.make_async_copy(wout_hbm, wout.at[d], loc_sem.at[4])
    load_wout.start()
    own_slab = kv.at[:, pl.ds(pl.multiple_of(h * SLAB, SLAB), SLAB), :]
    load_kv = pltpu.make_async_copy(cache_hbm.at[:, h], own_slab, loc_sem.at[5])
    load_kv.start()
    lane = lax.broadcasted_iota(jnp.int32, (HIST, TOK), 1)
    placed = jnp.where(lane // SLAB == y, jnp.concatenate([buckets[:, 0, :]] * 4, axis=1), 0)
    for u in range(HIST):
        bk_out[u] = jnp.broadcast_to(placed[u : u + 1, :], (8, TOK))

    def run(copy, stop, what, *half):
        def step(k, carry):
            getattr(copy(*half, k), what)()
            return carry

        lax.fori_loop(1, stop, step, 0)

    load_act.wait()

    def norm_rows(r, carry):
        part = pl.ds(pl.multiple_of(r * 16, 16), 16)
        values = act[part, :].astype(F32)
        center = values - jnp.mean(values, axis=-1, keepdims=True)
        inverse = lax.rsqrt(jnp.mean(center * center, axis=-1, keepdims=True) + NORM_EPS)
        rows[d, part, :] = (center * inverse * ln_gain[...]).astype(BF16)
        return carry

    lax.fori_loop(0, TOK // 16, norm_rows, 0)
    pl.semaphore_wait(barrier, HIST - 1 + DP - 1)

    def remote(src, dst, send, recv, device):
        return pltpu.make_async_remote_copy(
            src_ref=src, dst_ref=dst, send_sem=send, recv_sem=recv, device_id=device, device_id_type=MESH
        )

    def ring_gather(block, half, own, send, recv, first=0):
        right, left, sibling = (h, dpx(1, 0)), (h, dpx(3, 0)), (h, dpx(0, 1))
        from_left, from_right, far = dpx(3, 0), dpx(1, 0), dpx(2, 0)
        specs = [
            (own, block(d), sibling),
            (own, block(d), right),
            (own, block(d), left),
            (half(from_left, 0), half(from_left, 0), right),
            (half(from_right, 1), half(from_right, 1), left),
            (block(from_left), block(from_left), sibling),
            (block(from_right), block(from_right), sibling),
            (half(far, 0), half(far, 0), sibling),
            (half(far, 1), half(far, 1), sibling),
        ]
        numbered = list(enumerate(specs))[first:]
        return {i: remote(s, t, send.at[i], recv.at[i], dev) for i, (s, t, dev) in numbered}

    ring = ring_gather(
        lambda i: rows.at[i],
        lambda i, k: rows.at[i, pl.ds(k * (TOK // 2), TOK // 2)],
        rows.at[d],
        g_s,
        g_r,
    )
    for i in (1, 2, 0):
        ring[i].start()

    def kv_copy(i):
        piece, turn = divmod(i - 1, HIST - 1)
        to = hist(LINK_ORDER[turn])
        part, low = piece % 2, piece // 2 * 16
        src = cache_hbm.at[part, to, pl.ds(low, 16)]
        dst = kv.at[part, pl.ds(pl.multiple_of(h * SLAB + low, 16), 16), :]
        return remote(src, dst, kv_s.at[i], kv_r.at[i], (to, d))

    def bk_copy(k):
        to = hist(k)
        return remote(bk_out.at[to], bks.at[h], bk_s.at[k], bk_r.at[k], (to, d))

    def plane_x(k):
        return remote(wout_hbm.at[0, z, y], wout.at[d, 0, z, y], px_s.at[k], px_r.at[k], (h, dpx(k, 0)))

    def plane_one(k, kx):
        slot, i = dpx(kx, 0), 3 * (k - 1) + kx - 1
        over_z, over_y = wout.at[slot, 0, z, y, 0], wout.at[slot, 0, z, y, 1]
        to_z, to_y = lax.rem(z + k, 4) * 4 + y, z * 4 + lax.rem(y + k, 4)
        return (
            remote(over_z, over_z, p1_s.at[i], p1_r.at[i], (to_z, d)),
            remote(over_y, over_y, p1_s.at[9 + i], p1_r.at[9 + i], (to_y, d)),
        )

    def plane_two(k, kx):
        slot, i = dpx(kx, 0), 3 * (k - 1) + kx - 1
        over_y, over_z = wout.at[slot, 0, :, y, 0], wout.at[slot, 0, z, :, 1]
        to_z, to_y = lax.rem(z + k, 4) * 4 + y, z * 4 + lax.rem(y + k, 4)
        return (
            remote(over_y, over_y, p2_s.at[i], p2_r.at[i], (to_y, d)),
            remote(over_z, over_z, p2_s.at[9 + i], p2_r.at[9 + i], (to_z, d)),
        )

    def plane_share(kx):
        block = wout.at[dpx(kx, 0), 0]
        return remote(block, block, p3_s.at[kx], p3_r.at[kx], (h, dpx(0, 1)))

    own_wout = remote(wout_hbm, wout.at[d], p3_s.at[0], p3_r.at[0], (h, dpx(0, 1)))
    wring = ring_gather(
        lambda i: wout.at[i, 1],
        lambda i, k: wout.at[i, 1, pl.ds(2 * k, 2)],
        wout_hbm.at[1],
        w_s,
        w_r,
        first=1,
    )
    plane_steps = [(k, kx) for k in (1, 3, 2) for kx in (1, 2, 3)]
    for k in range(1, 4):
        plane_x(k).start()

    def send_bk(k, carry):
        bk_copy(k).start()
        return carry

    lax.fori_loop(1, HIST, send_bk, 0)
    for i in range(1, KV_HALF):
        kv_copy(i).start()

    def project(chip):
        part = pl.ds(pl.multiple_of(chip * 2, 2), 2)
        chip_rows = rows[part].reshape(2 * TOK, WIDTH)
        for j in range(4):
            pre = dot_nn(chip_rows, wts[j])
            sigmoid = 0.5 * jnp.tanh(0.5 * pre) + 0.5
            acted = pre * sigmoid
            if j == 0:
                pre_slope[part] = (sigmoid + acted * (1.0 - sigmoid)).reshape(2, TOK, COLS)
            sent[part, :, pl.ds(j * COLS, COLS)] = acted.astype(BF16).reshape(2, TOK, COLS)

    def pj_copy(k):
        to = dpo(k)
        return remote(sent.at[to], proj.at[d], pj_s.at[k], pj_r.at[k], (h, to))

    load_query.wait()
    load_frozen.wait()
    ring[0].wait_recv()
    project(x)
    pj_copy(1).start()
    own_proj = pltpu.make_async_copy(sent.at[d], proj.at[d], loc_sem.at[7])
    own_proj.start()
    for k in range(1, 4):
        plane_x(k).wait_recv()
    for step in plane_steps:
        for copy in plane_one(*step):
            copy.start()
    for i in range(KV_HALF, KV_COPIES):
        kv_copy(i).start()
    ring[1].wait_recv()
    ring[3].start()
    ring[5].start()
    ring[2].wait_recv()
    ring[4].start()
    ring[6].start()
    ring[5].wait_recv()
    project(lax.rem(x + 3, 4))
    pj_copy(6).start()
    pj_copy(7).start()
    ring[6].wait_recv()
    project(lax.rem(x + 1, 4))
    pj_copy(2).start()
    pj_copy(3).start()
    for i in (1, 2):
        wring[i].start()
    own_wout.start()
    ring[3].wait_recv()
    ring[7].start()
    ring[4].wait_recv()
    ring[8].start()
    ring[7].wait_recv()
    ring[8].wait_recv()
    project(lax.rem(x + 2, 4))
    pj_copy(4).start()
    pj_copy(5).start()

    for step in plane_steps:
        for copy in plane_one(*step):
            copy.wait_recv()
    for step in plane_steps:
        for copy in plane_two(*step):
            copy.start()

    bks[h] = bk_out[h]

    def wait_bk(k, carry):
        bk_copy(k).wait_recv()
        return carry

    lax.fori_loop(1, HIST, wait_bk, 0)
    levels = lax.broadcasted_iota(jnp.int32, (BUCKETS, TOK), 0)
    for q in range(4):
        ids = (bks[4 * q] + bks[4 * q + 1] + bks[4 * q + 2] + bks[4 * q + 3])[0:1, :]
        onehot[:, pl.ds(q * TOK, TOK)] = jnp.where(levels == ids, 1.0, 0.0).astype(BF16)
    onehot[:, pl.ds(CACHED, TOK)] = jnp.where(levels == new_bucket[...], 1.0, 0.0).astype(BF16)
    hot = onehot[...]
    bias_sum = jnp.zeros((HEADS, KEYS), F32)
    for term in reversed(three_parts(rab[...])):
        bias_sum = bias_sum + dot_nn(term, hot)
    bias[...] = bias_sum

    count = length[0, 0]
    share = 1.0 / jnp.full((1, TOK), count + TOK, jnp.int32).astype(F32)
    cached_pos = lax.broadcasted_iota(jnp.int32, (1, CACHED), 1)
    share_cached = jnp.where(cached_pos < count, jnp.concatenate([share] * 4, axis=1), 0.0)
    row_pos = lax.broadcasted_iota(jnp.int32, (TOK, TOK), 0)
    col_pos = lax.broadcasted_iota(jnp.int32, (TOK, TOK), 1)
    share_new = jnp.where(col_pos <= row_pos, jnp.broadcast_to(share, (TOK, TOK)), 0.0)

    for i in (1, 2):
        wring[i].wait_recv()
        wring[i + 2].start()
        wring[i + 4].start()

    def wait_pj(k, carry):
        pj_copy(k).wait_recv()
        return carry

    own_proj.wait()
    lax.fori_loop(1, DP, wait_pj, 0)

    load_kv.wait()
    for i in range(1, KV_COPIES):
        kv_copy(i).wait_recv()

    def attend(m, carry):
        for k in range(2):
            head = m * 2 + k
            lanes = pl.ds(pl.multiple_of(head * HEAD, HEAD), HEAD)
            query = proj[m, :, pl.ds(k * HEAD, HEAD)]
            value_new = proj[m, :, pl.ds(2 * COLS + k * HEAD, HEAD)]
            key_new = proj[m, :, pl.ds(3 * COLS + k * HEAD, HEAD)]
            key_bias = bias[pl.ds(head, 1), :]
            total = jnp.zeros((TOK, HEAD), F32)
            parts = (
                (kv[0, :, lanes], kv[1, :, lanes], pl.ds(0, CACHED), key_bias[:, :CACHED], share_cached),
                (key_new, value_new, pl.ds(CACHED, TOK), key_bias[:, CACHED:], share_new),
            )
            for keys, values, where, bias_part, share_part in parts:
                score = dot_nt(query, keys) * SCALE + bias_part
                sigmoid = 0.5 * jnp.tanh(0.5 * score) + 0.5
                weight = score * sigmoid * share_part
                slope[head, :, where] = sigmoid * share_part + weight * (1.0 - sigmoid)
                total = total + dot_nn(weight.astype(BF16), values)
            att[:, lanes] = total
        return carry

    lax.fori_loop(0, DP, attend, 0)

    def stat_rows(r, carry):
        part = pl.ds(pl.multiple_of(r * 16, 16), 16)
        values = att[part, :]
        center = values - jnp.mean(values, axis=-1, keepdims=True)
        inverse = lax.rsqrt(jnp.mean(center * center, axis=-1, keepdims=True) + NORM_EPS)
        nhat = center * inverse
        gate = jnp.concatenate([proj[m, part, pl.ds(COLS, COLS)] for m in range(DP)], axis=1).astype(F32)
        scaled = gate * norm_gain[...]
        att[part, :] = nhat
        gate_scaled[part, :] = scaled
        gated[part, :] = (nhat * scaled).astype(BF16)
        inverse_std[part, :] = jnp.broadcast_to(inverse, (16, TOK))
        return carry

    lax.fori_loop(0, TOK // 16, stat_rows, 0)

    load_cot.wait()
    load_wout.wait()

    def gated_part(m, half, first=False):
        lanes = pl.ds(pl.multiple_of(m * COLS, COLS), COLS)
        for n in range(2):
            cols = pl.ds(half * 1024 + n * 512, 512)
            part = dot_nt(cot[:, lanes], wout[m, half, pl.ds(2 * n, 2)].reshape(512, COLS))
            grad_gated[:, cols] = part if first else grad_gated[:, cols] + part

    run(bk_copy, HIST, "wait_send")
    run(pj_copy, DP, "wait_send")
    for i in range(1, KV_COPIES):
        kv_copy(i).wait_send()
    for copy in ring.values():
        copy.wait_send()
    for k in range(1, 4):
        plane_x(k).wait_send()
    for step in plane_steps:
        for copy in plane_one(*step):
            copy.wait_send()

    for step in plane_steps:
        for copy in plane_two(*step):
            copy.wait_recv()
    for k in range(1, 4):
        plane_share(k).start()
    gated_part(d, 0, True)
    gated_part(d, 1, True)
    own_wout.wait_recv()
    gated_part(dpx(0, 1), 0)
    gated_part(dpx(0, 1), 1)
    gated_part(dpx(3, 0), 1)
    gated_part(dpx(1, 0), 1)
    for i in (3, 4):
        wring[i].wait_recv()
        wring[i + 4].start()
    for k in (3, 1, 2):
        gated_part(dpx(k, 0), 0)
    for k in (3, 1, 2):
        plane_share(k).wait_recv()
        gated_part(dpx(k, 1), 0)
    wring[5].wait_recv()
    gated_part(dpx(3, 1), 1)
    wring[6].wait_recv()
    gated_part(dpx(1, 1), 1)
    gated_part(dpx(2, 0), 1)
    wring[7].wait_recv()
    wring[8].wait_recv()
    gated_part(dpx(2, 1), 1)

    def gate_rows(r, carry):
        part = pl.ds(pl.multiple_of(r * 16, 16), 16)
        nhat = att[part, :]
        grad_hat = grad_gated[part, :] * gate_scaled[part, :]
        along = jnp.mean(grad_hat * nhat, axis=-1, keepdims=True)
        grad = inverse_std[part, 0:1] * (grad_hat - jnp.mean(grad_hat, axis=-1, keepdims=True) - nhat * along)
        grad_att[part, :] = grad.astype(BF16)
        return carry

    lax.fori_loop(0, TOK // 16, gate_rows, 0)

    def gq_copy(half, k):
        to, i = dpo(k), half * DP + k
        return remote(gq_out.at[half, to], gq_in.at[half, d], gq_s.at[i], gq_r.at[i], (h, to))

    def attend_back(m, k):
        head = m * 2 + k
        lanes = pl.ds(pl.multiple_of(head * HEAD, HEAD), HEAD)
        value_new = proj[m, :, pl.ds(2 * COLS + k * HEAD, HEAD)]
        key_new = proj[m, :, pl.ds(3 * COLS + k * HEAD, HEAD)]
        grad = grad_att[:, lanes]
        total = jnp.zeros((TOK, HEAD), F32)
        parts = (
            (kv[0, :, lanes], kv[1, :, lanes], pl.ds(0, CACHED)),
            (key_new, value_new, pl.ds(CACHED, TOK)),
        )
        for keys, values, where in parts:
            grad_score = dot_nt(grad, values) * slope[head, :, where]
            tsum[head, :, where] = jnp.sum(grad_score.reshape(TOK // 8, 8, -1), axis=0)
            total = total + dot_nn(grad_score.astype(BF16), keys)
        gq_out[k, m] = (total * SCALE).astype(BF16)

    def back_steps(half, first, stop):
        def step(i, carry):
            k = 2 * i + 1
            attend_back(dpo(k), half)
            attend_back(dpo(k + 1), half)
            gq_copy(half, k).start()
            gq_copy(half, k + 1).start()
            return carry

        lax.fori_loop(first, stop, step, 0)

    def own_back(half):
        attend_back(dpo(DP - 1), half)
        attend_back(d, half)
        gq_copy(half, DP - 1).start()
        gq_in[half, d] = gq_out[half, d]

    def weight_half(half):
        run(gq_copy, DP, "wait_recv", half)
        for i in range(DP):
            pre = pre_slope[i, :, pl.ds(half * HEAD, HEAD)]
            grad_pre_t[half, :, pl.ds(i * TOK, TOK)] = (gq_in[half, i].astype(F32) * pre).astype(BF16).T
        for i in range(4):
            piece = dot_nn(grad_pre_t[half], rows[:, :, pl.ds(i * 512, 512)].reshape(DP * TOK, 512)).astype(BF16)
            rs_out[half, i] = piece.T.reshape(4, 2, HEAD // 2, HEAD)
        for k in (1, 3, 2):
            for side in range(2):
                sum_one(half, side, k).start()

    def along(side, k):
        return (lax.rem(z + k, 4), y) if side == 0 else (z, lax.rem(y + k, 4))

    def place(zy):
        return (zy[0] * 4 + zy[1], d)

    def line(ref, half, side, zy):
        return ref.at[half, zy[0], :, side] if side == 0 else ref.at[half, :, zy[1], side]

    def own(side):
        return z if side == 0 else y

    def sems(pair, half, side, k):
        i = (half * 2 + side) * 4 + k
        return pair[0].at[i], pair[1].at[i]

    def sum_one(half, side, k):
        to = along(side, k)
        return remote(line(rs_out, half, side, to), r1_in.at[half, side, own(side)], *sems((r1_s, r1_r), half, side, k), place(to))

    def sum_two(half, side, k):
        src, dst = r2_out.at[half, side], r2_in.at[half, side, own(1 - side)]
        return remote(src, dst, *sems((r2_s, r2_r), half, side, k), place(along(1 - side, k)))

    def gsum_line(half, side):
        lanes = pl.ds(half * HEAD, HEAD)
        return gsum_hbm.at[z, :, side, :, lanes] if side == 0 else gsum_hbm.at[:, y, side, :, lanes]

    def gather_two(half, side, k):
        src = line(ag_buf, half, side, (z, y))
        return remote(src, gsum_line(half, side), *sems((a2_s, a2_r), half, side, k), place(along(side, k)))

    def own_gsum(half, side):
        return pltpu.make_async_copy(line(ag_buf, half, side, (z, y)), gsum_line(half, side), loc_sem.at[8 + half * 2 + side])

    def after_one(half):
        for side in range(2):
            r1_in[half, side, own(side)] = rs_out[half, z, :, 0] if side == 0 else rs_out[half, :, y, 1]
            for k in (1, 3, 2):
                sum_one(half, side, k).wait_recv()
            total = r1_in[half, side, 0].astype(F32)
            for i in range(1, 4):
                total = total + r1_in[half, side, i].astype(F32)
            r2_out[half, side] = total.astype(BF16)
            for k in (1, 3, 2):
                sum_two(half, side, k).start()

    def after_two(half):
        for side in range(2):
            r2_in[half, side, own(1 - side)] = r2_out[half, side]
            for k in (1, 3, 2):
                sum_two(half, side, k).wait_recv()
            total = r2_in[half, side, 0].astype(F32)
            for i in range(1, 4):
                total = total + r2_in[half, side, i].astype(F32)
            if side == 0:
                ag_buf[half, z, :, 0] = total.astype(BF16)
            else:
                ag_buf[half, :, y, 1] = total.astype(BF16)
            for k in (1, 3, 2):
                gather_two(half, side, k).start()
            own_gsum(half, side).start()

    def out_cols(m, carry):
        lanes = pl.ds(pl.multiple_of(m * COLS, COLS), COLS)
        product = dot_nn(gated[...], wout[m].reshape(WIDTH, COLS))
        out_ref[:, lanes] = (product + act[:, lanes].astype(F32)).astype(BF16)
        return carry

    def t1_copy(k):
        return remote(tab_one.at[d], tab_one.at[d], t1_s.at[k], t1_r.at[k], (h, dpo(k)))

    def t2_copy(k):
        return remote(tab_two.at[z], tab_two.at[z], t2_s.at[k], t2_r.at[k], place(along(0, k)))

    def t3_copy(k):
        return remote(tab_three.at[y], tab_three.at[y], t3_s.at[k], t3_r.at[k], place(along(1, k)))

    def table_sum(ref, count):
        total = ref[0]
        for i in range(1, count):
            total = total + ref[i]
        return total

    back_steps(0, 0, 3)
    own_back(0)
    back_steps(1, 0, 2)
    weight_half(0)
    back_steps(1, 2, 3)
    own_back(1)

    table = jnp.zeros((HEADS, BUCKETS), F32)
    for term in reversed(three_parts(jnp.sum(tsum[...], axis=1))):
        table = table + dot_nt(term, hot)
    tab_one[d] = table
    run(t1_copy, DP, "start")

    lax.fori_loop(0, 2, out_cols, 0)
    after_one(0)
    weight_half(1)
    lax.fori_loop(2, 4, out_cols, 0)
    after_two(0)

    run(t1_copy, DP, "wait_recv")
    tab_two[z] = table_sum(tab_one, DP)
    for k in (1, 3, 2):
        t2_copy(k).start()

    after_one(1)
    for k in (1, 3, 2):
        t2_copy(k).wait_recv()
    tab_three[y] = table_sum(tab_two, 4)
    for k in (1, 3, 2):
        t3_copy(k).start()
    lax.fori_loop(4, 6, out_cols, 0)
    after_two(1)
    for copy in [*wring.values(), own_wout]:
        copy.wait_send()
    for k in range(1, 4):
        plane_share(k).wait_send()
    for step in plane_steps:
        for copy in plane_two(*step):
            copy.wait_send()
    lax.fori_loop(6, DP, out_cols, 0)

    for k in (1, 3, 2):
        t3_copy(k).wait_recv()
    gtab_ref[...] = table_sum(tab_three, 4)

    run(t1_copy, DP, "wait_send")
    for k in (1, 3, 2):
        t2_copy(k).wait_send()
        t3_copy(k).wait_send()
    for half in range(2):
        run(gq_copy, DP, "wait_send", half)
        for side in range(2):
            for k in (1, 3, 2):
                for copy in (sum_one, sum_two):
                    copy(half, side, k).wait_send()
                gather_two(half, side, k).wait()
            own_gsum(half, side).wait()


def layer(actions, cotangent, cache, length, buckets, new_bucket, ln_gain, norm_gain, w_frozen, w_query, w_out, rab):
    any_space = pl.BlockSpec(memory_space=pl.ANY)
    vmem = pl.BlockSpec(memory_space=pltpu.VMEM)
    smem = pl.BlockSpec(memory_space=pltpu.SMEM)
    dma = pltpu.SemaphoreType.DMA
    sem_sizes = (12, KV_COPIES, KV_COPIES, HIST, HIST, 9, 9, DP, DP, 9, 9, 4, 4, 18, 18, 18, 18, 4, 4, 2 * DP, 2 * DP, *[16] * 6, DP, DP, 4, 4, 4, 4)
    return pl.pallas_call(
        kernel,
        out_shape=(
            jax.ShapeDtypeStruct((TOK, WIDTH), BF16),
            jax.ShapeDtypeStruct((4, 4, 2, HEAD // 2, COLS), BF16),
            jax.ShapeDtypeStruct((HEADS, BUCKETS), F32),
        ),
        in_specs=[any_space, any_space, any_space, smem, vmem, vmem, vmem, vmem, any_space, any_space, any_space, vmem],
        out_specs=(vmem, any_space, vmem),
        scratch_shapes=[
            pltpu.VMEM((TOK, WIDTH), BF16),
            pltpu.VMEM((TOK, WIDTH), BF16),
            pltpu.VMEM((4, WIDTH, COLS), BF16),
            pltpu.VMEM((DP, TOK, WIDTH), BF16),
            pltpu.VMEM((DP, TOK, COLS), F32),
            pltpu.VMEM((DP, TOK, 4 * COLS), BF16),
            pltpu.VMEM((DP, TOK, 4 * COLS), BF16),
            pltpu.VMEM((2, CACHED, WIDTH), BF16),
            pltpu.VMEM((HIST, 8, TOK), jnp.int32),
        pltpu.VMEM((HIST, 8, TOK), jnp.int32),
            pltpu.VMEM((BUCKETS, KEYS), BF16),
            pltpu.VMEM((HEADS, KEYS), F32),
            pltpu.VMEM((TOK, WIDTH), F32),
            pltpu.VMEM((HEADS, TOK, KEYS), F32),
            pltpu.VMEM((DP, 2, 4, 4, 2, 32, COLS), BF16),
            pltpu.VMEM((TOK, WIDTH), F32),
            pltpu.VMEM((TOK, WIDTH), F32),
            pltpu.VMEM((TOK, TOK), F32),
            pltpu.VMEM((TOK, WIDTH), BF16),
            pltpu.VMEM((TOK, WIDTH), BF16),
            pltpu.VMEM((HEADS, 8, KEYS), F32),
            pltpu.VMEM((2, DP, TOK, HEAD), BF16),
            pltpu.VMEM((2, DP, TOK, HEAD), BF16),
            pltpu.VMEM((2, HEAD, DP * TOK), BF16),
            pltpu.VMEM((2, 4, 4, 2, HEAD // 2, HEAD), BF16),
            pltpu.VMEM((2, 2, 4, 4, HEAD // 2, HEAD), BF16),
            pltpu.VMEM((2, 2, 4, HEAD // 2, HEAD), BF16),
            pltpu.VMEM((2, 2, 4, 4, HEAD // 2, HEAD), BF16),
            pltpu.VMEM((2, 4, 4, 2, HEAD // 2, HEAD), BF16),
            pltpu.VMEM((DP, HEADS, BUCKETS), F32),
            pltpu.VMEM((4, HEADS, BUCKETS), F32),
            pltpu.VMEM((4, HEADS, BUCKETS), F32),
        ]
        + [dma((n,)) for n in sem_sizes],
        compiler_params=pltpu.CompilerParams(collective_id=0, has_side_effects=True, vmem_limit_bytes=60 * 1024 * 1024),
        name="layer",
    )(actions, cotangent, cache, length, buckets, new_bucket, ln_gain, norm_gain, w_frozen, w_query, w_out, rab)


ADAM_ROWS = 1024


def adam_kernel(
    grad, weight, moment_one, moment_two, table_grad, table, table_one, table_two, done,
    weight_new, one_new, two_new, table_new, table_one_new, table_two_new, result,
):
    gradient = grad[...].astype(F32)
    first = BETA_ONE * moment_one[...] + (1.0 - BETA_ONE) * gradient
    second = BETA_TWO * moment_two[...] + (1.0 - BETA_TWO) * gradient * gradient
    one_new[...] = first
    two_new[...] = second
    root = second * lax.rsqrt(second)
    stepped = weight[...].astype(F32) - LEARN_RATE * first * pl.reciprocal(root + ADAM_EPS)
    weight_new[...] = stepped.astype(BF16)
    result[...] = done[...]

    @pl.when(pl.program_id(0) == 0)
    def _():
        updated = adam_update(table[...], table_one[...], table_two[...], table_grad[...])
        table_new[...], table_one_new[...], table_two_new[...] = updated


def adam(grad, weight, moment_one, moment_two, table_grad, table, table_one, table_two, done):
    steps = WIDTH // ADAM_ROWS
    rows = pl.BlockSpec((ADAM_ROWS, COLS), lambda i: (i, 0))
    small = pl.BlockSpec((HEADS, BUCKETS), lambda i: (0, 0))
    tokens = pl.BlockSpec((TOK // steps, WIDTH), lambda i: (i, 0))
    operands = (grad, weight, moment_one, moment_two, table_grad, table, table_one, table_two, done)
    return pl.pallas_call(
        adam_kernel,
        grid=(steps,),
        out_shape=[jax.ShapeDtypeStruct(a.shape, a.dtype) for a in operands[1:4] + operands[5:]],
        in_specs=[rows] * 4 + [small] * 4 + [tokens],
        out_specs=[rows] * 3 + [small] * 3 + [tokens],
        name="adam",
    )(*operands)


def shards(
    actions, cotangent, cache_kv, cache_len, cache_bucket, new_bucket, ln_gain, norm_gain,
    w_frozen, w_query, query_m, query_v, w_out, rab_table, rab_m, rab_v,
):
    result, grad_sum, grad_table = layer(
        actions.reshape(TOK, WIDTH),
        cotangent.reshape(TOK, WIDTH),
        cache_kv.reshape(2, HIST, SLAB, WIDTH),
        cache_len.reshape(1, 1),
        cache_bucket,
        new_bucket.reshape(1, TOK),
        ln_gain.reshape(1, WIDTH),
        norm_gain.reshape(1, WIDTH),
        w_frozen,
        w_query,
        w_out.reshape(2, 4, 4, 2, 32, COLS),
        rab_table,
    )
    query_new, query_m_new, query_v_new, rab_new, rab_m_new, rab_v_new, result = adam(
        grad_sum.reshape(WIDTH, COLS), w_query, query_m, query_v, grad_table, rab_table, rab_m, rab_v, result
    )
    return (result.reshape(actions.shape), query_new, query_m_new, query_v_new, rab_new, rab_m_new, rab_v_new)


def solution(mesh):
    placed = (
        P("history", "dp", None, None),
        P("history", "dp", None, None),
        P(None, None, "dp", "history", None),
        P("history", "dp"),
        P(None, "dp", "history"),
        P("history", "dp", None),
        P(),
        P(),
        P(None, None, "dp"),
        P(None, "dp"),
        P(None, "dp"),
        P(None, "dp"),
        P(None, "dp"),
        P(),
        P(),
        P(),
    )
    return jax.shard_map(
        shards,
        mesh=mesh,
        in_specs=placed,
        out_specs=(
            P("history", "dp", None, None),
            P(None, "dp"),
            P(None, "dp"),
            P(None, "dp"),
            P(),
            P(),
            P(),
        ),
        check_vma=False,
    )
```

```python
import functools

import jax
import jax.numpy as jnp
from jax import lax
from jax.experimental import pallas as pl
from jax.experimental.pallas import tpu as pltpu
from jax.sharding import PartitionSpec as P

BETA_ONE = 0.9
BETA_TWO = 0.95
LEARN_RATE = 0.001
ADAM_EPS = 1e-08
NORM_EPS = 1e-05

MESH = pl.DeviceIdType.MESH
F32 = jnp.float32
BF16 = jnp.bfloat16

TOK = 128
WIDTH = 2048
COLS = 256
HEAD = 128
HEADS = 16
BUCKETS = 128
HIST = 16
DP = 8
SLAB = 32
CACHED = HIST * SLAB
KEYS = CACHED + TOK
SCALE = HEAD ** (-0.5)
KV_COPIES = 4 * (HIST - 1) + 1
KV_HALF = 2 * (HIST - 1) + 1
LINK_ORDER = (1, 4, 3, 12, 2, 8, 5, 15, 7, 13, 6, 9, 14, 11, 10)


def adam_update(weight, moment_one, moment_two, gradient):
    first_new = BETA_ONE * moment_one + (1.0 - BETA_ONE) * gradient
    second_new = BETA_TWO * moment_two + (1.0 - BETA_TWO) * gradient * gradient
    stepped = weight.astype(F32) - LEARN_RATE * first_new / (jnp.sqrt(second_new) + ADAM_EPS)
    return (stepped.astype(weight.dtype), first_new, second_new)


def dot_nn(a, b):
    return jnp.dot(a, b, preferred_element_type=F32)


def dot_nt(a, b):
    return lax.dot_general(a, b, (((1,), (1,)), ((), ())), preferred_element_type=F32)


def three_parts(values):
    first = values.astype(BF16)
    rest = values - first.astype(F32)
    second = rest.astype(BF16)
    third = (rest - second.astype(F32)).astype(BF16)
    return first, second, third


def silu_slope(values):
    sigmoid = 0.5 * jnp.tanh(0.5 * values) + 0.5
    return sigmoid * (1.0 + values * (1.0 - sigmoid))


def kernel(
    act_hbm, cot_hbm, cache_hbm, length, buckets, new_bucket, ln_gain, norm_gain, frozen_hbm, query_hbm, wout_hbm, rab,
    out_ref, gsum_hbm, gtab_ref,
    act, cot, wts, rows, pre_slope, sent, proj, kv, bk_out, bks, onehot, bias, att, slope, wout, grad_gated, gate_scaled, inverse_std, gated, grad_att,
    tsum, gq_out, gq_in, grad_pre_t, rs_out, r1_in, r2_out, r2_in, ag_buf, tab_one, tab_two, tab_three,
    loc_sem, kv_s, kv_r, bk_s, bk_r, g_s, g_r, pj_s, pj_r, w_s, w_r, px_s, px_r, p1_s, p1_r, p2_s, p2_r, p3_s, p3_r, gq_s, gq_r, r1_s, r1_r, r2_s, r2_r, a2_s, a2_r, t1_s, t1_r, t2_s, t2_r, t3_s, t3_r,
):
    h = lax.axis_index("history")
    d = lax.axis_index("dp")
    z, y = h // 4, lax.rem(h, 4)
    x, c = d // 2, lax.rem(d, 2)

    def hist(k):
        return lax.rem(z + k // 4, 4) * 4 + lax.rem(y + lax.rem(k, 4), 4)

    def dpx(kx, kc):
        return lax.rem(x + kx, 4) * 2 + lax.rem(c + kc, 2)

    def dpo(k):
        return lax.rem(x + k // 2, 4) * 2 + lax.rem(c + lax.rem(k, 2), 2)

    barrier = pltpu.get_barrier_semaphore()

    def greet_hist(k, carry):
        pl.semaphore_signal(barrier, inc=1, device_id=(hist(k), d), device_id_type=MESH)
        return carry

    def greet_dp(k, carry):
        pl.semaphore_signal(barrier, inc=1, device_id=(h, dpo(k)), device_id_type=MESH)
        return carry

    lax.fori_loop(1, DP, greet_dp, 0)
    lax.fori_loop(1, HIST, greet_hist, 0)

    load_act = pltpu.make_async_copy(act_hbm, act, loc_sem.at[0])
    load_act.start()
    load_query = pltpu.make_async_copy(query_hbm, wts.at[0], loc_sem.at[1])
    load_query.start()
    load_frozen = pltpu.make_async_copy(frozen_hbm, wts.at[pl.ds(1, 3)], loc_sem.at[2])
    load_frozen.start()
    load_cot = pltpu.make_async_copy(cot_hbm, cot, loc_sem.at[3])
    load_cot.start()
    load_wout = pltpu.make_async_copy(wout_hbm, wout.at[d], loc_sem.at[4])
    load_wout.start()
    own_slab = kv.at[:, pl.ds(pl.multiple_of(h * SLAB, SLAB), SLAB), :]
    load_kv = pltpu.make_async_copy(cache_hbm.at[:, h], own_slab, loc_sem.at[5])
    load_kv.start()
    lane = lax.broadcasted_iota(jnp.int32, (HIST, TOK), 1)
    placed = jnp.where(lane // SLAB == y, jnp.concatenate([buckets[:, 0, :]] * 4, axis=1), 0)
    for u in range(HIST):
        bk_out[u] = jnp.broadcast_to(placed[u : u + 1, :], (8, TOK))

    def run(copy, stop, what, *half):
        def step(k, carry):
            getattr(copy(*half, k), what)()
            return carry

        lax.fori_loop(1, stop, step, 0)

    load_act.wait()

    def norm_rows(r, carry):
        part = pl.ds(pl.multiple_of(r * 16, 16), 16)
        values = act[part, :].astype(F32)
        center = values - jnp.mean(values, axis=-1, keepdims=True)
        inverse = lax.rsqrt(jnp.mean(center * center, axis=-1, keepdims=True) + NORM_EPS)
        rows[d, part, :] = (center * inverse * ln_gain[...]).astype(BF16)
        return carry

    lax.fori_loop(0, TOK // 16, norm_rows, 0)
    pl.semaphore_wait(barrier, HIST - 1 + DP - 1)

    def remote(src, dst, send, recv, device):
        return pltpu.make_async_remote_copy(
            src_ref=src, dst_ref=dst, send_sem=send, recv_sem=recv, device_id=device, device_id_type=MESH
        )

    def ring_gather(block, half, own, send, recv, first=0):
        right, left, sibling = (h, dpx(1, 0)), (h, dpx(3, 0)), (h, dpx(0, 1))
        from_left, from_right, far = dpx(3, 0), dpx(1, 0), dpx(2, 0)
        specs = [
            (own, block(d), sibling),
            (own, block(d), right),
            (own, block(d), left),
            (half(from_left, 0), half(from_left, 0), right),
            (half(from_right, 1), half(from_right, 1), left),
            (block(from_left), block(from_left), sibling),
            (block(from_right), block(from_right), sibling),
            (half(far, 0), half(far, 0), sibling),
            (half(far, 1), half(far, 1), sibling),
        ]
        numbered = list(enumerate(specs))[first:]
        return {i: remote(s, t, send.at[i], recv.at[i], dev) for i, (s, t, dev) in numbered}

    ring = ring_gather(
        lambda i: rows.at[i],
        lambda i, k: rows.at[i, pl.ds(k * (TOK // 2), TOK // 2)],
        rows.at[d],
        g_s,
        g_r,
    )
    for i in (1, 2, 0):
        ring[i].start()

    def kv_copy(i):
        piece, turn = divmod(i - 1, HIST - 1)
        to = hist(LINK_ORDER[turn])
        part, low = piece % 2, piece // 2 * 16
        src = cache_hbm.at[part, to, pl.ds(low, 16)]
        dst = kv.at[part, pl.ds(pl.multiple_of(h * SLAB + low, 16), 16), :]
        return remote(src, dst, kv_s.at[i], kv_r.at[i], (to, d))

    def bk_copy(k):
        to = hist(k)
        return remote(bk_out.at[to], bks.at[h], bk_s.at[k], bk_r.at[k], (to, d))

    def plane_x(k):
        return remote(wout_hbm.at[0, z, y], wout.at[d, 0, z, y], px_s.at[k], px_r.at[k], (h, dpx(k, 0)))

    def plane_one(k, kx):
        slot, i = dpx(kx, 0), 3 * (k - 1) + kx - 1
        over_z, over_y = wout.at[slot, 0, z, y, 0], wout.at[slot, 0, z, y, 1]
        to_z, to_y = lax.rem(z + k, 4) * 4 + y, z * 4 + lax.rem(y + k, 4)
        return (
            remote(over_z, over_z, p1_s.at[i], p1_r.at[i], (to_z, d)),
            remote(over_y, over_y, p1_s.at[9 + i], p1_r.at[9 + i], (to_y, d)),
        )

    def plane_two(k, kx):
        slot, i = dpx(kx, 0), 3 * (k - 1) + kx - 1
        over_y, over_z = wout.at[slot, 0, :, y, 0], wout.at[slot, 0, z, :, 1]
        to_z, to_y = lax.rem(z + k, 4) * 4 + y, z * 4 + lax.rem(y + k, 4)
        return (
            remote(over_y, over_y, p2_s.at[i], p2_r.at[i], (to_y, d)),
            remote(over_z, over_z, p2_s.at[9 + i], p2_r.at[9 + i], (to_z, d)),
        )

    def plane_share(kx):
        block = wout.at[dpx(kx, 0), 0]
        return remote(block, block, p3_s.at[kx], p3_r.at[kx], (h, dpx(0, 1)))

    own_wout = remote(wout_hbm, wout.at[d], p3_s.at[0], p3_r.at[0], (h, dpx(0, 1)))
    wring = ring_gather(
        lambda i: wout.at[i, 1],
        lambda i, k: wout.at[i, 1, pl.ds(2 * k, 2)],
        wout_hbm.at[1],
        w_s,
        w_r,
        first=1,
    )
    plane_steps = [(k, kx) for k in (1, 3, 2) for kx in (1, 2, 3)]
    for k in range(1, 4):
        plane_x(k).start()

    def send_bk(k, carry):
        bk_copy(k).start()
        return carry

    lax.fori_loop(1, HIST, send_bk, 0)
    for i in range(1, KV_HALF):
        kv_copy(i).start()

    def project(chip):
        part = pl.ds(pl.multiple_of(chip * 2, 2), 2)
        chip_rows = rows[part].reshape(2 * TOK, WIDTH)
        for j in range(4):
            pre = dot_nn(chip_rows, wts[j])
            sigmoid = 0.5 * jnp.tanh(0.5 * pre) + 0.5
            acted = pre * sigmoid
            if j == 0:
                pre_slope[part] = (sigmoid + acted * (1.0 - sigmoid)).reshape(2, TOK, COLS)
            sent[part, :, pl.ds(j * COLS, COLS)] = acted.astype(BF16).reshape(2, TOK, COLS)

    def pj_copy(k):
        to = dpo(k)
        return remote(sent.at[to], proj.at[d], pj_s.at[k], pj_r.at[k], (h, to))

    load_query.wait()
    load_frozen.wait()
    ring[0].wait_recv()
    project(x)
    pj_copy(1).start()
    own_proj = pltpu.make_async_copy(sent.at[d], proj.at[d], loc_sem.at[7])
    own_proj.start()
    for k in range(1, 4):
        plane_x(k).wait_recv()
    for step in plane_steps:
        for copy in plane_one(*step):
            copy.start()
    for i in range(KV_HALF, KV_COPIES):
        kv_copy(i).start()
    ring[1].wait_recv()
    ring[3].start()
    ring[5].start()
    ring[2].wait_recv()
    ring[4].start()
    ring[6].start()
    ring[5].wait_recv()
    project(lax.rem(x + 3, 4))
    pj_copy(6).start()
    pj_copy(7).start()
    ring[6].wait_recv()
    project(lax.rem(x + 1, 4))
    pj_copy(2).start()
    pj_copy(3).start()
    for i in (1, 2):
        wring[i].start()
    own_wout.start()
    ring[3].wait_recv()
    ring[7].start()
    ring[4].wait_recv()
    ring[8].start()
    ring[7].wait_recv()
    ring[8].wait_recv()
    project(lax.rem(x + 2, 4))
    pj_copy(4).start()
    pj_copy(5).start()

    for step in plane_steps:
        for copy in plane_one(*step):
            copy.wait_recv()
    for step in plane_steps:
        for copy in plane_two(*step):
            copy.start()

    bks[h] = bk_out[h]

    def wait_bk(k, carry):
        bk_copy(k).wait_recv()
        return carry

    lax.fori_loop(1, HIST, wait_bk, 0)
    levels = lax.broadcasted_iota(jnp.int32, (BUCKETS, TOK), 0)
    for q in range(4):
        ids = (bks[4 * q] + bks[4 * q + 1] + bks[4 * q + 2] + bks[4 * q + 3])[0:1, :]
        onehot[:, pl.ds(q * TOK, TOK)] = jnp.where(levels == ids, 1.0, 0.0).astype(BF16)
    onehot[:, pl.ds(CACHED, TOK)] = jnp.where(levels == new_bucket[...], 1.0, 0.0).astype(BF16)
    hot = onehot[...]
    bias_sum = jnp.zeros((HEADS, KEYS), F32)
    for term in reversed(three_parts(rab[...])):
        bias_sum = bias_sum + dot_nn(term, hot)
    bias[...] = bias_sum

    count = length[0, 0]
    share = 1.0 / jnp.full((1, TOK), count + TOK, jnp.int32).astype(F32)
    cached_pos = lax.broadcasted_iota(jnp.int32, (1, CACHED), 1)
    share_cached = jnp.where(cached_pos < count, jnp.concatenate([share] * 4, axis=1), 0.0)
    row_pos = lax.broadcasted_iota(jnp.int32, (TOK, TOK), 0)
    col_pos = lax.broadcasted_iota(jnp.int32, (TOK, TOK), 1)
    share_new = jnp.where(col_pos <= row_pos, jnp.broadcast_to(share, (TOK, TOK)), 0.0)

    for i in (1, 2):
        wring[i].wait_recv()
        wring[i + 2].start()
        wring[i + 4].start()

    def wait_pj(k, carry):
        pj_copy(k).wait_recv()
        return carry

    own_proj.wait()
    lax.fori_loop(1, DP, wait_pj, 0)

    load_kv.wait()
    for i in range(1, KV_COPIES):
        kv_copy(i).wait_recv()

    def attend(m, carry):
        for k in range(2):
            head = m * 2 + k
            lanes = pl.ds(pl.multiple_of(head * HEAD, HEAD), HEAD)
            query = proj[m, :, pl.ds(k * HEAD, HEAD)]
            value_new = proj[m, :, pl.ds(2 * COLS + k * HEAD, HEAD)]
            key_new = proj[m, :, pl.ds(3 * COLS + k * HEAD, HEAD)]
            key_bias = bias[pl.ds(head, 1), :]
            total = jnp.zeros((TOK, HEAD), F32)
            parts = (
                (kv[0, :, lanes], kv[1, :, lanes], pl.ds(0, CACHED), key_bias[:, :CACHED], share_cached),
                (key_new, value_new, pl.ds(CACHED, TOK), key_bias[:, CACHED:], share_new),
            )
            for keys, values, where, bias_part, share_part in parts:
                score = dot_nt(query, keys) * SCALE + bias_part
                sigmoid = 0.5 * jnp.tanh(0.5 * score) + 0.5
                weight = score * sigmoid * share_part
                slope[head, :, where] = sigmoid * share_part + weight * (1.0 - sigmoid)
                total = total + dot_nn(weight.astype(BF16), values)
            att[:, lanes] = total
        return carry

    lax.fori_loop(0, DP, attend, 0)

    def stat_rows(r, carry):
        part = pl.ds(pl.multiple_of(r * 16, 16), 16)
        values = att[part, :]
        center = values - jnp.mean(values, axis=-1, keepdims=True)
        inverse = lax.rsqrt(jnp.mean(center * center, axis=-1, keepdims=True) + NORM_EPS)
        nhat = center * inverse
        gate = jnp.concatenate([proj[m, part, pl.ds(COLS, COLS)] for m in range(DP)], axis=1).astype(F32)
        scaled = gate * norm_gain[...]
        att[part, :] = nhat
        gate_scaled[part, :] = scaled
        gated[part, :] = (nhat * scaled).astype(BF16)
        inverse_std[part, :] = jnp.broadcast_to(inverse, (16, TOK))
        return carry

    lax.fori_loop(0, TOK // 16, stat_rows, 0)

    load_cot.wait()
    load_wout.wait()

    def gated_part(m, half, first=False):
        lanes = pl.ds(pl.multiple_of(m * COLS, COLS), COLS)
        for n in range(2):
            cols = pl.ds(half * 1024 + n * 512, 512)
            part = dot_nt(cot[:, lanes], wout[m, half, pl.ds(2 * n, 2)].reshape(512, COLS))
            grad_gated[:, cols] = part if first else grad_gated[:, cols] + part

    run(bk_copy, HIST, "wait_send")
    run(pj_copy, DP, "wait_send")
    for i in range(1, KV_COPIES):
        kv_copy(i).wait_send()
    for copy in ring.values():
        copy.wait_send()
    for k in range(1, 4):
        plane_x(k).wait_send()
    for step in plane_steps:
        for copy in plane_one(*step):
            copy.wait_send()

    for step in plane_steps:
        for copy in plane_two(*step):
            copy.wait_recv()
    for k in range(1, 4):
        plane_share(k).start()
    gated_part(d, 0, True)
    gated_part(d, 1, True)
    own_wout.wait_recv()
    gated_part(dpx(0, 1), 0)
    gated_part(dpx(0, 1), 1)
    gated_part(dpx(3, 0), 1)
    gated_part(dpx(1, 0), 1)
    for i in (3, 4):
        wring[i].wait_recv()
        wring[i + 4].start()
    for k in (3, 1, 2):
        gated_part(dpx(k, 0), 0)
    for k in (3, 1, 2):
        plane_share(k).wait_recv()
        gated_part(dpx(k, 1), 0)
    wring[5].wait_recv()
    gated_part(dpx(3, 1), 1)
    wring[6].wait_recv()
    gated_part(dpx(1, 1), 1)
    gated_part(dpx(2, 0), 1)
    wring[7].wait_recv()
    wring[8].wait_recv()
    gated_part(dpx(2, 1), 1)

    def gate_rows(r, carry):
        part = pl.ds(pl.multiple_of(r * 16, 16), 16)
        nhat = att[part, :]
        grad_hat = grad_gated[part, :] * gate_scaled[part, :]
        along = jnp.mean(grad_hat * nhat, axis=-1, keepdims=True)
        grad = inverse_std[part, 0:1] * (grad_hat - jnp.mean(grad_hat, axis=-1, keepdims=True) - nhat * along)
        grad_att[part, :] = grad.astype(BF16)
        return carry

    lax.fori_loop(0, TOK // 16, gate_rows, 0, unroll=2)

    def gq_copy(half, k):
        to, i = dpo(k), half * DP + k
        return remote(gq_out.at[half, to], gq_in.at[half, d], gq_s.at[i], gq_r.at[i], (h, to))

    def attend_back(m, k):
        head = m * 2 + k
        lanes = pl.ds(pl.multiple_of(head * HEAD, HEAD), HEAD)
        value_new = proj[m, :, pl.ds(2 * COLS + k * HEAD, HEAD)]
        key_new = proj[m, :, pl.ds(3 * COLS + k * HEAD, HEAD)]
        grad = grad_att[:, lanes]
        total = jnp.zeros((TOK, HEAD), F32)
        parts = (
            (kv[0, :, lanes], kv[1, :, lanes], pl.ds(0, CACHED)),
            (key_new, value_new, pl.ds(CACHED, TOK)),
        )
        for keys, values, where in parts:
            grad_score = dot_nt(grad, values) * slope[head, :, where]
            tsum[head, :, where] = jnp.sum(grad_score.reshape(TOK // 8, 8, -1), axis=0)
            total = total + dot_nn(grad_score.astype(BF16), keys)
        gq_out[k, m] = (total * SCALE).astype(BF16)

    def back_steps(half, first, stop):
        def step(i, carry):
            k = 2 * i + 1
            attend_back(dpo(k), half)
            attend_back(dpo(k + 1), half)
            gq_copy(half, k).start()
            gq_copy(half, k + 1).start()
            return carry

        lax.fori_loop(first, stop, step, 0)

    def own_back(half):
        attend_back(dpo(DP - 1), half)
        attend_back(d, half)
        gq_copy(half, DP - 1).start()
        gq_in[half, d] = gq_out[half, d]

    def weight_half(half):
        run(gq_copy, DP, "wait_recv", half)
        for i in range(DP):
            pre = pre_slope[i, :, pl.ds(half * HEAD, HEAD)]
            grad_pre_t[half, :, pl.ds(i * TOK, TOK)] = (gq_in[half, i].astype(F32) * pre).astype(BF16).T
        for i in range(4):
            piece = dot_nn(grad_pre_t[half], rows[:, :, pl.ds(i * 512, 512)].reshape(DP * TOK, 512)).astype(BF16)
            rs_out[half, i] = piece.T.reshape(4, 2, HEAD // 2, HEAD)
        for k in (1, 3, 2):
            for side in range(2):
                sum_one(half, side, k).start()

    def along(side, k):
        return (lax.rem(z + k, 4), y) if side == 0 else (z, lax.rem(y + k, 4))

    def place(zy):
        return (zy[0] * 4 + zy[1], d)

    def line(ref, half, side, zy):
        return ref.at[half, zy[0], :, side] if side == 0 else ref.at[half, :, zy[1], side]

    def own(side):
        return z if side == 0 else y

    def sems(pair, half, side, k):
        i = (half * 2 + side) * 4 + k
        return pair[0].at[i], pair[1].at[i]

    def sum_one(half, side, k):
        to = along(side, k)
        return remote(line(rs_out, half, side, to), r1_in.at[half, side, own(side)], *sems((r1_s, r1_r), half, side, k), place(to))

    def sum_two(half, side, k):
        src, dst = r2_out.at[half, side], r2_in.at[half, side, own(1 - side)]
        return remote(src, dst, *sems((r2_s, r2_r), half, side, k), place(along(1 - side, k)))

    def gsum_line(half, side):
        lanes = pl.ds(half * HEAD, HEAD)
        return gsum_hbm.at[z, :, side, :, lanes] if side == 0 else gsum_hbm.at[:, y, side, :, lanes]

    def gather_two(half, side, k):
        src = line(ag_buf, half, side, (z, y))
        return remote(src, gsum_line(half, side), *sems((a2_s, a2_r), half, side, k), place(along(side, k)))

    def own_gsum(half, side):
        return pltpu.make_async_copy(line(ag_buf, half, side, (z, y)), gsum_line(half, side), loc_sem.at[8 + half * 2 + side])

    def after_one(half):
        for side in range(2):
            r1_in[half, side, own(side)] = rs_out[half, z, :, 0] if side == 0 else rs_out[half, :, y, 1]
            for k in (1, 3, 2):
                sum_one(half, side, k).wait_recv()
            total = r1_in[half, side, 0].astype(F32)
            for i in range(1, 4):
                total = total + r1_in[half, side, i].astype(F32)
            r2_out[half, side] = total.astype(BF16)
            for k in (1, 3, 2):
                sum_two(half, side, k).start()

    def after_two(half):
        for side in range(2):
            r2_in[half, side, own(1 - side)] = r2_out[half, side]
            for k in (1, 3, 2):
                sum_two(half, side, k).wait_recv()
            total = r2_in[half, side, 0].astype(F32)
            for i in range(1, 4):
                total = total + r2_in[half, side, i].astype(F32)
            if side == 0:
                ag_buf[half, z, :, 0] = total.astype(BF16)
            else:
                ag_buf[half, :, y, 1] = total.astype(BF16)
            for k in (1, 3, 2):
                gather_two(half, side, k).start()
            own_gsum(half, side).start()

    def out_cols(m, carry):
        lanes = pl.ds(pl.multiple_of(m * COLS, COLS), COLS)
        product = dot_nn(gated[...], wout[m].reshape(WIDTH, COLS))
        out_ref[:, lanes] = (product + act[:, lanes].astype(F32)).astype(BF16)
        return carry

    def t1_copy(k):
        return remote(tab_one.at[d], tab_one.at[d], t1_s.at[k], t1_r.at[k], (h, dpo(k)))

    def t2_copy(k):
        return remote(tab_two.at[z], tab_two.at[z], t2_s.at[k], t2_r.at[k], place(along(0, k)))

    def t3_copy(k):
        return remote(tab_three.at[y], tab_three.at[y], t3_s.at[k], t3_r.at[k], place(along(1, k)))

    def table_sum(ref, count):
        total = ref[0]
        for i in range(1, count):
            total = total + ref[i]
        return total

    back_steps(0, 0, 3)
    own_back(0)
    back_steps(1, 0, 2)
    weight_half(0)
    back_steps(1, 2, 3)
    own_back(1)

    table = jnp.zeros((HEADS, BUCKETS), F32)
    for term in reversed(three_parts(jnp.sum(tsum[...], axis=1))):
        table = table + dot_nt(term, hot)
    tab_one[d] = table
    run(t1_copy, DP, "start")

    lax.fori_loop(0, 2, out_cols, 0)
    after_one(0)
    weight_half(1)
    lax.fori_loop(2, 4, out_cols, 0)
    after_two(0)

    run(t1_copy, DP, "wait_recv")
    tab_two[z] = table_sum(tab_one, DP)
    for k in (1, 3, 2):
        t2_copy(k).start()

    after_one(1)
    for k in (1, 3, 2):
        t2_copy(k).wait_recv()
    tab_three[y] = table_sum(tab_two, 4)
    for k in (1, 3, 2):
        t3_copy(k).start()
    lax.fori_loop(4, 6, out_cols, 0)
    after_two(1)
    for copy in [*wring.values(), own_wout]:
        copy.wait_send()
    for k in range(1, 4):
        plane_share(k).wait_send()
    for step in plane_steps:
        for copy in plane_two(*step):
            copy.wait_send()
    lax.fori_loop(6, DP, out_cols, 0)

    for k in (1, 3, 2):
        t3_copy(k).wait_recv()
    gtab_ref[...] = table_sum(tab_three, 4)

    run(t1_copy, DP, "wait_send")
    for k in (1, 3, 2):
        t2_copy(k).wait_send()
        t3_copy(k).wait_send()
    for half in range(2):
        run(gq_copy, DP, "wait_send", half)
        for side in range(2):
            for k in (1, 3, 2):
                for copy in (sum_one, sum_two):
                    copy(half, side, k).wait_send()
                gather_two(half, side, k).wait()
            own_gsum(half, side).wait()


def layer(actions, cotangent, cache, length, buckets, new_bucket, ln_gain, norm_gain, w_frozen, w_query, w_out, rab):
    any_space = pl.BlockSpec(memory_space=pl.ANY)
    vmem = pl.BlockSpec(memory_space=pltpu.VMEM)
    smem = pl.BlockSpec(memory_space=pltpu.SMEM)
    dma = pltpu.SemaphoreType.DMA
    sem_sizes = (12, KV_COPIES, KV_COPIES, HIST, HIST, 9, 9, DP, DP, 9, 9, 4, 4, 18, 18, 18, 18, 4, 4, 2 * DP, 2 * DP, *[16] * 6, DP, DP, 4, 4, 4, 4)
    return pl.pallas_call(
        kernel,
        out_shape=(
            jax.ShapeDtypeStruct((TOK, WIDTH), BF16),
            jax.ShapeDtypeStruct((4, 4, 2, HEAD // 2, COLS), BF16),
            jax.ShapeDtypeStruct((HEADS, BUCKETS), F32),
        ),
        in_specs=[any_space, any_space, any_space, smem, vmem, vmem, vmem, vmem, any_space, any_space, any_space, vmem],
        out_specs=(vmem, any_space, vmem),
        scratch_shapes=[
            pltpu.VMEM((TOK, WIDTH), BF16),
            pltpu.VMEM((TOK, WIDTH), BF16),
            pltpu.VMEM((4, WIDTH, COLS), BF16),
            pltpu.VMEM((DP, TOK, WIDTH), BF16),
            pltpu.VMEM((DP, TOK, COLS), F32),
            pltpu.VMEM((DP, TOK, 4 * COLS), BF16),
            pltpu.VMEM((DP, TOK, 4 * COLS), BF16),
            pltpu.VMEM((2, CACHED, WIDTH), BF16),
            pltpu.VMEM((HIST, 8, TOK), jnp.int32),
        pltpu.VMEM((HIST, 8, TOK), jnp.int32),
            pltpu.VMEM((BUCKETS, KEYS), BF16),
            pltpu.VMEM((HEADS, KEYS), F32),
            pltpu.VMEM((TOK, WIDTH), F32),
            pltpu.VMEM((HEADS, TOK, KEYS), F32),
            pltpu.VMEM((DP, 2, 4, 4, 2, 32, COLS), BF16),
            pltpu.VMEM((TOK, WIDTH), F32),
            pltpu.VMEM((TOK, WIDTH), F32),
            pltpu.VMEM((TOK, TOK), F32),
            pltpu.VMEM((TOK, WIDTH), BF16),
            pltpu.VMEM((TOK, WIDTH), BF16),
            pltpu.VMEM((HEADS, 8, KEYS), F32),
            pltpu.VMEM((2, DP, TOK, HEAD), BF16),
            pltpu.VMEM((2, DP, TOK, HEAD), BF16),
            pltpu.VMEM((2, HEAD, DP * TOK), BF16),
            pltpu.VMEM((2, 4, 4, 2, HEAD // 2, HEAD), BF16),
            pltpu.VMEM((2, 2, 4, 4, HEAD // 2, HEAD), BF16),
            pltpu.VMEM((2, 2, 4, HEAD // 2, HEAD), BF16),
            pltpu.VMEM((2, 2, 4, 4, HEAD // 2, HEAD), BF16),
            pltpu.VMEM((2, 4, 4, 2, HEAD // 2, HEAD), BF16),
            pltpu.VMEM((DP, HEADS, BUCKETS), F32),
            pltpu.VMEM((4, HEADS, BUCKETS), F32),
            pltpu.VMEM((4, HEADS, BUCKETS), F32),
        ]
        + [dma((n,)) for n in sem_sizes],
        compiler_params=pltpu.CompilerParams(collective_id=0, has_side_effects=True, vmem_limit_bytes=60 * 1024 * 1024),
        name="layer",
    )(actions, cotangent, cache, length, buckets, new_bucket, ln_gain, norm_gain, w_frozen, w_query, w_out, rab)


ADAM_ROWS = 1024


def adam_kernel(
    grad, weight, moment_one, moment_two, table_grad, table, table_one, table_two, done,
    weight_new, one_new, two_new, table_new, table_one_new, table_two_new, result,
):
    gradient = grad[...].astype(F32)
    first = BETA_ONE * moment_one[...] + (1.0 - BETA_ONE) * gradient
    second = BETA_TWO * moment_two[...] + (1.0 - BETA_TWO) * gradient * gradient
    one_new[...] = first
    two_new[...] = second
    root = second * lax.rsqrt(second)
    stepped = weight[...].astype(F32) - LEARN_RATE * first * pl.reciprocal(root + ADAM_EPS)
    weight_new[...] = stepped.astype(BF16)
    result[...] = done[...]

    @pl.when(pl.program_id(0) == 0)
    def _():
        updated = adam_update(table[...], table_one[...], table_two[...], table_grad[...])
        table_new[...], table_one_new[...], table_two_new[...] = updated


def adam(grad, weight, moment_one, moment_two, table_grad, table, table_one, table_two, done):
    steps = WIDTH // ADAM_ROWS
    rows = pl.BlockSpec((ADAM_ROWS, COLS), lambda i: (i, 0))
    small = pl.BlockSpec((HEADS, BUCKETS), lambda i: (0, 0))
    tokens = pl.BlockSpec((TOK // steps, WIDTH), lambda i: (i, 0))
    operands = (grad, weight, moment_one, moment_two, table_grad, table, table_one, table_two, done)
    return pl.pallas_call(
        adam_kernel,
        grid=(steps,),
        out_shape=[jax.ShapeDtypeStruct(a.shape, a.dtype) for a in operands[1:4] + operands[5:]],
        in_specs=[rows] * 4 + [small] * 4 + [tokens],
        out_specs=[rows] * 3 + [small] * 3 + [tokens],
        name="adam",
    )(*operands)


def shards(
    actions, cotangent, cache_kv, cache_len, cache_bucket, new_bucket, ln_gain, norm_gain,
    w_frozen, w_query, query_m, query_v, w_out, rab_table, rab_m, rab_v,
):
    result, grad_sum, grad_table = layer(
        actions.reshape(TOK, WIDTH),
        cotangent.reshape(TOK, WIDTH),
        cache_kv.reshape(2, HIST, SLAB, WIDTH),
        cache_len.reshape(1, 1),
        cache_bucket,
        new_bucket.reshape(1, TOK),
        ln_gain.reshape(1, WIDTH),
        norm_gain.reshape(1, WIDTH),
        w_frozen,
        w_query,
        w_out.reshape(2, 4, 4, 2, 32, COLS),
        rab_table,
    )
    query_new, query_m_new, query_v_new, rab_new, rab_m_new, rab_v_new, result = adam(
        grad_sum.reshape(WIDTH, COLS), w_query, query_m, query_v, grad_table, rab_table, rab_m, rab_v, result
    )
    return (result.reshape(actions.shape), query_new, query_m_new, query_v_new, rab_new, rab_m_new, rab_v_new)


def solution(mesh):
    placed = (
        P("history", "dp", None, None),
        P("history", "dp", None, None),
        P(None, None, "dp", "history", None),
        P("history", "dp"),
        P(None, "dp", "history"),
        P("history", "dp", None),
        P(),
        P(),
        P(None, None, "dp"),
        P(None, "dp"),
        P(None, "dp"),
        P(None, "dp"),
        P(None, "dp"),
        P(),
        P(),
        P(),
    )
    return jax.shard_map(
        shards,
        mesh=mesh,
        in_specs=placed,
        out_specs=(
            P("history", "dp", None, None),
            P(None, "dp"),
            P(None, "dp"),
            P(None, "dp"),
            P(),
            P(),
            P(),
        ),
        check_vma=False,
    )
```
